32 devices in a mesh: wide: 2 (over core), tensor: 4 (over y, x), expert: 4 (over z).
Axes of the slice: x: 2, y: 2, z: 4, core: 2. Of those that a mesh axis runs over, the one named last changes fastest.
Arguments:
- tokens: bfloat16 [512, 6144], P('expert', 'wide'), may hold values from -6 to 6
- expert_ids: int32 [512, 2], P('expert'), may hold values from 0 to 3, all different within a row; in each aligned block of 128 rows (0 to 127, 128 to 255, ...) at most 96 rows name the same one
- gate_values: float32 [512, 2], P('expert'), may hold values from 0.1 to 1
- w_gate: bfloat16 [4, 6144, 8192], P('expert', 'wide', 'tensor'), may hold values from -0.078125 to 0.078125
- w_up: bfloat16 [4, 6144, 8192], P('expert', 'wide', 'tensor'), may hold values from -0.078125 to 0.078125
- w_down: bfloat16 [4, 8192, 6144], P('expert', 'tensor', 'wide'), may hold values from -0.0625 to 0.0625
- cotangent: bfloat16 [512, 6144], P('expert', 'wide'), may hold values from -6 to 6
Outputs:
- layer_out: bfloat16 [512, 6144], P('expert', 'wide')
- token_grad: bfloat16 [512, 6144], P('expert', 'wide')
- gate_grad: float32 [512, 2], P('expert')
The draws below stay inside these ranges and needn't reach their ends.
Inputs may be any that keep to these rules, and one draw needn't show every extreme that they name: `expert_ids`: in each block of 128 rows no expert is named by more than 96 rows, a bound that some block reaches; the two experts of a row differ.
All inputs are finite; a program needn't handle non-finite values.
Results may differ from the reference program's by a relative error of at most 0.0066.
Values may be sent and summed in bfloat16 or wider, within the bound.
No kernel may reach another device: no remote copies, remote signals or barrier semaphores. Data moves between devices by JAX's collectives and lax.ppermute only.
A program may use at most 128 MiB of HBM per device.

```python
import math
import jax
import jax.numpy as jnp
import numpy as np
from jax import lax

D = 6144
FF = 8192
TOK_DEV = 128
EXPERTS = 4
TOKENS = 512
CAP = 96
N_EXPERT = 4


def level_of(own_key, shape, split, least, high):
    def one(dim, shards_of):
        draws = jax.random.uniform(jax.random.fold_in(jax.random.fold_in(own_key, 6), dim), (shards_of,), jnp.float32, least / len(split), high / len(split))
        return jnp.repeat(jnp.exp(draws), shape[dim] // shards_of).reshape((-1,) + (1,) * (len(shape) - dim - 1))

    gain = one(*split[0])
    for cut in split[1:]:
        gain = gain * one(*cut)
    return gain


def routed_block(rng, own, number, rows, count, top, bound, lean):
    order = jax.random.permutation(rng, count)
    heavy_load, ordinary = load_shares(count, rows * top, bound, lean, True), load_shares(count, rows * top, bound, lean, False)
    places = jnp.arange(count)

    def named(lengths, offset_by):
        used = int((lengths > 0).sum())
        fixed = max(1, used // 4)
        moved = fixed + (places - fixed + offset_by * (used - fixed)) % max(1, count - fixed)
        return jnp.zeros((count,), jnp.int32).at[order[jnp.where(places < fixed, places, moved)]].set(jnp.asarray(lengths, jnp.int32))

    lengths = jnp.where(number % 4 == 0, named(heavy_load, number // 4), named(ordinary, number - number // 4 - 1))
    mixed = jax.random.permutation(jax.random.fold_in(own, 3), count)
    source_of, sink = mixed[0:count // 2 * 2:2], mixed[1:count // 2 * 2:2]
    room = jnp.minimum(lengths[source_of] - 1, bound - lengths[sink]) // 2
    room = jnp.where((source_of == order[0]) | (sink == order[0]) | (lengths[sink] == 0), 0, jnp.maximum(room, 0))
    moved = jax.random.randint(jax.random.fold_in(own, 4), (count // 2,), 0, 1 << 20) % (room + 1)
    lengths = lengths.at[source_of].add(-moved).at[sink].add(moved)
    items = jnp.searchsorted(jnp.cumsum(lengths), jnp.arange(rows * top), side="right").astype(jnp.int32)
    table = items.reshape(top, rows).T
    table = table[jax.random.permutation(jax.random.fold_in(own, 1), rows)]
    offset_by = jax.random.randint(jax.random.fold_in(own, 2), (rows, 1), 0, top)
    return jnp.take_along_axis(table, (jnp.arange(top)[None, :] + offset_by) % top, axis=1)


def load_shares(count, total, reach, lean, full):
    portions = [(1 << 20) // math.isqrt(rank ** lean) + 1 for rank in range(1, count + 1)]
    largest = reach if full else min(reach, max(-(-total // count), total * portions[0] // sum(portions)))
    least = 1 if total - largest >= count - 1 else 0
    counts, rest = [largest] + [least] * (count - 1), total - largest - least * (count - 1)
    while rest > 0:
        movable = [i for i in range(1, count) if counts[i] < largest] or [i for i in range(1, count) if counts[i] < reach]
        pool, left = sum([portions[i] for i in movable]), rest
        for i in movable:
            addition = min(reach - counts[i], max(1, left * portions[i] // pool), rest)
            counts[i] = counts[i] + addition
            rest = rest - addition
    return np.array(counts)


def noise(key, extent, width, limit, pieces=(), held_as=jnp.bfloat16):
    array = jax.random.normal(key, extent, jnp.float32) * width
    if len(pieces) > 0:
        array = level_of(key, extent, pieces, -0.22, 0.18) * array
    return jnp.clip(array, min=-limit, max=limit).astype(held_as)


def setup_inputs(seed: int = 0) -> dict:
    splits = jax.random.split(jax.random.key(seed), 8)
    tokens = noise(splits[0], (TOKENS, D), 1.0, 6.0, ((0, 4), (1, 2)))
    expert_ids_keys = jax.random.split(jax.random.fold_in(splits[1], 1), TOKENS // TOK_DEV)
    expert_ids_turns = jax.random.permutation(jax.random.fold_in(splits[1], 3), TOKENS // TOK_DEV)
    expert_ids = jax.vmap(lambda own, number: routed_block(jax.random.fold_in(splits[1], 2), own, number, TOK_DEV, EXPERTS, 2, CAP, 2))(expert_ids_keys, expert_ids_turns).reshape((TOKENS, 2))
    gate_values = jnp.clip(0.1 + 0.9 * jax.random.uniform(splits[2], (TOKENS, 2), jnp.float32) ** level_of(splits[2], (TOKENS, 2), ((0, 4),), -0.2, 0.2), 0.1, 1.0)
    w_gate = noise(splits[3], (EXPERTS, D, FF), D ** -0.5, 0.078125, ((0, 4), (1, 2), (2, 4)))
    w_up = noise(splits[4], (EXPERTS, D, FF), D ** -0.5, 0.078125, ((0, 4), (1, 2), (2, 4)))
    w_down = noise(splits[5], (EXPERTS, FF, D), FF ** -0.5, 0.0625, ((0, 4), (1, 4), (2, 2)))
    cotangent = noise(splits[6], (TOKENS, D), 1.0, 6.0, ((0, 4), (1, 2)))
    return {"tokens": tokens, "expert_ids": expert_ids, "gate_values": gate_values, "w_gate": w_gate, "w_up": w_up, "w_down": w_down, "cotangent": cotangent}


def slot_table(expert_ids):
    grouped = expert_ids.reshape(N_EXPERT, TOK_DEV, 2)
    hit_table = (grouped[:, :, :, None] == jnp.arange(EXPERTS, dtype=jnp.int32)).astype(jnp.int32)
    per_row = jnp.sum(hit_table, axis=2)
    before = jnp.cumsum(per_row, axis=1) - per_row
    return jnp.sum(hit_table * before[:, :, None, :], axis=3).reshape(TOKENS, 2).astype(jnp.int32)


def reference(tokens, expert_ids, gate_values, w_gate, w_up, w_down, cotangent):
    slot_of = slot_table(expert_ids)
    owners = (jnp.arange(TOKENS, dtype=jnp.int32) // TOK_DEV).astype(jnp.int32)

    def place_rows(values):
        buffer = jnp.zeros((EXPERTS, N_EXPERT, CAP, D), values.dtype)
        for which in range(2):
            buffer = buffer.at[expert_ids[:, which], owners, slot_of[:, which]].set(values[:, which])
        return buffer.reshape(EXPERTS, N_EXPERT * CAP, D)

    def pick_rows(buffer, which):
        shaped = buffer.reshape(EXPERTS, N_EXPERT, CAP, D)
        return shaped[expert_ids[:, which], owners, slot_of[:, which]].astype(jnp.float32)

    dispatched = place_rows(jnp.stack([tokens, tokens], axis=1))

    def pre_acts(arrived, gate_mat, up_mat):
        gate_pre = jnp.dot(arrived, gate_mat, preferred_element_type=jnp.float32)
        up_pre = jnp.dot(arrived, up_mat, preferred_element_type=jnp.float32)
        return gate_pre, up_pre

    def forward_one(inputs):
        arrived, gate_mat, up_mat, down_mat = inputs
        gate_pre, up_pre = pre_acts(arrived, gate_mat, up_mat)
        hidden = (gate_pre * jax.nn.sigmoid(gate_pre) * up_pre).astype(jnp.bfloat16)
        return jnp.dot(hidden, down_mat, preferred_element_type=jnp.float32).astype(jnp.bfloat16)

    expert_out = lax.map(forward_one, (dispatched, w_gate, w_up, w_down))
    chosen = [pick_rows(expert_out, which) for which in range(2)]
    layer_out = (gate_values[:, 0:1] * chosen[0] + gate_values[:, 1:2] * chosen[1]).astype(jnp.bfloat16)
    upstream = cotangent.astype(jnp.float32)
    gate_grad = jnp.stack([jnp.sum(upstream * chosen[which], axis=1) for which in range(2)], axis=1)
    grad_out = place_rows((gate_values[:, :, None] * upstream[:, None, :]).astype(jnp.bfloat16))

    def backward_one(inputs):
        arrived, grad_arrived, gate_mat, up_mat, down_mat = inputs
        gate_pre, up_pre = pre_acts(arrived, gate_mat, up_mat)
        grad_hidden = jnp.dot(grad_arrived, down_mat.T, preferred_element_type=jnp.float32)
        sigmoid_gate = jax.nn.sigmoid(gate_pre)
        grad_gate = (grad_hidden * up_pre * (sigmoid_gate * (1.0 + gate_pre * (1.0 - sigmoid_gate)))).astype(jnp.bfloat16)
        grad_up = (grad_hidden * (gate_pre * sigmoid_gate)).astype(jnp.bfloat16)
        summed = jnp.dot(grad_gate, gate_mat.T, preferred_element_type=jnp.float32) + jnp.dot(grad_up, up_mat.T, preferred_element_type=jnp.float32)
        return summed.astype(jnp.bfloat16)

    grad_rows = lax.map(backward_one, (dispatched, grad_out, w_gate, w_up, w_down))
    token_grad = (pick_rows(grad_rows, 0) + pick_rows(grad_rows, 1)).astype(jnp.bfloat16)
    return (layer_out, token_grad, gate_grad)
```

```python
import jax
import jax.numpy as jnp
from jax import lax
from jax.experimental import pallas as pl
from jax.experimental.pallas import tpu as pltpu
from jax.sharding import PartitionSpec as P

BF = jnp.bfloat16
F32 = jnp.float32
MIB = 1024 * 1024


def slot_index(expert_ids, experts):
    hit_table = (expert_ids[:, :, None] == jnp.arange(experts, dtype=jnp.int32)).astype(jnp.int32)
    per_row = jnp.sum(hit_table, axis=1)
    before = jnp.cumsum(per_row, axis=0) - per_row
    return jnp.sum(hit_table * before[:, None, :], axis=2)


def exchange(array, axis, bit):
    size = lax.axis_size(axis)
    return lax.ppermute(array, axis, [(i, i ^ bit) for i in range(size)])


def dot_nn(a, b):
    return jnp.dot(a, b, preferred_element_type=F32)


def dot_nt(a, b):
    return lax.dot_general(a, b, (((1,), (1,)), ((), ())), preferred_element_type=F32)


def params(mib):
    return pltpu.CompilerParams(vmem_limit_bytes=mib * MIB)


def whole(shape):
    zeros = (0,) * len(shape)
    return pl.BlockSpec(shape, lambda i, *_: zeros, pipeline_mode=pl.Buffered(1))


def sds(shape, dtype):
    return jax.ShapeDtypeStruct(shape, dtype)


def cost(flops, nbytes):
    return pl.CostEstimate(flops=flops, bytes_accessed=nbytes, transcendentals=0)


def gather_rows(t, own_ref, parts, rows_ref):
    cap = own_ref.shape[0]
    n = len(parts)
    quarter = parts[0].shape[1]
    for q in range(n):
        rows_ref[q, :cap, :] = own_ref[:, q * quarter : (q + 1) * quarter]
    for j in range(n):
        rows_ref[t ^ j, cap:, :] = parts[j][...]


def pre_act_kernel(t_ref, own_ref, *refs):
    parts, (gate_w, up_w, gate_o, up_o, gate_s, up_s, rows_ref) = refs[:-7], refs[-7:]

    @pl.when(pl.program_id(0) == 0)
    def _():
        gather_rows(t_ref[0], own_ref, parts, rows_ref)

    n, _, quarter = rows_ref.shape
    for w, out, send in ((gate_w, gate_o, gate_s), (up_w, up_o, up_s)):
        total = dot_nn(rows_ref[0], w[:quarter, :])
        for q in range(1, n):
            total += dot_nn(rows_ref[q], w[q * quarter : (q + 1) * quarter, :])
        out[...] = total
        send[...] = total.astype(BF)


def pre_acts(t, own, parts, gate_mat, up_mat, block):
    depth, hidden = gate_mat.shape
    cap = own.shape[0]
    n = len(parts)
    rows = cap + parts[0].shape[0]
    weight = pl.BlockSpec((depth, block), lambda i, *_: (0, i))
    out = pl.BlockSpec((rows, block), lambda i, *_: (0, i))
    return pl.pallas_call(
        pre_act_kernel,
        grid_spec=pltpu.PrefetchScalarGridSpec(
            num_scalar_prefetch=1,
            grid=(hidden // block,),
            in_specs=[whole(own.shape)] + [whole(p.shape) for p in parts] + [weight, weight],
            out_specs=[out] * 4,
            scratch_shapes=[pltpu.VMEM((n, rows, depth // n), BF)],
        ),
        out_shape=[sds((rows, hidden), F32)] * 2 + [sds((rows, hidden), BF)] * 2,
        compiler_params=params(48),
        cost_estimate=cost(4 * rows * depth * hidden, 4 * depth * hidden),
        name="pre_acts",
    )(t, own, *parts, gate_mat, up_mat)


def grad_hidden_kernel(t_ref, own_ref, *refs):
    parts, (down_w, out, send, rows_ref) = refs[:-4], refs[-4:]

    @pl.when(pl.program_id(0) == 0)
    def _():
        gather_rows(t_ref[0], own_ref, parts, rows_ref)

    n, _, quarter = rows_ref.shape
    total = dot_nt(rows_ref[0], down_w[:, :quarter])
    for q in range(1, n):
        total += dot_nt(rows_ref[q], down_w[:, q * quarter : (q + 1) * quarter])
    out[...] = total
    send[...] = total.astype(BF)


def grad_hiddens(t, own, parts, down_mat, block):
    hidden, depth = down_mat.shape
    n = len(parts)
    rows = own.shape[0] + parts[0].shape[0]
    weight = pl.BlockSpec((block, depth), lambda i, *_: (i, 0))
    out = pl.BlockSpec((rows, block), lambda i, *_: (0, i))
    return pl.pallas_call(
        grad_hidden_kernel,
        grid_spec=pltpu.PrefetchScalarGridSpec(
            num_scalar_prefetch=1,
            grid=(hidden // block,),
            in_specs=[whole(own.shape)] + [whole(p.shape) for p in parts] + [weight],
            out_specs=[out] * 2,
            scratch_shapes=[pltpu.VMEM((n, rows, depth // n), BF)],
        ),
        out_shape=[sds((rows, hidden), F32), sds((rows, hidden), BF)],
        compiler_params=params(48),
        cost_estimate=cost(2 * rows * depth * hidden, 2 * depth * hidden),
        name="grad_hidden",
    )(t, own, *parts, down_mat)


STRIP = 32


def project_kernel(t_ref, gate_o, up_o, gate_r, up_r, down_w, pieces, kept, hidden_ref):
    step = pl.program_id(0)

    @pl.when(step == 0)
    def _():
        @pl.loop(0, hidden_ref.shape[0] // STRIP)
        def _(i):
            here = pl.ds(pl.multiple_of(i * STRIP, STRIP), STRIP)
            gate = gate_o[here, :] + gate_r[here, :].astype(F32)
            up = up_o[here, :] + up_r[here, :].astype(F32)
            hidden_ref[here, :] = (gate * jax.nn.sigmoid(gate) * up).astype(BF)

    total = dot_nn(hidden_ref[...], down_w[...])

    @pl.when(step < pl.num_programs(0) - 1)
    def _():
        pieces[0] = total.astype(BF)

    @pl.when(step == pl.num_programs(0) - 1)
    def _():
        kept[...] = total


def projected(t, n, gate_o, up_o, gate_r, up_r, down_mat):
    hidden, depth = down_mat.shape
    rows = gate_o.shape[0]
    quarter = depth // n

    def which(i, t):
        return t[0] ^ ((i + 1) % n)

    return pl.pallas_call(
        project_kernel,
        grid_spec=pltpu.PrefetchScalarGridSpec(
            num_scalar_prefetch=1,
            grid=(n,),
            in_specs=[whole(gate_o.shape)] * 4
            + [pl.BlockSpec((hidden, quarter), lambda i, t: (0, which(i, t)))],
            out_specs=[
                pl.BlockSpec((1, rows, quarter), lambda i, t: (jnp.minimum(i, n - 2), 0, 0)),
                pl.BlockSpec((rows, quarter), lambda i, t: (0, 0)),
            ],
            scratch_shapes=[pltpu.VMEM((rows, hidden), BF)],
        ),
        out_shape=[sds((n - 1, rows, quarter), BF), sds((rows, quarter), F32)],
        compiler_params=params(48),
        cost_estimate=cost(2 * rows * depth * hidden, 2 * depth * hidden),
        name="project",
    )(t, gate_o, up_o, gate_r, up_r, down_mat)


def grad_rows_kernel(
    t_ref, gate_o, up_o, gate_r, up_r, gh_o, gh_r, gate_w, up_w, pieces, kept, gg_ref, gu_ref
):
    step = pl.program_id(0)

    @pl.when(step == 0)
    def _():
        @pl.loop(0, gg_ref.shape[0] // STRIP)
        def _(i):
            here = pl.ds(pl.multiple_of(i * STRIP, STRIP), STRIP)
            gate = gate_o[here, :] + gate_r[here, :].astype(F32)
            up = up_o[here, :] + up_r[here, :].astype(F32)
            grad = gh_o[here, :] + gh_r[here, :].astype(F32)
            s = jax.nn.sigmoid(gate)
            gg_ref[here, :] = (grad * up * (s * (1.0 + gate * (1.0 - s)))).astype(BF)
            gu_ref[here, :] = (grad * (gate * s)).astype(BF)

    total = dot_nt(gg_ref[...], gate_w[...]) + dot_nt(gu_ref[...], up_w[...])

    @pl.when(step < pl.num_programs(0) - 1)
    def _():
        pieces[0] = total.astype(BF)

    @pl.when(step == pl.num_programs(0) - 1)
    def _():
        kept[...] = total


def grad_rows(t, n, gate_o, up_o, gate_r, up_r, gh_o, gh_r, gate_mat, up_mat):
    depth, hidden = gate_mat.shape
    rows = gate_o.shape[0]
    quarter = depth // n

    def which(i, t):
        return t[0] ^ ((i + 1) % n)

    weight = pl.BlockSpec((quarter, hidden), lambda i, t: (which(i, t), 0))
    return pl.pallas_call(
        grad_rows_kernel,
        grid_spec=pltpu.PrefetchScalarGridSpec(
            num_scalar_prefetch=1,
            grid=(n,),
            in_specs=[whole(gate_o.shape)] * 6 + [weight, weight],
            out_specs=[
                pl.BlockSpec((1, rows, quarter), lambda i, t: (jnp.minimum(i, n - 2), 0, 0)),
                pl.BlockSpec((rows, quarter), lambda i, t: (0, 0)),
            ],
            scratch_shapes=[pltpu.VMEM((rows, hidden), BF)] * 2,
        ),
        out_shape=[sds((n - 1, rows, quarter), BF), sds((rows, quarter), F32)],
        compiler_params=params(52),
        cost_estimate=cost(4 * rows * depth * hidden, 4 * depth * hidden),
        name="grad_rows",
    )(t, gate_o, up_o, gate_r, up_r, gh_o, gh_r, gate_mat, up_mat)


def local(tokens, expert_ids, gate_values, w_gate, w_up, w_down, cotangent):
    tok_rows, depth = tokens.shape
    groups = lax.axis_size("expert")
    n = lax.axis_size("tensor")
    z = lax.axis_index("expert")
    t = lax.axis_index("tensor")
    t_arr = t.astype(jnp.int32).reshape(1)
    experts = groups
    cap = min(tok_rows, 3 * tok_rows // experts)
    quarter = depth // n
    gate_mat, up_mat, down_mat = w_gate[0], w_up[0], w_down[0]

    slot_of = slot_index(expert_ids, experts)
    order = (expert_ids ^ z) * cap + slot_of
    cells = jnp.arange(experts * cap, dtype=jnp.int32)
    pick = [order[:, k][None, :] == cells[:, None] for k in range(2)]
    spread = jnp.logical_or(pick[0], pick[1]).astype(BF)
    slot_gate = jnp.sum(
        jnp.where(pick[0], gate_values[:, 0][None, :], 0.0)
        + jnp.where(pick[1], gate_values[:, 1][None, :], 0.0),
        axis=1,
        keepdims=True,
    )

    def dispatch(source, scale):
        part = lax.dynamic_slice(source, (0, t * quarter), (tok_rows, quarter))
        out = dot_nn(spread[cap:], part)
        own = dot_nn(spread[:cap], source)
        if scale is not None:
            out, own = out * scale[cap:], own * scale[:cap]
        out, own = out.astype(BF), own.astype(BF)
        arrived = jnp.concatenate(
            [exchange(out[(k - 1) * cap : k * cap], "expert", k) for k in range(1, groups)], axis=0
        )
        return own, arrived

    tok_own, tok_part = dispatch(tokens, None)
    tok_parts = [tok_part] + [exchange(tok_part, "tensor", j) for j in range(1, n)]
    cot_own, cot_part = dispatch(cotangent, slot_gate)
    cot_parts = [cot_part] + [exchange(cot_part, "tensor", j) for j in range(1, n)]

    gate_o, up_o, gate_s, up_s = pre_acts(t_arr, tok_own, tok_parts, gate_mat, up_mat, 512)
    gate_r, up_r = exchange(gate_s, "wide", 1), exchange(up_s, "wide", 1)
    gh_o, gh_s = grad_hiddens(t_arr, cot_own, cot_parts, down_mat, 512)
    gh_r = exchange(gh_s, "wide", 1)

    def send_back(pieces, kept):
        total = kept
        for j in range(1, n):
            total = total + exchange(pieces[j - 1], "tensor", j).astype(F32)
        total = total.astype(BF)
        back = [total[:cap]] + [
            exchange(total[k * cap : (k + 1) * cap], "expert", k) for k in range(1, groups)
        ]
        return jnp.concatenate(back, axis=0)

    def spread_out(part):
        got = [part] + [exchange(part, "tensor", j) for j in range(1, n)]
        out = jnp.zeros((tok_rows, depth), part.dtype)
        for j in range(n):
            out = lax.dynamic_update_slice(out, got[j], (0, (t ^ j) * quarter))
        return out

    gather = [(order[:, k][:, None] == cells[None, :]).astype(BF) for k in range(2)]
    pieces, kept = projected(t_arr, n, gate_o, up_o, gate_r, up_r, down_mat)
    returned = send_back(pieces, kept)
    chosen = [dot_nn(g, returned) for g in gather]
    layer_part = (gate_values[:, 0:1] * chosen[0] + gate_values[:, 1:2] * chosen[1]).astype(BF)
    layer_out = spread_out(layer_part)
    cot_here = lax.dynamic_slice(cotangent, (0, t * quarter), (tok_rows, quarter)).astype(F32)
    gate_grad = lax.psum(
        jnp.stack([jnp.sum(cot_here * c, axis=1) for c in chosen], axis=1), ("wide", "tensor")
    )

    gpieces, gkept = grad_rows(
        t_arr, n, gate_o, up_o, gate_r, up_r, gh_o, gh_r, gate_mat, up_mat
    )
    greturned = send_back(gpieces, gkept)
    grad_part = (dot_nn(gather[0], greturned) + dot_nn(gather[1], greturned)).astype(BF)
    token_grad = spread_out(grad_part)
    return (layer_out, token_grad, gate_grad)


def plain_local(tokens, expert_ids, gate_values, w_gate, w_up, w_down, cotangent):
    tok_rows, depth = tokens.shape
    groups = lax.axis_size("expert")
    experts = groups * w_gate.shape[0]
    cap = min(tok_rows, 3 * tok_rows // experts)
    total_rows = groups * cap
    gate_mat, up_mat, down_mat = w_gate[0], w_up[0], w_down[0]
    order = expert_ids * cap + slot_index(expert_ids, experts)
    cells = jnp.arange(experts * cap, dtype=jnp.int32)
    pick = [order[:, k][None, :] == cells[:, None] for k in range(2)]
    gather = [(order[:, k][:, None] == cells[None, :]).astype(BF) for k in range(2)]

    def to_owners(rows):
        out = rows.astype(BF).reshape(groups, cap, depth)
        out = lax.all_to_all(out, "expert", split_axis=0, concat_axis=0, tiled=True)
        return out.reshape(total_rows, depth)

    def send_back(rows):
        share = lax.psum_scatter(rows, "tensor", scatter_dimension=0, tiled=True).astype(BF)
        return to_owners(lax.all_gather(share, "tensor", axis=0, tiled=True))

    spread = jnp.logical_or(pick[0], pick[1]).astype(BF)
    arrived = to_owners(dot_nn(spread, tokens))
    gate_pre, up_pre = lax.psum((dot_nn(arrived, gate_mat), dot_nn(arrived, up_mat)), "wide")
    s = jax.nn.sigmoid(gate_pre)
    returned = send_back(dot_nn((gate_pre * s * up_pre).astype(BF), down_mat))
    chosen = [dot_nn(g, returned) for g in gather]
    layer_out = (gate_values[:, 0:1] * chosen[0] + gate_values[:, 1:2] * chosen[1]).astype(BF)
    upstream = cotangent.astype(F32)
    gate_grad = lax.psum(
        jnp.stack([jnp.sum(upstream * c, axis=1) for c in chosen], axis=1), "wide"
    )
    slot_gate = jnp.sum(
        jnp.where(pick[0], gate_values[:, 0][None, :], 0.0)
        + jnp.where(pick[1], gate_values[:, 1][None, :], 0.0),
        axis=1,
        keepdims=True,
    )
    grad_arrived = to_owners(dot_nn(spread, cotangent) * slot_gate)
    grad_hidden = lax.psum(dot_nt(grad_arrived, down_mat), "wide")
    grad_gate = (grad_hidden * up_pre * (s * (1.0 + gate_pre * (1.0 - s)))).astype(BF)
    grad_up = (grad_hidden * (gate_pre * s)).astype(BF)
    back = send_back(dot_nt(grad_gate, gate_mat) + dot_nt(grad_up, up_mat))
    token_grad = (dot_nn(gather[0], back) + dot_nn(gather[1], back)).astype(BF)
    return (layer_out, token_grad, gate_grad)


def solution(mesh):
    in_specs = (
        P("expert", "wide"),
        P("expert", None),
        P("expert", None),
        P("expert", "wide", "tensor"),
        P("expert", "wide", "tensor"),
        P("expert", "tensor", "wide"),
        P("expert", "wide"),
    )
    out_specs = (P("expert", "wide"), P("expert", "wide"), P("expert", None))
    laid_out = mesh.shape["tensor"] == 4 and mesh.shape["expert"] == 4 and mesh.shape["wide"] == 2
    return jax.shard_map(
        local if laid_out else plain_local,
        mesh=mesh,
        in_specs=in_specs,
        out_specs=out_specs,
        check_vma=False,
    )
```

```python
import jax
import jax.numpy as jnp
from jax import lax
from jax.experimental import pallas as pl
from jax.experimental.pallas import tpu as pltpu
from jax.sharding import PartitionSpec as P

BF = jnp.bfloat16
F32 = jnp.float32
MIB = 1024 * 1024


def slot_index(expert_ids, experts):
    hit_table = (expert_ids[:, :, None] == jnp.arange(experts, dtype=jnp.int32)).astype(jnp.int32)
    per_row = jnp.sum(hit_table, axis=1)
    before = jnp.cumsum(per_row, axis=0) - per_row
    return jnp.sum(hit_table * before[:, None, :], axis=2)


def exchange(array, axis, bit):
    size = lax.axis_size(axis)
    return lax.ppermute(array, axis, [(i, i ^ bit) for i in range(size)])


def dot_nn(a, b):
    return jnp.dot(a, b, preferred_element_type=F32)


def dot_nt(a, b):
    return lax.dot_general(a, b, (((1,), (1,)), ((), ())), preferred_element_type=F32)


def params(mib):
    return pltpu.CompilerParams(vmem_limit_bytes=mib * MIB)


def whole(shape):
    zeros = (0,) * len(shape)
    return pl.BlockSpec(shape, lambda i, *_: zeros, pipeline_mode=pl.Buffered(1))


def sds(shape, dtype):
    return jax.ShapeDtypeStruct(shape, dtype)


def cost(flops, nbytes):
    return pl.CostEstimate(flops=flops, bytes_accessed=nbytes, transcendentals=0)


def gather_rows(t, own_ref, parts, rows_ref):
    cap = own_ref.shape[0]
    n = len(parts)
    quarter = parts[0].shape[1]
    for q in range(n):
        rows_ref[q, :cap, :] = own_ref[:, q * quarter : (q + 1) * quarter]
    for j in range(n):
        rows_ref[t ^ j, cap:, :] = parts[j][...]


def pre_act_kernel(t_ref, own_ref, *refs):
    parts, (gate_w, up_w, gate_o, up_o, gate_s, up_s, rows_ref) = refs[:-7], refs[-7:]

    @pl.when(pl.program_id(0) == 0)
    def _():
        gather_rows(t_ref[0], own_ref, parts, rows_ref)

    n, _, quarter = rows_ref.shape
    for w, out, send in ((gate_w, gate_o, gate_s), (up_w, up_o, up_s)):
        total = dot_nn(rows_ref[0], w[:quarter, :])
        for q in range(1, n):
            total += dot_nn(rows_ref[q], w[q * quarter : (q + 1) * quarter, :])
        out[...] = total
        send[...] = total.astype(BF)


def pre_acts(t, own, parts, gate_mat, up_mat, block, start, stop):
    depth, hidden = gate_mat.shape[0], stop - start
    first = start // block
    cap = own.shape[0]
    n = len(parts)
    rows = cap + parts[0].shape[0]
    weight = pl.BlockSpec((depth, block), lambda i, *_: (0, first + i))
    out = pl.BlockSpec((rows, block), lambda i, *_: (0, i))
    return pl.pallas_call(
        pre_act_kernel,
        grid_spec=pltpu.PrefetchScalarGridSpec(
            num_scalar_prefetch=1,
            grid=(hidden // block,),
            in_specs=[whole(own.shape)] + [whole(p.shape) for p in parts] + [weight, weight],
            out_specs=[out] * 4,
            scratch_shapes=[pltpu.VMEM((n, rows, depth // n), BF)],
        ),
        out_shape=[sds((rows, hidden), F32)] * 2 + [sds((rows, hidden), BF)] * 2,
        compiler_params=params(40),
        cost_estimate=cost(4 * rows * depth * hidden, 4 * depth * hidden),
        name="pre_acts",
    )(t, own, *parts, gate_mat, up_mat)


def grad_hidden_kernel(t_ref, own_ref, *refs):
    parts, (down_w, out, send, rows_ref) = refs[:-4], refs[-4:]

    @pl.when(pl.program_id(0) == 0)
    def _():
        gather_rows(t_ref[0], own_ref, parts, rows_ref)

    n, _, quarter = rows_ref.shape
    total = dot_nt(rows_ref[0], down_w[:, :quarter])
    for q in range(1, n):
        total += dot_nt(rows_ref[q], down_w[:, q * quarter : (q + 1) * quarter])
    out[...] = total
    send[...] = total.astype(BF)


def grad_hiddens(t, own, parts, down_mat, block, start, stop):
    depth, hidden = down_mat.shape[1], stop - start
    first = start // block
    n = len(parts)
    rows = own.shape[0] + parts[0].shape[0]
    weight = pl.BlockSpec((block, depth), lambda i, *_: (first + i, 0))
    out = pl.BlockSpec((rows, block), lambda i, *_: (0, i))
    return pl.pallas_call(
        grad_hidden_kernel,
        grid_spec=pltpu.PrefetchScalarGridSpec(
            num_scalar_prefetch=1,
            grid=(hidden // block,),
            in_specs=[whole(own.shape)] + [whole(p.shape) for p in parts] + [weight],
            out_specs=[out] * 2,
            scratch_shapes=[pltpu.VMEM((n, rows, depth // n), BF)],
        ),
        out_shape=[sds((rows, hidden), F32), sds((rows, hidden), BF)],
        compiler_params=params(40),
        cost_estimate=cost(2 * rows * depth * hidden, 2 * depth * hidden),
        name="grad_hidden",
    )(t, own, *parts, down_mat)


STRIP = 32


def hidden_strips(*refs):
    groups, hidden_ref = refs[:-1], refs[-1]

    @pl.loop(0, hidden_ref.shape[0] // STRIP)
    def _(i):
        here = pl.ds(pl.multiple_of(i * STRIP, STRIP), STRIP)
        at = 0
        for g in range(0, len(groups), 4):
            gate_o, up_o, gate_r, up_r = groups[g : g + 4]
            width = gate_o.shape[1]
            gate = gate_o[here, :] + gate_r[here, :].astype(F32)
            up = up_o[here, :] + up_r[here, :].astype(F32)
            hidden_ref[here, at : at + width] = (gate * jax.nn.sigmoid(gate) * up).astype(BF)
            at += width


def grad_strips(*refs):
    refs, (gg_ref, gu_ref) = refs[:-2], refs[-2:]
    share = len(refs) // 6
    groups, grads = refs[: 4 * share], refs[4 * share :]

    @pl.loop(0, gg_ref.shape[0] // STRIP)
    def _(i):
        here = pl.ds(pl.multiple_of(i * STRIP, STRIP), STRIP)
        at = 0
        for g in range(0, len(groups), 4):
            gate_o, up_o, gate_r, up_r = groups[g : g + 4]
            gh_o, gh_r = grads[g // 2 : g // 2 + 2]
            cols = slice(at, at + gate_o.shape[1])
            gate = gate_o[here, :] + gate_r[here, :].astype(F32)
            up = up_o[here, :] + up_r[here, :].astype(F32)
            grad = gh_o[here, :] + gh_r[here, :].astype(F32)
            s = jax.nn.sigmoid(gate)
            gg_ref[here, cols] = (grad * up * (s * (1.0 + gate * (1.0 - s)))).astype(BF)
            gu_ref[here, cols] = (grad * (gate * s)).astype(BF)
            at += gate_o.shape[1]


def first_piece_kernel(make, product, n_in, n_w, n_act):
    def kernel(t_ref, *refs):
        ins, refs = refs[:n_in], refs[n_in:]
        weights, refs = refs[:n_w], refs[n_w:]
        halves, acts = refs[:2], refs[2:]

        @pl.when(pl.program_id(0) == 0)
        def _():
            make(*ins, *acts)

        total = product(acts, weights).astype(BF)
        for h in range(2):

            @pl.when(pl.program_id(0) == h)
            def _():
                halves[h][...] = total

    return kernel


def rest_kernel(product, n_act, n_w, order):
    def kernel(t_ref, *refs):
        acts, refs = refs[:n_act], refs[n_act:]
        weights, refs = refs[:n_w], refs[n_w:]
        added, outs = (refs[:2], refs[2:]) if 1 in order else ((), refs)
        total = product(acts, weights)
        half = total.shape[1] // 2
        for i, j in enumerate(order):

            @pl.when(pl.program_id(0) == i)
            def _():
                if j == 0:
                    outs[i][...] = total
                elif j == 1:
                    outs[i][:, :half] = total[:, :half].astype(BF)
                    outs[i][:, half:] = (total[:, half:] + added[1][...].astype(F32)).astype(BF)
                else:
                    outs[i][:, :half] = (total[:, :half] + added[0][...].astype(F32)).astype(BF)
                    outs[i][:, half:] = total[:, half:].astype(BF)

    return kernel


def forward_product(acts, weights):
    return dot_nn(acts[0][...], weights[0][...])


def backward_product(acts, weights):
    return dot_nt(acts[0][...], weights[0][...]) + dot_nt(acts[1][...], weights[1][...])


def weight_specs(mats, nn, block, index):
    if nn:
        return [pl.BlockSpec((m.shape[0], block), lambda i, t: (0, index(i, t))) for m in mats]
    return [pl.BlockSpec((block, m.shape[1]), lambda i, t: (index(i, t), 0)) for m in mats]


def sizes(mats, nn):
    return mats[0].shape if nn else mats[0].shape[::-1]


def first_piece(t, n, make, product, nn, ins, mats, mib, name):
    hidden, depth = sizes(mats, nn)
    rows = ins[0].shape[0]
    half = depth // n // 2
    acts = [sds((rows, hidden), BF)] * len(mats)
    return pl.pallas_call(
        first_piece_kernel(make, product, len(ins), len(mats), len(acts)),
        grid_spec=pltpu.PrefetchScalarGridSpec(
            num_scalar_prefetch=1,
            grid=(2,),
            in_specs=[whole(x.shape) for x in ins]
            + weight_specs(mats, nn, half, lambda i, t: (t[0] ^ 3) * 2 + i),
            out_specs=[pl.BlockSpec((rows, half), lambda i, t: (0, 0))] * 2
            + [pl.BlockSpec((rows, hidden), lambda i, t: (0, 0))] * len(acts),
        ),
        out_shape=[sds((rows, half), BF)] * 2 + acts,
        compiler_params=params(mib),
        cost_estimate=cost(2 * rows * depth * hidden * len(mats) // n, 2 * depth * hidden),
        name=name,
    )(t, *ins, *mats)


def rest_pieces(t, n, product, nn, acts, mats, added, order, mib, name):
    hidden, depth = sizes(mats, nn)
    rows = acts[0].shape[0]
    quarter = depth // n

    def index(i, t):
        j = order[-1]
        for k in range(len(order) - 2, -1, -1):
            j = jnp.where(i == k, order[k], j)
        return t[0] ^ j

    return pl.pallas_call(
        rest_kernel(product, len(acts), len(mats), order),
        grid_spec=pltpu.PrefetchScalarGridSpec(
            num_scalar_prefetch=1,
            grid=(len(order),),
            in_specs=[whole(x.shape) for x in acts]
            + weight_specs(mats, nn, quarter, index)
            + [whole(x.shape) for x in added],
            out_specs=[pl.BlockSpec((rows, quarter), lambda i, t: (0, 0))] * len(order),
        ),
        out_shape=[sds((rows, quarter), F32 if j == 0 else BF) for j in order],
        compiler_params=params(mib),
        cost_estimate=cost(
            2 * rows * quarter * len(order) * hidden * len(mats), 2 * quarter * len(order) * hidden
        ),
        name=name,
    )(t, *acts, *mats, *added)


def assemble_kernel(t_ref, *refs):
    parts, out = refs[:-1], refs[-1]
    width = parts[0].shape[1]
    for j, part in enumerate(parts):
        out[:, pl.ds(pl.multiple_of((t_ref[0] ^ j) * width, 128), width)] = part[...]


def assemble(t, parts):
    rows, width = parts[0].shape
    return pl.pallas_call(
        assemble_kernel,
        grid_spec=pltpu.PrefetchScalarGridSpec(
            num_scalar_prefetch=1,
            grid=(1,),
            in_specs=[whole(p.shape) for p in parts],
            out_specs=pl.BlockSpec((rows, width * len(parts)), lambda i, t: (0, 0)),
        ),
        out_shape=sds((rows, width * len(parts)), parts[0].dtype),
        compiler_params=params(16),
        name="assemble",
    )(t, *parts)


def after(value, *others):
    return lax.optimization_barrier((value,) + others)[0]


def local(tokens, expert_ids, gate_values, w_gate, w_up, w_down, cotangent):
    tok_rows, depth = tokens.shape
    groups = lax.axis_size("expert")
    n = lax.axis_size("tensor")
    z = lax.axis_index("expert")
    t = lax.axis_index("tensor")
    t_arr = t.astype(jnp.int32).reshape(1)
    experts = groups
    cap = min(tok_rows, 3 * tok_rows // experts)
    quarter = depth // n
    half = quarter // 2
    gate_mat, up_mat, down_mat = (
        pltpu.with_memory_space_constraint(w[0], pltpu.HBM) for w in (w_gate, w_up, w_down)
    )

    slot_of = slot_index(expert_ids, experts)
    order = (expert_ids ^ z) * cap + slot_of
    cells = jnp.arange(experts * cap, dtype=jnp.int32)
    pick = [order[:, k][None, :] == cells[:, None] for k in range(2)]
    spread = jnp.logical_or(pick[0], pick[1]).astype(BF)
    slot_gate = jnp.sum(
        jnp.where(pick[0], gate_values[:, 0][None, :], 0.0)
        + jnp.where(pick[1], gate_values[:, 1][None, :], 0.0),
        axis=1,
        keepdims=True,
    )

    def outgoing(source, scale):
        part = lax.dynamic_slice(source, (0, t * quarter), (tok_rows, quarter))
        out = dot_nn(spread[cap:], part)
        own = dot_nn(spread[:cap], source)
        if scale is not None:
            out, own = out * scale[cap:], own * scale[:cap]
        return own.astype(BF), out.astype(BF)

    def over_z(out):
        return jnp.concatenate(
            [exchange(out[(k - 1) * cap : k * cap], "expert", k) for k in range(1, groups)], axis=0
        )

    tok_own, tok_out = outgoing(tokens, None)
    cot_own, cot_out = outgoing(cotangent, slot_gate)
    tok_part = over_z(tok_out)
    tok_x, tok_y = exchange(tok_part, "tensor", 1), exchange(tok_part, "tensor", 2)
    cot_part = over_z(after(cot_out, tok_part))
    tok_d = jnp.concatenate(
        [exchange(tok_y[:, :half], "tensor", 1), exchange(tok_x[:, half:], "tensor", 2)], axis=1
    )
    tok_parts = [tok_part, tok_x, tok_y, tok_d]
    cot_ready = after(cot_part, tok_d)
    cot_parts = [cot_part] + [exchange(cot_ready, "tensor", j) for j in range(1, n)]

    acts_in = ()
    hidden_here = gate_mat.shape[1]
    turn = after(t_arr, cot_part)
    for start in range(0, hidden_here, hidden_here // 2):
        if start:
            turn = after(t_arr, *cot_parts[1:3])
        gate_o, up_o, gate_s, up_s = pre_acts(
            turn, tok_own, tok_parts, gate_mat, up_mat, 512, start, start + hidden_here // 2
        )
        acts_in += (gate_o, up_o, exchange(gate_s, "wide", 1), exchange(up_s, "wide", 1))

    def sum_back(rest, keep):
        total = keep
        for j, piece in zip((1, 2), rest):
            total = total + exchange(piece, "tensor", j).astype(F32)
        total = total.astype(BF)
        back = [total[:cap]] + [
            exchange(total[k * cap : (k + 1) * cap], "expert", k) for k in range(1, groups)
        ]
        return jnp.concatenate(back, axis=0)

    def gathered(part):
        return assemble(t_arr, [part] + [exchange(part, "tensor", j) for j in range(1, n)])

    gather = [(order[:, k][:, None] == cells[None, :]).astype(BF) for k in range(2)]

    d_a, d_b, hidden = first_piece(
        t_arr, n, hidden_strips, forward_product, True, acts_in, [down_mat], 36, "project_first"
    )
    added = [exchange(d_a, "tensor", 1), exchange(d_b, "tensor", 2)]
    gh_in = ()
    for start in range(0, hidden_here, hidden_here // 2):
        turn = after(t_arr, *added) if start else after(t_arr, hidden)
        gh_o, gh_s = grad_hiddens(
            turn, cot_own, cot_parts, down_mat, 512, start, start + hidden_here // 2
        )
        gh_in += (gh_o, exchange(gh_s, "wide", 1))
    to_x, to_y, keep = rest_pieces(
        t_arr, n, forward_product, True, [hidden], [down_mat], added, (1, 2, 0), 34, "project_rest"
    )

    e_a, e_b, grad_g, grad_u = first_piece(
        t_arr, n, grad_strips, backward_product, False, acts_in + gh_in,
        [gate_mat, up_mat], 36, "rows_first",
    )
    gadded = [exchange(e_a, "tensor", 1), exchange(e_b, "tensor", 2)]
    (gkeep,) = rest_pieces(
        t_arr, n, backward_product, False, [grad_g, grad_u], [gate_mat, up_mat], [], (0,), 47,
        "rows_kept",
    )
    gto_x, gto_y = rest_pieces(
        after(t_arr, gkeep), n, backward_product, False, [grad_g, grad_u], [gate_mat, up_mat], gadded, (1, 2),
        47, "rows_rest",
    )

    returned = sum_back((to_x, to_y), after(keep, e_a))
    chosen = [dot_nn(g, returned) for g in gather]
    layer_part = (gate_values[:, 0:1] * chosen[0] + gate_values[:, 1:2] * chosen[1]).astype(BF)
    layer_out = gathered(layer_part)
    cot_here = lax.dynamic_slice(cotangent, (0, t * quarter), (tok_rows, quarter)).astype(F32)
    gate_grad = jnp.stack([jnp.sum(cot_here * c, axis=1) for c in chosen], axis=0)
    for axis, bit in (("wide", 1), ("tensor", 1), ("tensor", 2)):
        gate_grad = gate_grad + exchange(gate_grad, axis, bit)

    greturned = sum_back((gto_x, gto_y), gkeep)
    grad_part = (dot_nn(gather[0], greturned) + dot_nn(gather[1], greturned)).astype(BF)
    token_grad = gathered(grad_part)
    return (layer_out, token_grad, gate_grad.T)


def plain_local(tokens, expert_ids, gate_values, w_gate, w_up, w_down, cotangent):
    tok_rows, depth = tokens.shape
    groups = lax.axis_size("expert")
    experts = groups * w_gate.shape[0]
    cap = min(tok_rows, 3 * tok_rows // experts)
    total_rows = groups * cap
    gate_mat, up_mat, down_mat = w_gate[0], w_up[0], w_down[0]
    order = expert_ids * cap + slot_index(expert_ids, experts)
    cells = jnp.arange(experts * cap, dtype=jnp.int32)
    pick = [order[:, k][None, :] == cells[:, None] for k in range(2)]
    gather = [(order[:, k][:, None] == cells[None, :]).astype(BF) for k in range(2)]

    def to_owners(rows):
        out = rows.astype(BF).reshape(groups, cap, depth)
        out = lax.all_to_all(out, "expert", split_axis=0, concat_axis=0, tiled=True)
        return out.reshape(total_rows, depth)

    def send_back(rows):
        share = lax.psum_scatter(rows, "tensor", scatter_dimension=0, tiled=True).astype(BF)
        return to_owners(lax.all_gather(share, "tensor", axis=0, tiled=True))

    spread = jnp.logical_or(pick[0], pick[1]).astype(BF)
    arrived = to_owners(dot_nn(spread, tokens))
    gate_pre, up_pre = lax.psum((dot_nn(arrived, gate_mat), dot_nn(arrived, up_mat)), "wide")
    s = jax.nn.sigmoid(gate_pre)
    returned = send_back(dot_nn((gate_pre * s * up_pre).astype(BF), down_mat))
    chosen = [dot_nn(g, returned) for g in gather]
    layer_out = (gate_values[:, 0:1] * chosen[0] + gate_values[:, 1:2] * chosen[1]).astype(BF)
    upstream = cotangent.astype(F32)
    gate_grad = lax.psum(
        jnp.stack([jnp.sum(upstream * c, axis=1) for c in chosen], axis=1), "wide"
    )
    slot_gate = jnp.sum(
        jnp.where(pick[0], gate_values[:, 0][None, :], 0.0)
        + jnp.where(pick[1], gate_values[:, 1][None, :], 0.0),
        axis=1,
        keepdims=True,
    )
    grad_arrived = to_owners(dot_nn(spread, cotangent) * slot_gate)
    grad_hidden = lax.psum(dot_nt(grad_arrived, down_mat), "wide")
    grad_gate = (grad_hidden * up_pre * (s * (1.0 + gate_pre * (1.0 - s)))).astype(BF)
    grad_up = (grad_hidden * (gate_pre * s)).astype(BF)
    back = send_back(dot_nt(grad_gate, gate_mat) + dot_nt(grad_up, up_mat))
    token_grad = (dot_nn(gather[0], back) + dot_nn(gather[1], back)).astype(BF)
    return (layer_out, token_grad, gate_grad)


def solution(mesh):
    in_specs = (
        P("expert", "wide"),
        P("expert", None),
        P("expert", None),
        P("expert", "wide", "tensor"),
        P("expert", "wide", "tensor"),
        P("expert", "tensor", "wide"),
        P("expert", "wide"),
    )
    out_specs = (P("expert", "wide"), P("expert", "wide"), P("expert", None))
    laid_out = mesh.shape["tensor"] == 4 and mesh.shape["expert"] == 4 and mesh.shape["wide"] == 2
    return jax.shard_map(
        local if laid_out else plain_local,
        mesh=mesh,
        in_specs=in_specs,
        out_specs=out_specs,
        check_vma=False,
    )
```

```python
import jax
import jax.numpy as jnp
from jax import lax
from jax.experimental import pallas as pl
from jax.experimental.pallas import tpu as pltpu
from jax.sharding import PartitionSpec as P

BF = jnp.bfloat16
F32 = jnp.float32
MIB = 1024 * 1024


def slot_index(expert_ids, experts):
    hit_table = (expert_ids[:, :, None] == jnp.arange(experts, dtype=jnp.int32)).astype(jnp.int32)
    per_row = jnp.sum(hit_table, axis=1)
    before = jnp.cumsum(per_row, axis=0) - per_row
    return jnp.sum(hit_table * before[:, None, :], axis=2)


def exchange(array, axis, bit):
    size = lax.axis_size(axis)
    return lax.ppermute(array, axis, [(i, i ^ bit) for i in range(size)])


def dot_nn(a, b):
    return jnp.dot(a, b, preferred_element_type=F32)


def dot_nt(a, b):
    return lax.dot_general(a, b, (((1,), (1,)), ((), ())), preferred_element_type=F32)


def params(mib):
    return pltpu.CompilerParams(vmem_limit_bytes=mib * MIB)


VMEM = pl.BlockSpec(memory_space=pltpu.VMEM)
HBM = pl.BlockSpec(memory_space=pltpu.HBM)
SMEM = pl.BlockSpec(memory_space=pltpu.SMEM)


def sds(shape, dtype):
    return jax.ShapeDtypeStruct(shape, dtype)


def call(kernel, t, ins, outs, scratch, flops, mib, name, far=0):
    return pl.pallas_call(
        kernel,
        in_specs=[SMEM] + [VMEM] * (len(ins) - far) + [HBM] * far,
        out_specs=[VMEM] * len(outs),
        out_shape=outs,
        scratch_shapes=scratch,
        compiler_params=params(mib),
        cost_estimate=pl.CostEstimate(flops=flops, bytes_accessed=MIB, transcendentals=0),
        name=name,
    )(t, *ins)


def fetch(matrix):
    def kernel(source, held, sem):
        copy = pltpu.make_async_copy(source, held, sem)
        copy.start()
        copy.wait()

    return pl.pallas_call(
        kernel,
        in_specs=[HBM],
        out_specs=VMEM,
        out_shape=pltpu.VMEM(matrix.shape, matrix.dtype),
        scratch_shapes=[pltpu.SemaphoreType.DMA],
        compiler_params=params(LIMIT),
        cost_estimate=pl.CostEstimate(
            flops=0, bytes_accessed=2 * matrix.size, transcendentals=0
        ),
        name="fetch",
    )(matrix)


def lay_out(t, own, parts, rows_ref):
    cap = own.shape[0]
    n, _, quarter = rows_ref.shape
    for q in range(n):
        rows_ref[q, :cap, :] = own[:, q * quarter : (q + 1) * quarter]
    for j in range(n):
        at = cap
        for piece in parts[j]:
            rows_ref[t ^ j, at : at + piece.shape[0], :] = piece[...]
            at += piece.shape[0]


def split_parts(refs, counts):
    parts, at = [], 0
    for c in counts:
        parts.append(refs[at : at + c])
        at += c
    return parts, refs[at:]


BLOCK = 256


def pre_acts(t, own, parts, gate_mat, up_mat, start, stop):
    depth = gate_mat.shape[0]
    n = len(parts)
    quarter = depth // n
    rows = own.shape[0] + sum(p.shape[0] for p in parts[0])
    counts = [len(p) for p in parts]

    def kernel(t_ref, own_ref, *refs):
        pieces, refs = split_parts(refs, counts)
        gate_w, up_w, gate_o, up_o, gate_s, up_s, rows_ref = refs
        lay_out(t_ref[0], own_ref, pieces, rows_ref)

        @pl.loop(0, (stop - start) // BLOCK)
        def _(i):
            off = pl.multiple_of(i * BLOCK, BLOCK)
            for w, out, send in ((gate_w, gate_o, gate_s), (up_w, up_o, up_s)):
                total = None
                for q in range(n):
                    part = dot_nn(
                        rows_ref[q], w[q * quarter : (q + 1) * quarter, pl.ds(start + off, BLOCK)]
                    )
                    total = part if total is None else total + part
                out[:, pl.ds(off, BLOCK)] = total
                send[:, pl.ds(off, BLOCK)] = total.astype(BF)

    shape = (rows, stop - start)
    return call(
        kernel,
        t,
        [own] + [x for p in parts for x in p] + [gate_mat, up_mat],
        [sds(shape, F32)] * 2 + [sds(shape, BF)] * 2,
        [pltpu.VMEM((n, rows, quarter), BF)],
        4 * rows * depth * (stop - start),
        LIMIT,
        "pre_acts",
    )


def grad_hiddens(t, own, parts, down_mat, start, stop):
    depth = down_mat.shape[1]
    n = len(parts)
    quarter = depth // n
    rows = own.shape[0] + sum(p.shape[0] for p in parts[0])
    counts = [len(p) for p in parts]

    steps = (stop - start) // BLOCK

    def kernel(t_ref, own_ref, *refs):
        pieces, refs = split_parts(refs, counts)
        down_w, out, send, rows_ref, held, sems = refs
        copies = [
            pltpu.make_async_copy(
                down_w.at[pl.ds(start + i * BLOCK, BLOCK)], held.at[i], sems.at[i]
            )
            for i in range(steps)
        ]
        for copy in copies:
            copy.start()
        lay_out(t_ref[0], own_ref, pieces, rows_ref)
        for i in range(steps):
            copies[i].wait()
            total = None
            for q in range(n):
                part = dot_nt(rows_ref[q], held[i, :, q * quarter : (q + 1) * quarter])
                total = part if total is None else total + part
            out[:, i * BLOCK : (i + 1) * BLOCK] = total
            send[:, i * BLOCK : (i + 1) * BLOCK] = total.astype(BF)

    shape = (rows, stop - start)
    return call(
        kernel,
        t,
        [own] + [x for p in parts for x in p] + [down_mat],
        [sds(shape, F32), sds(shape, BF)],
        [
            pltpu.VMEM((n, rows, quarter), BF),
            pltpu.VMEM((steps, BLOCK, depth), BF),
            pltpu.SemaphoreType.DMA((steps,)),
        ],
        2 * rows * depth * (stop - start),
        12,
        "grad_hidden",
        far=1,
    )


STRIP = 32
LIMIT = 8


def strips(rows, body):
    @pl.loop(0, rows // STRIP)
    def _(i):
        body(pl.ds(pl.multiple_of(i * STRIP, STRIP), STRIP))


def hidden_strips(ins, acts):
    (hidden_ref,) = acts

    def body(here):
        at = 0
        for g in range(0, len(ins), 4):
            gate_o, up_o, gate_r, up_r = ins[g : g + 4]
            cols = slice(at, at + gate_o.shape[1])
            gate = gate_o[here, :] + gate_r[here, :].astype(F32)
            up = up_o[here, :] + up_r[here, :].astype(F32)
            hidden_ref[here, cols] = (gate * jax.nn.sigmoid(gate) * up).astype(BF)
            at += gate_o.shape[1]

    strips(hidden_ref.shape[0], body)


def grad_strips(ins, acts):
    gg_ref, gu_ref = acts

    def body(here):
        at = 0
        for g in range(0, len(ins), 6):
            gate_o, up_o, gate_r, up_r, gh_o, gh_r = ins[g : g + 6]
            cols = slice(at, at + gate_o.shape[1])
            gate = gate_o[here, :] + gate_r[here, :].astype(F32)
            up = up_o[here, :] + up_r[here, :].astype(F32)
            grad = gh_o[here, :] + gh_r[here, :].astype(F32)
            s = jax.nn.sigmoid(gate)
            gg_ref[here, cols] = (grad * up * (s * (1.0 + gate * (1.0 - s)))).astype(BF)
            gu_ref[here, cols] = (grad * (gate * s)).astype(BF)
            at += gate_o.shape[1]

    strips(gg_ref.shape[0], body)


class Stream:
    def __init__(self, mats, n, nn, pieces):
        self.mats, self.nn = len(mats), nn
        self.hidden, depth = mats[0].shape if nn else mats[0].shape[::-1]
        self.quarter = depth // n
        self.width = self.quarter if nn else BLOCK
        self.each = self.quarter // self.width
        chunk = (self.hidden, self.width) if nn else (self.width, self.hidden)
        count = pieces * self.each * self.mats
        self.scratch = [pltpu.VMEM((count,) + chunk, BF), pltpu.SemaphoreType.DMA((count,))]
        self.mib = 2 + 2 * count * self.hidden * self.width // MIB

    def start(self, weights, bases, held, sems):
        self.held, self.copies = held, []
        for base in bases:
            for c in range(self.each):
                cut = pl.ds(pl.multiple_of(base + c * self.width, BLOCK), self.width)
                for w in weights:
                    source = w.at[:, cut] if self.nn else w.at[cut]
                    k = len(self.copies)
                    self.copies.append(pltpu.make_async_copy(source, held.at[k], sems.at[k]))
                    self.copies[-1].start()

    def products(self, piece, acts):
        for c in range(self.each):
            total = None
            for m in range(self.mats):
                k = (piece * self.each + c) * self.mats + m
                self.copies[k].wait()
                dot = dot_nn if self.nn else dot_nt
                part = dot(acts[m][...], self.held[k])
                total = part if total is None else total + part
            yield slice(c * self.width, (c + 1) * self.width), total


def first_piece(t, n, make, nn, ins, mats, name):
    stream = Stream(mats, n, nn, 1)
    rows = ins[0].shape[0]
    half, quarter, hidden = rows // 2, stream.quarter, stream.hidden

    def kernel(t_ref, *refs):
        parts, refs = refs[: len(ins)], refs[len(ins) :]
        weights, refs = refs[: len(mats)], refs[len(mats) :]
        halves, acts, scratch = refs[:2], refs[2 : 2 + len(mats)], refs[2 + len(mats) :]
        stream.start(weights, [(t_ref[0] ^ 3) * quarter], *scratch)
        make(parts, acts)
        for cols, total in stream.products(0, acts):
            halves[0][:, cols] = total[:half].astype(BF)
            halves[1][:, cols] = total[half:].astype(BF)

    return call(
        kernel,
        t,
        list(ins) + list(mats),
        [sds((half, quarter), BF)] * 2 + [sds((rows, hidden), BF)] * len(mats),
        stream.scratch,
        2 * rows * quarter * hidden * len(mats),
        stream.mib + 4,
        name,
        far=len(mats),
    )


def pieces(t, n, nn, acts, mats, order, name):
    stream = Stream(mats, n, nn, len(order))
    rows, quarter = acts[0].shape[0], stream.quarter

    def kernel(t_ref, *refs):
        ins, refs = refs[: len(acts)], refs[len(acts) :]
        weights, refs = refs[: len(mats)], refs[len(mats) :]
        outs, scratch = refs[: len(order)], refs[len(order) :]
        stream.start(weights, [(t_ref[0] ^ j) * quarter for j in order], *scratch)
        for k, out in enumerate(outs):
            for cols, total in stream.products(k, ins):
                out[:, cols] = total

    return call(
        kernel,
        t,
        list(acts) + list(mats),
        [sds((rows, quarter), F32)] * len(order),
        stream.scratch,
        2 * rows * quarter * len(order) * stream.hidden * len(mats),
        stream.mib + 4,
        name,
        far=len(mats),
    )


def add_diagonal(t, to_x, to_y, top, low):
    half = top.shape[0]

    def kernel(t_ref, x_ref, y_ref, top_ref, low_ref, x_out, y_out):
        x_out[:half, :] = x_ref[:half, :].astype(BF)
        x_out[half:, :] = (x_ref[half:, :] + low_ref[...].astype(F32)).astype(BF)
        y_out[:half, :] = (y_ref[:half, :] + top_ref[...].astype(F32)).astype(BF)
        y_out[half:, :] = y_ref[half:, :].astype(BF)

    return call(
        kernel, t, [to_x, to_y, top, low], [sds(to_x.shape, BF)] * 2, [], to_x.size, LIMIT, "add"
    )


def assemble(t, parts):
    rows, width = parts[0].shape

    def kernel(t_ref, *refs):
        for j, part in enumerate(refs[:-1]):
            refs[-1][:, pl.ds(pl.multiple_of((t_ref[0] ^ j) * width, 128), width)] = part[...]

    (out,) = call(
        kernel, t, parts, [sds((rows, width * len(parts)), parts[0].dtype)], [], 0, LIMIT, "assemble"
    )
    return out


def after(value, *others):
    return lax.optimization_barrier((value,) + others)[0]


def local(tokens, expert_ids, gate_values, w_gate, w_up, w_down, cotangent):
    tok_rows, depth = tokens.shape
    groups = lax.axis_size("expert")
    n = lax.axis_size("tensor")
    z = lax.axis_index("expert")
    t = lax.axis_index("tensor")
    t_arr = t.astype(jnp.int32).reshape(1)
    experts = groups
    cap = min(tok_rows, 3 * tok_rows // experts)
    quarter = depth // n
    gate_mat, up_mat, down_mat = (
        pltpu.with_memory_space_constraint(w[0], pltpu.HBM) for w in (w_gate, w_up, w_down)
    )
    gate_held, up_held = fetch(gate_mat), fetch(up_mat)
    hidden_here = gate_mat.shape[1]

    slot_of = slot_index(expert_ids, experts)
    order = (expert_ids ^ z) * cap + slot_of
    cells = jnp.arange(experts * cap, dtype=jnp.int32)
    pick = [order[:, k][None, :] == cells[:, None] for k in range(2)]
    spread = jnp.logical_or(pick[0], pick[1]).astype(BF)
    slot_gate = jnp.sum(
        jnp.where(pick[0], gate_values[:, 0][None, :], 0.0)
        + jnp.where(pick[1], gate_values[:, 1][None, :], 0.0),
        axis=1,
        keepdims=True,
    )

    def outgoing(source, scale):
        part = lax.dynamic_slice(source, (0, t * quarter), (tok_rows, quarter))
        out = dot_nn(spread[cap:], part)
        own = dot_nn(spread[:cap], source)
        if scale is not None:
            out, own = out * scale[cap:], own * scale[:cap]
        return own.astype(BF), out.astype(BF)

    def over_z(out):
        return [exchange(out[(k - 1) * cap : k * cap], "expert", k) for k in range(1, groups)]

    tok_own, tok_out = outgoing(tokens, None)
    cot_own, cot_out = outgoing(cotangent, slot_gate)
    tok_part = jnp.concatenate(over_z(tok_out), axis=0)
    tok_x, tok_y = exchange(tok_part, "tensor", 1), exchange(tok_part, "tensor", 2)
    cot_pieces = over_z(after(cot_out, tok_part))
    split = tok_part.shape[0] // 2
    tok_d = [exchange(tok_y[:split], "tensor", 1), exchange(tok_x[split:], "tensor", 2)]
    tok_d[0], tok_d[1], *cot_pieces = lax.optimization_barrier((*tok_d, *cot_pieces))
    tok_parts = [[tok_part], [tok_x], [tok_y], tok_d]
    cot_part = jnp.concatenate(cot_pieces, axis=0)
    cot_parts = [[cot_part]] + [[exchange(cot_part, "tensor", j)] for j in range(1, n)]

    turn = after(t_arr, cot_part)
    pres = []
    for start in range(0, hidden_here, hidden_here // 2):
        if start:
            turn = after(t_arr, cot_parts[1][0], cot_parts[2][0])
        gate_o, up_o, gate_s, up_s = pre_acts(
            turn, tok_own, tok_parts, gate_held, up_held, start, start + hidden_here // 2
        )
        pres.append([gate_o, up_o, exchange(gate_s, "wide", 1), exchange(up_s, "wide", 1)])

    def sum_back(arrived, keep, *others):
        total = keep
        for piece in arrived:
            total = total + piece.astype(F32)
        total = total.astype(BF)
        back = [total[:cap]] + [
            exchange(total[k * cap : (k + 1) * cap], "expert", k) for k in range(1, groups)
        ]
        back = lax.optimization_barrier((*back, *others))[:groups]
        return jnp.concatenate(back, axis=0)

    def gathered(part):
        return assemble(t_arr, [part] + [exchange(part, "tensor", j) for j in range(1, n)])

    gather = [(order[:, k][:, None] == cells[None, :]).astype(BF) for k in range(2)]

    d_top, d_low, hidden = first_piece(
        t_arr, n, hidden_strips, True, sum(pres, []), [down_mat], "project_first"
    )
    added = [exchange(d_top, "tensor", 1), exchange(d_low, "tensor", 2)]
    to_x, to_y = pieces(t_arr, n, True, [hidden], [down_mat], (1, 2), "project_send")
    grads = []
    turn = after(t_arr, to_x)
    for start in range(0, hidden_here, hidden_here // 2):
        if start:
            to_x, to_y = add_diagonal(t_arr, to_x, to_y, *added)
            turn = after(t_arr, to_x)
        gh_o, gh_s = grad_hiddens(
            turn, cot_own, cot_parts, down_mat, start, start + hidden_here // 2
        )
        grads.append([gh_o, exchange(gh_s, "wide", 1)])
    (keep,) = pieces(after(t_arr, gh_s), n, True, [hidden], [down_mat], (0,), "project_keep")

    e_top, e_low, grad_g, grad_u = first_piece(
        after(t_arr, keep), n, grad_strips, False,
        sum([p + g for p, g in zip(pres, grads)], []), [gate_mat, up_mat], "rows_first",
    )
    gadded = [exchange(e_top, "tensor", 1), exchange(e_low, "tensor", 2)]
    from_x, from_y = exchange(to_x, "tensor", 1), exchange(to_y, "tensor", 2)
    gto_x, gto_y = pieces(
        t_arr, n, False, [grad_g, grad_u], [gate_mat, up_mat], (1, 2), "rows_send",
    )
    gto_x, gto_y = add_diagonal(t_arr, gto_x, gto_y, *gadded)
    (gkeep,) = pieces(
        after(t_arr, gto_x), n, False, [grad_g, grad_u], [gate_mat, up_mat], (0,), "rows_keep"
    )
    returned = sum_back((from_x, from_y), after(keep, gto_x), gkeep)
    chosen = [dot_nn(g, returned) for g in gather]
    layer_part = (gate_values[:, 0:1] * chosen[0] + gate_values[:, 1:2] * chosen[1]).astype(BF)
    layer_out = gathered(layer_part)
    cot_here = lax.dynamic_slice(cotangent, (0, t * quarter), (tok_rows, quarter)).astype(F32)
    gate_grad = jnp.stack([jnp.sum(cot_here * c, axis=1) for c in chosen], axis=0)
    for axis, bit in (("wide", 1), ("tensor", 1), ("tensor", 2)):
        gate_grad = gate_grad + exchange(gate_grad, axis, bit)

    greturned = sum_back((exchange(gto_x, "tensor", 1), exchange(gto_y, "tensor", 2)), gkeep)
    grad_part = (dot_nn(gather[0], greturned) + dot_nn(gather[1], greturned)).astype(BF)
    token_grad = gathered(grad_part)
    return (layer_out, token_grad, gate_grad.T)


def plain_local(tokens, expert_ids, gate_values, w_gate, w_up, w_down, cotangent):
    tok_rows, depth = tokens.shape
    groups = lax.axis_size("expert")
    experts = groups * w_gate.shape[0]
    cap = min(tok_rows, 3 * tok_rows // experts)
    total_rows = groups * cap
    gate_mat, up_mat, down_mat = w_gate[0], w_up[0], w_down[0]
    order = expert_ids * cap + slot_index(expert_ids, experts)
    cells = jnp.arange(experts * cap, dtype=jnp.int32)
    pick = [order[:, k][None, :] == cells[:, None] for k in range(2)]
    gather = [(order[:, k][:, None] == cells[None, :]).astype(BF) for k in range(2)]

    def to_owners(rows):
        out = rows.astype(BF).reshape(groups, cap, depth)
        out = lax.all_to_all(out, "expert", split_axis=0, concat_axis=0, tiled=True)
        return out.reshape(total_rows, depth)

    def send_back(rows):
        share = lax.psum_scatter(rows, "tensor", scatter_dimension=0, tiled=True).astype(BF)
        return to_owners(lax.all_gather(share, "tensor", axis=0, tiled=True))

    spread = jnp.logical_or(pick[0], pick[1]).astype(BF)
    arrived = to_owners(dot_nn(spread, tokens))
    gate_pre, up_pre = lax.psum((dot_nn(arrived, gate_mat), dot_nn(arrived, up_mat)), "wide")
    s = jax.nn.sigmoid(gate_pre)
    returned = send_back(dot_nn((gate_pre * s * up_pre).astype(BF), down_mat))
    chosen = [dot_nn(g, returned) for g in gather]
    layer_out = (gate_values[:, 0:1] * chosen[0] + gate_values[:, 1:2] * chosen[1]).astype(BF)
    upstream = cotangent.astype(F32)
    gate_grad = lax.psum(
        jnp.stack([jnp.sum(upstream * c, axis=1) for c in chosen], axis=1), "wide"
    )
    slot_gate = jnp.sum(
        jnp.where(pick[0], gate_values[:, 0][None, :], 0.0)
        + jnp.where(pick[1], gate_values[:, 1][None, :], 0.0),
        axis=1,
        keepdims=True,
    )
    grad_arrived = to_owners(dot_nn(spread, cotangent) * slot_gate)
    grad_hidden = lax.psum(dot_nt(grad_arrived, down_mat), "wide")
    grad_gate = (grad_hidden * up_pre * (s * (1.0 + gate_pre * (1.0 - s)))).astype(BF)
    grad_up = (grad_hidden * (gate_pre * s)).astype(BF)
    back = send_back(dot_nt(grad_gate, gate_mat) + dot_nt(grad_up, up_mat))
    token_grad = (dot_nn(gather[0], back) + dot_nn(gather[1], back)).astype(BF)
    return (layer_out, token_grad, gate_grad)


def solution(mesh):
    in_specs = (
        P("expert", "wide"),
        P("expert", None),
        P("expert", None),
        P("expert", "wide", "tensor"),
        P("expert", "wide", "tensor"),
        P("expert", "tensor", "wide"),
        P("expert", "wide"),
    )
    out_specs = (P("expert", "wide"), P("expert", "wide"), P("expert", None))
    laid_out = mesh.shape["tensor"] == 4 and mesh.shape["expert"] == 4 and mesh.shape["wide"] == 2
    return jax.shard_map(
        local if laid_out else plain_local,
        mesh=mesh,
        in_specs=in_specs,
        out_specs=out_specs,
        check_vma=False,
    )
```

```python
import jax
import jax.numpy as jnp
from jax import lax
from jax.experimental import pallas as pl
from jax.experimental.pallas import tpu as pltpu
from jax.sharding import PartitionSpec as P

BF = jnp.bfloat16
F32 = jnp.float32
MIB = 1024 * 1024


def slot_index(expert_ids, experts):
    hit_table = (expert_ids[:, :, None] == jnp.arange(experts, dtype=jnp.int32)).astype(jnp.int32)
    per_row = jnp.sum(hit_table, axis=1)
    before = jnp.cumsum(per_row, axis=0) - per_row
    return jnp.sum(hit_table * before[:, None, :], axis=2)


def exchange(array, axis, bit):
    size = lax.axis_size(axis)
    return lax.ppermute(array, axis, [(i, i ^ bit) for i in range(size)])


def dot_nn(a, b):
    return jnp.dot(a, b, preferred_element_type=F32)


def dot_nt(a, b):
    return lax.dot_general(a, b, (((1,), (1,)), ((), ())), preferred_element_type=F32)


def params(mib):
    return pltpu.CompilerParams(vmem_limit_bytes=mib * MIB)


VMEM = pl.BlockSpec(memory_space=pltpu.VMEM)
HBM = pl.BlockSpec(memory_space=pltpu.HBM)
SMEM = pl.BlockSpec(memory_space=pltpu.SMEM)


def sds(shape, dtype):
    return jax.ShapeDtypeStruct(shape, dtype)


def call(kernel, t, ins, outs, scratch, flops, mib, name, far=0):
    return pl.pallas_call(
        kernel,
        in_specs=[SMEM] + [VMEM] * (len(ins) - far) + [HBM] * far,
        out_specs=[VMEM] * len(outs),
        out_shape=outs,
        scratch_shapes=scratch,
        compiler_params=params(mib),
        cost_estimate=pl.CostEstimate(flops=flops, bytes_accessed=MIB, transcendentals=0),
        name=name,
    )(t, *ins)


def fetch(matrix):
    def kernel(source, held, sem):
        copy = pltpu.make_async_copy(source, held, sem)
        copy.start()
        copy.wait()

    return pl.pallas_call(
        kernel,
        in_specs=[HBM],
        out_specs=VMEM,
        out_shape=pltpu.VMEM(matrix.shape, matrix.dtype),
        scratch_shapes=[pltpu.SemaphoreType.DMA],
        compiler_params=params(LIMIT),
        cost_estimate=pl.CostEstimate(
            flops=0, bytes_accessed=2 * matrix.size, transcendentals=0
        ),
        name="fetch",
    )(matrix)


def lay_out(t, own, parts, rows_ref):
    cap = own.shape[0]
    n, _, quarter = rows_ref.shape
    for q in range(n):
        rows_ref[q, :cap, :] = own[:, q * quarter : (q + 1) * quarter]
    for j in range(n):
        at = cap
        for piece in parts[j]:
            rows_ref[t ^ j, at : at + piece.shape[0], :] = piece[...]
            at += piece.shape[0]


def split_parts(refs, counts):
    parts, at = [], 0
    for c in counts:
        parts.append(refs[at : at + c])
        at += c
    return parts, refs[at:]


BLOCK = 256


def pre_acts(t, own, parts, gate_mat, up_mat, start, stop):
    depth = gate_mat.shape[0]
    n = len(parts)
    quarter = depth // n
    rows = own.shape[0] + sum(p.shape[0] for p in parts[0])
    counts = [len(p) for p in parts]

    def kernel(t_ref, own_ref, *refs):
        pieces, refs = split_parts(refs, counts)
        gate_w, up_w, gate_o, up_o, gate_s, up_s, rows_ref = refs
        lay_out(t_ref[0], own_ref, pieces, rows_ref)

        @pl.loop(0, (stop - start) // BLOCK)
        def _(i):
            off = pl.multiple_of(i * BLOCK, BLOCK)
            for w, out, send in ((gate_w, gate_o, gate_s), (up_w, up_o, up_s)):
                total = None
                for q in range(n):
                    part = dot_nn(
                        rows_ref[q], w[q * quarter : (q + 1) * quarter, pl.ds(start + off, BLOCK)]
                    )
                    total = part if total is None else total + part
                out[:, pl.ds(off, BLOCK)] = total
                send[:, pl.ds(off, BLOCK)] = total.astype(BF)

    shape = (rows, stop - start)
    return call(
        kernel,
        t,
        [own] + [x for p in parts for x in p] + [gate_mat, up_mat],
        [sds(shape, F32)] * 2 + [sds(shape, BF)] * 2,
        [pltpu.VMEM((n, rows, quarter), BF)],
        4 * rows * depth * (stop - start),
        LIMIT,
        "pre_acts",
    )


def grad_hiddens(t, own, parts, down_mat, start, stop):
    depth = down_mat.shape[1]
    n = len(parts)
    quarter = depth // n
    rows = own.shape[0] + sum(p.shape[0] for p in parts[0])
    counts = [len(p) for p in parts]

    block = 2 * BLOCK
    steps = (stop - start) // block

    def kernel(t_ref, own_ref, *refs):
        pieces, refs = split_parts(refs, counts)
        down_w, out, send, rows_ref, held, sems = refs
        copies = [
            pltpu.make_async_copy(
                down_w.at[pl.ds(start + i * block, block)], held.at[i], sems.at[i]
            )
            for i in range(steps)
        ]
        for copy in copies:
            copy.start()
        lay_out(t_ref[0], own_ref, pieces, rows_ref)
        for i in range(steps):
            copies[i].wait()
            total = None
            for q in range(n):
                part = dot_nt(rows_ref[q], held[i, :, q * quarter : (q + 1) * quarter])
                total = part if total is None else total + part
            out[:, i * block : (i + 1) * block] = total
            send[:, i * block : (i + 1) * block] = total.astype(BF)

    shape = (rows, stop - start)
    return call(
        kernel,
        t,
        [own] + [x for p in parts for x in p] + [down_mat],
        [sds(shape, F32), sds(shape, BF)],
        [
            pltpu.VMEM((n, rows, quarter), BF),
            pltpu.VMEM((steps, block, depth), BF),
            pltpu.SemaphoreType.DMA((steps,)),
        ],
        2 * rows * depth * (stop - start),
        12,
        "grad_hidden",
        far=1,
    )


STRIP = 32
LIMIT = 8


def strips(rows, body):
    @pl.loop(0, rows // STRIP)
    def _(i):
        body(pl.ds(pl.multiple_of(i * STRIP, STRIP), STRIP))


def hidden_strips(ins, acts):
    (hidden_ref,) = acts

    def body(here):
        at = 0
        for g in range(0, len(ins), 4):
            gate_o, up_o, gate_r, up_r = ins[g : g + 4]
            cols = slice(at, at + gate_o.shape[1])
            gate = gate_o[here, :] + gate_r[here, :].astype(F32)
            up = up_o[here, :] + up_r[here, :].astype(F32)
            hidden_ref[here, cols] = (gate * jax.nn.sigmoid(gate) * up).astype(BF)
            at += gate_o.shape[1]

    strips(hidden_ref.shape[0], body)


def grad_strips(ins, acts):
    gg_ref, gu_ref = acts

    def body(here):
        at = 0
        for g in range(0, len(ins), 6):
            gate_o, up_o, gate_r, up_r, gh_o, gh_r = ins[g : g + 6]
            cols = slice(at, at + gate_o.shape[1])
            gate = gate_o[here, :] + gate_r[here, :].astype(F32)
            up = up_o[here, :] + up_r[here, :].astype(F32)
            grad = gh_o[here, :] + gh_r[here, :].astype(F32)
            s = jax.nn.sigmoid(gate)
            gg_ref[here, cols] = (grad * up * (s * (1.0 + gate * (1.0 - s)))).astype(BF)
            gu_ref[here, cols] = (grad * (gate * s)).astype(BF)
            at += gate_o.shape[1]

    strips(gg_ref.shape[0], body)


class Stream:
    def __init__(self, mats, n, nn, pieces):
        self.mats, self.nn = len(mats), nn
        self.hidden, depth = mats[0].shape if nn else mats[0].shape[::-1]
        self.quarter = depth // n
        self.width, self.each = self.quarter, 1
        chunk = (self.hidden, self.width) if nn else (self.width, self.hidden)
        count = pieces * self.each * self.mats
        self.scratch = [pltpu.VMEM((count,) + chunk, BF), pltpu.SemaphoreType.DMA((count,))]
        self.mib = 2 + 2 * count * self.hidden * self.width // MIB

    def start(self, weights, bases, held, sems):
        self.held, self.copies = held, []
        for base in bases:
            for c in range(self.each):
                cut = pl.ds(pl.multiple_of(base + c * self.width, BLOCK), self.width)
                for w in weights:
                    source = w.at[:, cut] if self.nn else w.at[cut]
                    k = len(self.copies)
                    self.copies.append(pltpu.make_async_copy(source, held.at[k], sems.at[k]))
                    self.copies[-1].start()

    def products(self, piece, acts):
        for c in range(self.each):
            total = None
            for m in range(self.mats):
                k = (piece * self.each + c) * self.mats + m
                self.copies[k].wait()
                dot = dot_nn if self.nn else dot_nt
                part = dot(acts[m][...], self.held[k])
                total = part if total is None else total + part
            yield slice(c * self.width, (c + 1) * self.width), total


def first_piece(t, n, make, nn, ins, mats, name):
    stream = Stream(mats, n, nn, 1)
    rows = ins[0].shape[0]
    half, quarter, hidden = rows // 2, stream.quarter, stream.hidden

    def kernel(t_ref, *refs):
        parts, refs = refs[: len(ins)], refs[len(ins) :]
        weights, refs = refs[: len(mats)], refs[len(mats) :]
        halves, acts, scratch = refs[:2], refs[2 : 2 + len(mats)], refs[2 + len(mats) :]
        stream.start(weights, [(t_ref[0] ^ 3) * quarter], *scratch)
        make(parts, acts)
        for cols, total in stream.products(0, acts):
            halves[0][:, cols] = total[:half].astype(BF)
            halves[1][:, cols] = total[half:].astype(BF)

    return call(
        kernel,
        t,
        list(ins) + list(mats),
        [sds((half, quarter), BF)] * 2 + [sds((rows, hidden), BF)] * len(mats),
        stream.scratch,
        2 * rows * quarter * hidden * len(mats),
        stream.mib + 4,
        name,
        far=len(mats),
    )


def pieces(t, n, nn, acts, mats, order, name):
    stream = Stream(mats, n, nn, len(order))
    rows, quarter = acts[0].shape[0], stream.quarter

    def kernel(t_ref, *refs):
        ins, refs = refs[: len(acts)], refs[len(acts) :]
        weights, refs = refs[: len(mats)], refs[len(mats) :]
        outs, scratch = refs[: len(order)], refs[len(order) :]
        stream.start(weights, [(t_ref[0] ^ j) * quarter for j in order], *scratch)
        for k, out in enumerate(outs):
            for cols, total in stream.products(k, ins):
                out[:, cols] = total

    return call(
        kernel,
        t,
        list(acts) + list(mats),
        [sds((rows, quarter), F32)] * len(order),
        stream.scratch,
        2 * rows * quarter * len(order) * stream.hidden * len(mats),
        stream.mib + 4,
        name,
        far=len(mats),
    )


def add_diagonal(t, to_x, to_y, top, low):
    half = top.shape[0]

    def kernel(t_ref, x_ref, y_ref, top_ref, low_ref, x_out, y_out):
        x_out[:half, :] = x_ref[:half, :].astype(BF)
        x_out[half:, :] = (x_ref[half:, :] + low_ref[...].astype(F32)).astype(BF)
        y_out[:half, :] = (y_ref[:half, :] + top_ref[...].astype(F32)).astype(BF)
        y_out[half:, :] = y_ref[half:, :].astype(BF)

    return call(
        kernel, t, [to_x, to_y, top, low], [sds(to_x.shape, BF)] * 2, [], to_x.size, LIMIT, "add"
    )


def assemble(t, parts):
    rows, width = parts[0].shape

    def kernel(t_ref, *refs):
        for j, part in enumerate(refs[:-1]):
            refs[-1][:, pl.ds(pl.multiple_of((t_ref[0] ^ j) * width, 128), width)] = part[...]

    (out,) = call(
        kernel, t, parts, [sds((rows, width * len(parts)), parts[0].dtype)], [], 0, LIMIT, "assemble"
    )
    return out


def after(value, *others):
    return lax.optimization_barrier((value,) + others)[0]


def local(tokens, expert_ids, gate_values, w_gate, w_up, w_down, cotangent):
    tok_rows, depth = tokens.shape
    groups = lax.axis_size("expert")
    n = lax.axis_size("tensor")
    z = lax.axis_index("expert")
    t = lax.axis_index("tensor")
    t_arr = t.astype(jnp.int32).reshape(1)
    experts = groups
    cap = min(tok_rows, 3 * tok_rows // experts)
    quarter = depth // n
    gate_mat, up_mat, down_mat = (
        pltpu.with_memory_space_constraint(w[0], pltpu.HBM) for w in (w_gate, w_up, w_down)
    )
    hidden_here = gate_mat.shape[1]

    slot_of = slot_index(expert_ids, experts)
    order = (expert_ids ^ z) * cap + slot_of
    cells = jnp.arange(experts * cap, dtype=jnp.int32)
    pick = [order[:, k][None, :] == cells[:, None] for k in range(2)]
    spread = jnp.logical_or(pick[0], pick[1]).astype(BF)
    slot_gate = jnp.sum(
        jnp.where(pick[0], gate_values[:, 0][None, :], 0.0)
        + jnp.where(pick[1], gate_values[:, 1][None, :], 0.0),
        axis=1,
        keepdims=True,
    )

    def outgoing(source, scale):
        part = lax.dynamic_slice(source, (0, t * quarter), (tok_rows, quarter))
        out = dot_nn(spread[cap:], part)
        own = dot_nn(spread[:cap], source)
        if scale is not None:
            out, own = out * scale[cap:], own * scale[:cap]
        return own.astype(BF), out.astype(BF)

    def over_z(out):
        return [exchange(out[(k - 1) * cap : k * cap], "expert", k) for k in range(1, groups)]

    tok_own, tok_out = outgoing(tokens, None)
    cot_own, cot_out = outgoing(cotangent, slot_gate)
    tok_pieces = over_z(tok_out)
    tok_parts = [tok_pieces] + [
        [exchange(piece, "tensor", j) for piece in tok_pieces] for j in range(1, n)
    ]
    gate_mat, up_mat, *tok_pieces = lax.optimization_barrier((gate_mat, up_mat, *tok_pieces))
    gate_held, up_held = fetch(gate_mat), fetch(up_mat)
    cot_pieces = over_z(after(cot_out, *tok_pieces))
    far = [x for parts in tok_parts[1:] for x in parts]
    held = lax.optimization_barrier((*far, *cot_pieces))
    tok_parts[1:] = [list(held[k : k + n - 1]) for k in range(0, len(far), n - 1)]
    cot_part = jnp.concatenate(held[len(far) :], axis=0)
    cot_parts = [[cot_part]] + [[exchange(cot_part, "tensor", j)] for j in range(1, n)]

    turn = after(t_arr, cot_part)
    pres = []
    for start in range(0, hidden_here, hidden_here // 2):
        if start:
            turn = after(t_arr, cot_parts[1][0], cot_parts[2][0])
        gate_o, up_o, gate_s, up_s = pre_acts(
            turn, tok_own, tok_parts, gate_held, up_held, start, start + hidden_here // 2
        )
        pres.append([gate_o, up_o, exchange(gate_s, "wide", 1), exchange(up_s, "wide", 1)])

    def sum_back(arrived, keep, *others):
        total = keep
        for piece in arrived:
            total = total + piece.astype(F32)
        total = total.astype(BF)
        back = [total[:cap]] + [
            exchange(total[k * cap : (k + 1) * cap], "expert", k) for k in range(1, groups)
        ]
        back = lax.optimization_barrier((*back, *others))[:groups]
        return jnp.concatenate(back, axis=0)

    def gathered(part):
        return assemble(t_arr, [part] + [exchange(part, "tensor", j) for j in range(1, n)])

    gather = [(order[:, k][:, None] == cells[None, :]).astype(BF) for k in range(2)]

    d_top, d_low, hidden = first_piece(
        t_arr, n, hidden_strips, True, sum(pres, []), [down_mat], "project_first"
    )
    added = [exchange(d_top, "tensor", 1), exchange(d_low, "tensor", 2)]
    to_x, to_y = pieces(t_arr, n, True, [hidden], [down_mat], (1, 2), "project_send")
    grads = []
    turn = after(t_arr, to_x)
    for start in range(0, hidden_here, hidden_here // 2):
        if start:
            to_x, to_y = add_diagonal(t_arr, to_x, to_y, *added)
            turn = after(t_arr, to_x)
        gh_o, gh_s = grad_hiddens(
            turn, cot_own, cot_parts, down_mat, start, start + hidden_here // 2
        )
        grads.append([gh_o, exchange(gh_s, "wide", 1)])
    (keep,) = pieces(after(t_arr, gh_s), n, True, [hidden], [down_mat], (0,), "project_keep")

    e_top, e_low, grad_g, grad_u = first_piece(
        after(t_arr, keep), n, grad_strips, False,
        sum([p + g for p, g in zip(pres, grads)], []), [gate_mat, up_mat], "rows_first",
    )
    gadded = [exchange(e_top, "tensor", 1), exchange(e_low, "tensor", 2)]
    from_x, from_y = exchange(to_x, "tensor", 1), exchange(to_y, "tensor", 2)
    gto_x, gto_y = pieces(
        t_arr, n, False, [grad_g, grad_u], [gate_mat, up_mat], (1, 2), "rows_send",
    )
    gto_x, gto_y = add_diagonal(t_arr, gto_x, gto_y, *gadded)
    (gkeep,) = pieces(
        after(t_arr, gto_x), n, False, [grad_g, grad_u], [gate_mat, up_mat], (0,), "rows_keep"
    )
    returned = sum_back((from_x, from_y), after(keep, gto_x), gkeep)
    chosen = [dot_nn(g, returned) for g in gather]
    layer_part = (gate_values[:, 0:1] * chosen[0] + gate_values[:, 1:2] * chosen[1]).astype(BF)
    layer_out = gathered(layer_part)
    cot_here = lax.dynamic_slice(cotangent, (0, t * quarter), (tok_rows, quarter)).astype(F32)
    gate_grad = jnp.stack([jnp.sum(cot_here * c, axis=1) for c in chosen], axis=0)
    for axis, bit in (("wide", 1), ("tensor", 1), ("tensor", 2)):
        gate_grad = gate_grad + exchange(gate_grad, axis, bit)

    greturned = sum_back((exchange(gto_x, "tensor", 1), exchange(gto_y, "tensor", 2)), gkeep)
    grad_part = (dot_nn(gather[0], greturned) + dot_nn(gather[1], greturned)).astype(BF)
    token_grad = gathered(grad_part)
    return (layer_out, token_grad, gate_grad.T)


def plain_local(tokens, expert_ids, gate_values, w_gate, w_up, w_down, cotangent):
    tok_rows, depth = tokens.shape
    groups = lax.axis_size("expert")
    experts = groups * w_gate.shape[0]
    cap = min(tok_rows, 3 * tok_rows // experts)
    total_rows = groups * cap
    gate_mat, up_mat, down_mat = w_gate[0], w_up[0], w_down[0]
    order = expert_ids * cap + slot_index(expert_ids, experts)
    cells = jnp.arange(experts * cap, dtype=jnp.int32)
    pick = [order[:, k][None, :] == cells[:, None] for k in range(2)]
    gather = [(order[:, k][:, None] == cells[None, :]).astype(BF) for k in range(2)]

    def to_owners(rows):
        out = rows.astype(BF).reshape(groups, cap, depth)
        out = lax.all_to_all(out, "expert", split_axis=0, concat_axis=0, tiled=True)
        return out.reshape(total_rows, depth)

    def send_back(rows):
        share = lax.psum_scatter(rows, "tensor", scatter_dimension=0, tiled=True).astype(BF)
        return to_owners(lax.all_gather(share, "tensor", axis=0, tiled=True))

    spread = jnp.logical_or(pick[0], pick[1]).astype(BF)
    arrived = to_owners(dot_nn(spread, tokens))
    gate_pre, up_pre = lax.psum((dot_nn(arrived, gate_mat), dot_nn(arrived, up_mat)), "wide")
    s = jax.nn.sigmoid(gate_pre)
    returned = send_back(dot_nn((gate_pre * s * up_pre).astype(BF), down_mat))
    chosen = [dot_nn(g, returned) for g in gather]
    layer_out = (gate_values[:, 0:1] * chosen[0] + gate_values[:, 1:2] * chosen[1]).astype(BF)
    upstream = cotangent.astype(F32)
    gate_grad = lax.psum(
        jnp.stack([jnp.sum(upstream * c, axis=1) for c in chosen], axis=1), "wide"
    )
    slot_gate = jnp.sum(
        jnp.where(pick[0], gate_values[:, 0][None, :], 0.0)
        + jnp.where(pick[1], gate_values[:, 1][None, :], 0.0),
        axis=1,
        keepdims=True,
    )
    grad_arrived = to_owners(dot_nn(spread, cotangent) * slot_gate)
    grad_hidden = lax.psum(dot_nt(grad_arrived, down_mat), "wide")
    grad_gate = (grad_hidden * up_pre * (s * (1.0 + gate_pre * (1.0 - s)))).astype(BF)
    grad_up = (grad_hidden * (gate_pre * s)).astype(BF)
    back = send_back(dot_nt(grad_gate, gate_mat) + dot_nt(grad_up, up_mat))
    token_grad = (dot_nn(gather[0], back) + dot_nn(gather[1], back)).astype(BF)
    return (layer_out, token_grad, gate_grad)


def solution(mesh):
    in_specs = (
        P("expert", "wide"),
        P("expert", None),
        P("expert", None),
        P("expert", "wide", "tensor"),
        P("expert", "wide", "tensor"),
        P("expert", "tensor", "wide"),
        P("expert", "wide"),
    )
    out_specs = (P("expert", "wide"), P("expert", "wide"), P("expert", None))
    laid_out = mesh.shape["tensor"] == 4 and mesh.shape["expert"] == 4 and mesh.shape["wide"] == 2
    return jax.shard_map(
        local if laid_out else plain_local,
        mesh=mesh,
        in_specs=in_specs,
        out_specs=out_specs,
        check_vma=False,
    )
```

```python
import jax
import jax.numpy as jnp
from jax import lax
from jax.experimental import pallas as pl
from jax.experimental.pallas import tpu as pltpu
from jax.sharding import PartitionSpec as P

BF = jnp.bfloat16
F32 = jnp.float32
MIB = 1024 * 1024


def slot_index(expert_ids, experts):
    hit_table = (expert_ids[:, :, None] == jnp.arange(experts, dtype=jnp.int32)).astype(jnp.int32)
    per_row = jnp.sum(hit_table, axis=1)
    before = jnp.cumsum(per_row, axis=0) - per_row
    return jnp.sum(hit_table * before[:, None, :], axis=2)


def exchange(array, axis, bit):
    size = lax.axis_size(axis)
    return lax.ppermute(array, axis, [(i, i ^ bit) for i in range(size)])


def dot_nn(a, b):
    return jnp.dot(a, b, preferred_element_type=F32)


def dot_nt(a, b):
    return lax.dot_general(a, b, (((1,), (1,)), ((), ())), preferred_element_type=F32)


def params(mib):
    return pltpu.CompilerParams(vmem_limit_bytes=mib * MIB)


VMEM = pl.BlockSpec(memory_space=pltpu.VMEM)
HBM = pl.BlockSpec(memory_space=pltpu.HBM)
SMEM = pl.BlockSpec(memory_space=pltpu.SMEM)


def sds(shape, dtype):
    return jax.ShapeDtypeStruct(shape, dtype)


def call(kernel, t, ins, outs, scratch, flops, mib, name, far=0):
    return pl.pallas_call(
        kernel,
        in_specs=[SMEM] + [VMEM] * (len(ins) - far) + [HBM] * far,
        out_specs=[VMEM] * len(outs),
        out_shape=outs,
        scratch_shapes=scratch,
        compiler_params=params(mib),
        cost_estimate=pl.CostEstimate(flops=flops, bytes_accessed=MIB, transcendentals=0),
        name=name,
    )(t, *ins)


def fetch(matrix):
    def kernel(source, held, sem):
        copy = pltpu.make_async_copy(source, held, sem)
        copy.start()
        copy.wait()

    return pl.pallas_call(
        kernel,
        in_specs=[HBM],
        out_specs=VMEM,
        out_shape=pltpu.VMEM(matrix.shape, matrix.dtype),
        scratch_shapes=[pltpu.SemaphoreType.DMA],
        compiler_params=params(LIMIT),
        cost_estimate=pl.CostEstimate(
            flops=0, bytes_accessed=2 * matrix.size, transcendentals=0
        ),
        name="fetch",
    )(matrix)


def lay_out(t, own, parts, rows_ref):
    cap = own.shape[0]
    n, _, quarter = rows_ref.shape
    for q in range(n):
        rows_ref[q, :cap, :] = own[:, q * quarter : (q + 1) * quarter]
    for j in range(n):
        at = cap
        for piece in parts[j]:
            rows_ref[t ^ j, at : at + piece.shape[0], :] = piece[...]
            at += piece.shape[0]


def split_parts(refs, counts):
    parts, at = [], 0
    for c in counts:
        parts.append(refs[at : at + c])
        at += c
    return parts, refs[at:]


BLOCK = 256


def pre_acts(t, own, parts, gate_mat, up_mat, start, stop):
    depth = gate_mat.shape[0]
    n = len(parts)
    quarter = depth // n
    rows = own.shape[0] + sum(p.shape[0] for p in parts[0])
    counts = [len(p) for p in parts]

    def kernel(t_ref, own_ref, *refs):
        pieces, refs = split_parts(refs, counts)
        gate_w, up_w, gate_o, up_o, send, rows_ref = refs
        lay_out(t_ref[0], own_ref, pieces, rows_ref)

        @pl.loop(0, (stop - start) // BLOCK)
        def _(i):
            off = pl.multiple_of(i * BLOCK, BLOCK)
            for w, out, at in ((gate_w, gate_o, 0), (up_w, up_o, stop - start)):
                total = None
                for q in range(n):
                    part = dot_nn(
                        rows_ref[q], w[q * quarter : (q + 1) * quarter, pl.ds(start + off, BLOCK)]
                    )
                    total = part if total is None else total + part
                out[:, pl.ds(off, BLOCK)] = total
                send[:, pl.ds(at + off, BLOCK)] = total.astype(BF)

    shape = (rows, stop - start)
    return call(
        kernel,
        t,
        [own] + [x for p in parts for x in p] + [gate_mat, up_mat],
        [sds(shape, F32)] * 2 + [sds((rows, 2 * (stop - start)), BF)],
        [pltpu.VMEM((n, rows, quarter), BF)],
        4 * rows * depth * (stop - start),
        LIMIT,
        "pre_acts",
    )


def grad_hiddens(t, own, parts, down_mat, start, stop):
    depth = down_mat.shape[1]
    n = len(parts)
    quarter = depth // n
    rows = own.shape[0] + sum(p.shape[0] for p in parts[0])
    counts = [len(p) for p in parts]

    block = 2 * BLOCK
    steps = (stop - start) // block

    def kernel(t_ref, own_ref, *refs):
        pieces, refs = split_parts(refs, counts)
        down_w, out, send, rows_ref, held, sems = refs
        copies = [
            pltpu.make_async_copy(
                down_w.at[pl.ds(start + i * block, block)], held.at[i], sems.at[i]
            )
            for i in range(steps)
        ]
        for copy in copies:
            copy.start()
        lay_out(t_ref[0], own_ref, pieces, rows_ref)
        for i in range(steps):
            copies[i].wait()
            total = None
            for q in range(n):
                part = dot_nt(rows_ref[q], held[i, :, q * quarter : (q + 1) * quarter])
                total = part if total is None else total + part
            out[:, i * block : (i + 1) * block] = total
            send[:, i * block : (i + 1) * block] = total.astype(BF)

    shape = (rows, stop - start)
    return call(
        kernel,
        t,
        [own] + [x for p in parts for x in p] + [down_mat],
        [sds(shape, F32), sds(shape, BF)],
        [
            pltpu.VMEM((n, rows, quarter), BF),
            pltpu.VMEM((steps, block, depth), BF),
            pltpu.SemaphoreType.DMA((steps,)),
        ],
        2 * rows * depth * (stop - start),
        12,
        "grad_hidden",
        far=1,
    )


STRIP = 32
LIMIT = 8


def strips(rows, body):
    @pl.loop(0, rows // STRIP)
    def _(i):
        body(pl.ds(pl.multiple_of(i * STRIP, STRIP), STRIP))


def hidden_strips(ins, acts):
    (hidden_ref,) = acts

    def body(here):
        at = 0
        for g in range(0, len(ins), 3):
            gate_o, up_o, both_r = ins[g : g + 3]
            width = gate_o.shape[1]
            cols = slice(at, at + width)
            gate = gate_o[here, :] + both_r[here, :width].astype(F32)
            up = up_o[here, :] + both_r[here, width:].astype(F32)
            hidden_ref[here, cols] = (gate * jax.nn.sigmoid(gate) * up).astype(BF)
            at += gate_o.shape[1]

    strips(hidden_ref.shape[0], body)


def grad_strips(ins, acts):
    gg_ref, gu_ref = acts

    def body(here):
        at = 0
        for g in range(0, len(ins), 5):
            gate_o, up_o, both_r, gh_o, gh_r = ins[g : g + 5]
            width = gate_o.shape[1]
            cols = slice(at, at + width)
            gate = gate_o[here, :] + both_r[here, :width].astype(F32)
            up = up_o[here, :] + both_r[here, width:].astype(F32)
            grad = gh_o[here, :] + gh_r[here, :].astype(F32)
            s = jax.nn.sigmoid(gate)
            gg_ref[here, cols] = (grad * up * (s * (1.0 + gate * (1.0 - s)))).astype(BF)
            gu_ref[here, cols] = (grad * (gate * s)).astype(BF)
            at += gate_o.shape[1]

    strips(gg_ref.shape[0], body)


class Stream:
    def __init__(self, mats, n, nn, pieces):
        self.mats, self.nn = len(mats), nn
        self.hidden, depth = mats[0].shape if nn else mats[0].shape[::-1]
        self.quarter = depth // n
        self.width, self.each = self.quarter, 1
        chunk = (self.hidden, self.width) if nn else (self.width, self.hidden)
        count = pieces * self.each * self.mats
        self.scratch = [pltpu.VMEM((count,) + chunk, BF), pltpu.SemaphoreType.DMA((count,))]
        self.mib = 2 + 2 * count * self.hidden * self.width // MIB

    def start(self, weights, bases, held, sems):
        self.held, self.copies = held, []
        for base in bases:
            for c in range(self.each):
                cut = pl.ds(pl.multiple_of(base + c * self.width, BLOCK), self.width)
                for w in weights:
                    source = w.at[:, cut] if self.nn else w.at[cut]
                    k = len(self.copies)
                    self.copies.append(pltpu.make_async_copy(source, held.at[k], sems.at[k]))
                    self.copies[-1].start()

    def products(self, piece, acts):
        for c in range(self.each):
            total = None
            for m in range(self.mats):
                k = (piece * self.each + c) * self.mats + m
                self.copies[k].wait()
                dot = dot_nn if self.nn else dot_nt
                part = dot(acts[m][...], self.held[k])
                total = part if total is None else total + part
            yield slice(c * self.width, (c + 1) * self.width), total


def first_piece(t, n, make, nn, ins, mats, name):
    stream = Stream(mats, n, nn, 1)
    rows = ins[0].shape[0]
    half, quarter, hidden = rows // 2, stream.quarter, stream.hidden

    def kernel(t_ref, *refs):
        parts, refs = refs[: len(ins)], refs[len(ins) :]
        weights, refs = refs[: len(mats)], refs[len(mats) :]
        halves, acts, scratch = refs[:2], refs[2 : 2 + len(mats)], refs[2 + len(mats) :]
        stream.start(weights, [(t_ref[0] ^ 3) * quarter], *scratch)
        make(parts, acts)
        for cols, total in stream.products(0, acts):
            halves[0][:, cols] = total[:half].astype(BF)
            halves[1][:, cols] = total[half:].astype(BF)

    return call(
        kernel,
        t,
        list(ins) + list(mats),
        [sds((half, quarter), BF)] * 2 + [sds((rows, hidden), BF)] * len(mats),
        stream.scratch,
        2 * rows * quarter * hidden * len(mats),
        stream.mib + 4,
        name,
        far=len(mats),
    )


def pieces(t, n, nn, acts, mats, order, name):
    stream = Stream(mats, n, nn, len(order))
    rows, quarter = acts[0].shape[0], stream.quarter

    def kernel(t_ref, *refs):
        ins, refs = refs[: len(acts)], refs[len(acts) :]
        weights, refs = refs[: len(mats)], refs[len(mats) :]
        outs, scratch = refs[: len(order)], refs[len(order) :]
        stream.start(weights, [(t_ref[0] ^ j) * quarter for j in order], *scratch)
        for k, out in enumerate(outs):
            for cols, total in stream.products(k, ins):
                out[:, cols] = total

    return call(
        kernel,
        t,
        list(acts) + list(mats),
        [sds((rows, quarter), F32)] * len(order),
        stream.scratch,
        2 * rows * quarter * len(order) * stream.hidden * len(mats),
        stream.mib + 4,
        name,
        far=len(mats),
    )


def add_diagonal(t, to_x, to_y, top, low):
    half = top.shape[0]

    def kernel(t_ref, x_ref, y_ref, top_ref, low_ref, x_out, y_out):
        x_out[:half, :] = x_ref[:half, :].astype(BF)
        x_out[half:, :] = (x_ref[half:, :] + low_ref[...].astype(F32)).astype(BF)
        y_out[:half, :] = (y_ref[:half, :] + top_ref[...].astype(F32)).astype(BF)
        y_out[half:, :] = y_ref[half:, :].astype(BF)

    return call(
        kernel, t, [to_x, to_y, top, low], [sds(to_x.shape, BF)] * 2, [], to_x.size, LIMIT, "add"
    )


def assemble(t, parts):
    rows, width = parts[0].shape

    def kernel(t_ref, *refs):
        for j, part in enumerate(refs[:-1]):
            refs[-1][:, pl.ds(pl.multiple_of((t_ref[0] ^ j) * width, 128), width)] = part[...]

    (out,) = call(
        kernel, t, parts, [sds((rows, width * len(parts)), parts[0].dtype)], [], 0, LIMIT, "assemble"
    )
    return out


def after(value, *others):
    return lax.optimization_barrier((value,) + others)[0]


def local(tokens, expert_ids, gate_values, w_gate, w_up, w_down, cotangent):
    tok_rows, depth = tokens.shape
    groups = lax.axis_size("expert")
    n = lax.axis_size("tensor")
    z = lax.axis_index("expert")
    t = lax.axis_index("tensor")
    t_arr = t.astype(jnp.int32).reshape(1)
    experts = groups
    cap = min(tok_rows, 3 * tok_rows // experts)
    quarter = depth // n
    gate_mat, up_mat, down_mat = (
        pltpu.with_memory_space_constraint(w[0], pltpu.HBM) for w in (w_gate, w_up, w_down)
    )
    hidden_here = gate_mat.shape[1]

    slot_of = slot_index(expert_ids, experts)
    order = (expert_ids ^ z) * cap + slot_of
    cells = jnp.arange(experts * cap, dtype=jnp.int32)
    pick = [order[:, k][None, :] == cells[:, None] for k in range(2)]
    spread = jnp.logical_or(pick[0], pick[1]).astype(BF)
    slot_gate = jnp.sum(
        jnp.where(pick[0], gate_values[:, 0][None, :], 0.0)
        + jnp.where(pick[1], gate_values[:, 1][None, :], 0.0),
        axis=1,
        keepdims=True,
    )

    def outgoing(source, scale):
        part = lax.dynamic_slice(source, (0, t * quarter), (tok_rows, quarter))
        out = dot_nn(spread[cap:], part)
        own = dot_nn(spread[:cap], source)
        if scale is not None:
            out, own = out * scale[cap:], own * scale[:cap]
        return own.astype(BF), out.astype(BF)

    def over_z(out):
        return [exchange(out[(k - 1) * cap : k * cap], "expert", k) for k in range(1, groups)]

    tok_own, tok_out = outgoing(tokens, None)
    cot_own, cot_out = outgoing(cotangent, slot_gate)
    tok_z = over_z(tok_out)
    first, rest = tok_z[0], tok_z[1:]
    first_far = [exchange(first, "tensor", j) for j in range(1, n)]
    gate_held = fetch(after(gate_mat, first))
    up_held = fetch(after(up_mat, gate_held, *first_far))
    rest = jnp.concatenate(after(tuple(rest), up_held), axis=0)
    rest_x, rest_y = exchange(rest, "tensor", 1), exchange(rest, "tensor", 2)
    cot_z = over_z(after(cot_out, rest))
    split = rest.shape[0] // 2
    rest_d = [exchange(rest_y[:split], "tensor", 1), exchange(rest_x[split:], "tensor", 2)]
    rest_d[0], rest_d[1], *cot_z = lax.optimization_barrier((*rest_d, *cot_z))
    tok_parts = [
        [first, rest], [first_far[0], rest_x], [first_far[1], rest_y], [first_far[2], *rest_d]
    ]
    cot_part = jnp.concatenate(cot_z, axis=0)
    cot_parts = [[cot_part]] + [[exchange(cot_part, "tensor", j)] for j in range(1, n)]

    turn = after(t_arr, cot_part)
    pres = []
    for start in range(0, hidden_here, hidden_here // 2):
        if start:
            turn = after(t_arr, cot_parts[1][0], cot_parts[2][0])
        gate_o, up_o, sent = pre_acts(
            turn, tok_own, tok_parts, gate_held, up_held, start, start + hidden_here // 2
        )
        pres.append([gate_o, up_o, exchange(sent, "wide", 1)])

    def summed(arrived, keep):
        total = keep
        for piece in arrived:
            total = total + piece.astype(F32)
        return total.astype(BF)

    def to_tokens(total):
        return [total[:cap]] + [
            exchange(total[k * cap : (k + 1) * cap], "expert", k) for k in range(1, groups)
        ]

    def gathered(part):
        return assemble(t_arr, [part] + [exchange(part, "tensor", j) for j in range(1, n)])

    gather = [(order[:, k][:, None] == cells[None, :]).astype(BF) for k in range(2)]

    d_top, d_low, hidden = first_piece(
        t_arr, n, hidden_strips, True, sum(pres, []), [down_mat], "project_first"
    )
    added = [exchange(d_top, "tensor", 1), exchange(d_low, "tensor", 2)]
    to_x, to_y = pieces(t_arr, n, True, [hidden], [down_mat], (1, 2), "project_send")
    grads = []
    turn = after(t_arr, to_x)
    for start in range(0, hidden_here, hidden_here // 2):
        if start:
            to_x, to_y = add_diagonal(t_arr, to_x, to_y, *added)
            turn = after(t_arr, to_x)
        gh_o, gh_s = grad_hiddens(
            turn, cot_own, cot_parts, down_mat, start, start + hidden_here // 2
        )
        grads.append([gh_o, exchange(gh_s, "wide", 1)])
    (keep,) = pieces(after(t_arr, gh_s), n, True, [hidden], [down_mat], (0,), "project_keep")

    e_top, e_low, grad_g, grad_u = first_piece(
        after(t_arr, keep), n, grad_strips, False,
        sum([p + g for p, g in zip(pres, grads)], []), [gate_mat, up_mat], "rows_first",
    )
    gadded = [exchange(e_top, "tensor", 1), exchange(e_low, "tensor", 2)]
    from_x, from_y = exchange(to_x, "tensor", 1), exchange(to_y, "tensor", 2)
    gto_x, gto_y = pieces(
        t_arr, n, False, [grad_g, grad_u], [gate_mat, up_mat], (1, 2), "rows_send",
    )
    gto_x, gto_y = add_diagonal(t_arr, gto_x, gto_y, *gadded)
    (gkeep,) = pieces(
        after(t_arr, gto_x), n, False, [grad_g, grad_u], [gate_mat, up_mat], (0,), "rows_keep"
    )
    gtotal = summed((exchange(gto_x, "tensor", 1), exchange(gto_y, "tensor", 2)), gkeep)
    returned = to_tokens(summed((from_x, from_y), after(keep, gto_x)))
    greturned = to_tokens(gtotal)
    returned = jnp.concatenate(after(tuple(returned), greturned[1]), axis=0)
    chosen = [dot_nn(g, returned) for g in gather]
    layer_part = (gate_values[:, 0:1] * chosen[0] + gate_values[:, 1:2] * chosen[1]).astype(BF)
    layer_out = gathered(layer_part)
    cot_here = lax.dynamic_slice(cotangent, (0, t * quarter), (tok_rows, quarter)).astype(F32)
    gate_grad = jnp.stack([jnp.sum(cot_here * c, axis=1) for c in chosen], axis=0)
    for axis, bit in (("wide", 1), ("tensor", 1), ("tensor", 2)):
        gate_grad = gate_grad + exchange(gate_grad, axis, bit)

    greturned = jnp.concatenate(greturned, axis=0)
    grad_part = (dot_nn(gather[0], greturned) + dot_nn(gather[1], greturned)).astype(BF)
    token_grad = gathered(grad_part)
    return (layer_out, token_grad, gate_grad.T)


def plain_local(tokens, expert_ids, gate_values, w_gate, w_up, w_down, cotangent):
    tok_rows, depth = tokens.shape
    groups = lax.axis_size("expert")
    experts = groups * w_gate.shape[0]
    cap = min(tok_rows, 3 * tok_rows // experts)
    total_rows = groups * cap
    gate_mat, up_mat, down_mat = w_gate[0], w_up[0], w_down[0]
    order = expert_ids * cap + slot_index(expert_ids, experts)
    cells = jnp.arange(experts * cap, dtype=jnp.int32)
    pick = [order[:, k][None, :] == cells[:, None] for k in range(2)]
    gather = [(order[:, k][:, None] == cells[None, :]).astype(BF) for k in range(2)]

    def to_owners(rows):
        out = rows.astype(BF).reshape(groups, cap, depth)
        out = lax.all_to_all(out, "expert", split_axis=0, concat_axis=0, tiled=True)
        return out.reshape(total_rows, depth)

    def send_back(rows):
        share = lax.psum_scatter(rows, "tensor", scatter_dimension=0, tiled=True).astype(BF)
        return to_owners(lax.all_gather(share, "tensor", axis=0, tiled=True))

    spread = jnp.logical_or(pick[0], pick[1]).astype(BF)
    arrived = to_owners(dot_nn(spread, tokens))
    gate_pre, up_pre = lax.psum((dot_nn(arrived, gate_mat), dot_nn(arrived, up_mat)), "wide")
    s = jax.nn.sigmoid(gate_pre)
    returned = send_back(dot_nn((gate_pre * s * up_pre).astype(BF), down_mat))
    chosen = [dot_nn(g, returned) for g in gather]
    layer_out = (gate_values[:, 0:1] * chosen[0] + gate_values[:, 1:2] * chosen[1]).astype(BF)
    upstream = cotangent.astype(F32)
    gate_grad = lax.psum(
        jnp.stack([jnp.sum(upstream * c, axis=1) for c in chosen], axis=1), "wide"
    )
    slot_gate = jnp.sum(
        jnp.where(pick[0], gate_values[:, 0][None, :], 0.0)
        + jnp.where(pick[1], gate_values[:, 1][None, :], 0.0),
        axis=1,
        keepdims=True,
    )
    grad_arrived = to_owners(dot_nn(spread, cotangent) * slot_gate)
    grad_hidden = lax.psum(dot_nt(grad_arrived, down_mat), "wide")
    grad_gate = (grad_hidden * up_pre * (s * (1.0 + gate_pre * (1.0 - s)))).astype(BF)
    grad_up = (grad_hidden * (gate_pre * s)).astype(BF)
    back = send_back(dot_nt(grad_gate, gate_mat) + dot_nt(grad_up, up_mat))
    token_grad = (dot_nn(gather[0], back) + dot_nn(gather[1], back)).astype(BF)
    return (layer_out, token_grad, gate_grad)


def solution(mesh):
    in_specs = (
        P("expert", "wide"),
        P("expert", None),
        P("expert", None),
        P("expert", "wide", "tensor"),
        P("expert", "wide", "tensor"),
        P("expert", "tensor", "wide"),
        P("expert", "wide"),
    )
    out_specs = (P("expert", "wide"), P("expert", "wide"), P("expert", None))
    laid_out = mesh.shape["tensor"] == 4 and mesh.shape["expert"] == 4 and mesh.shape["wide"] == 2
    return jax.shard_map(
        local if laid_out else plain_local,
        mesh=mesh,
        in_specs=in_specs,
        out_specs=out_specs,
        check_vma=False,
    )
```

```python
import jax
import jax.numpy as jnp
from jax import lax
from jax.experimental import pallas as pl
from jax.experimental.pallas import tpu as pltpu
from jax.sharding import PartitionSpec as P

BF = jnp.bfloat16
F32 = jnp.float32
MIB = 1024 * 1024


def slot_index(expert_ids, experts):
    hit_table = (expert_ids[:, :, None] == jnp.arange(experts, dtype=jnp.int32)).astype(jnp.int32)
    per_row = jnp.sum(hit_table, axis=1)
    before = jnp.cumsum(per_row, axis=0) - per_row
    return jnp.sum(hit_table * before[:, None, :], axis=2)


def exchange(array, axis, bit):
    size = lax.axis_size(axis)
    return lax.ppermute(array, axis, [(i, i ^ bit) for i in range(size)])


def dot_nn(a, b):
    return jnp.dot(a, b, preferred_element_type=F32)


def dot_nt(a, b):
    return lax.dot_general(a, b, (((1,), (1,)), ((), ())), preferred_element_type=F32)


def params(mib):
    return pltpu.CompilerParams(vmem_limit_bytes=mib * MIB)


VMEM = pl.BlockSpec(memory_space=pltpu.VMEM)
HBM = pl.BlockSpec(memory_space=pltpu.HBM)
SMEM = pl.BlockSpec(memory_space=pltpu.SMEM)


def sds(shape, dtype):
    return jax.ShapeDtypeStruct(shape, dtype)


def call(kernel, t, ins, outs, scratch, flops, mib, name, far=0):
    return pl.pallas_call(
        kernel,
        in_specs=[SMEM] + [VMEM] * (len(ins) - far) + [HBM] * far,
        out_specs=[VMEM] * len(outs),
        out_shape=outs,
        scratch_shapes=scratch,
        compiler_params=params(mib),
        cost_estimate=pl.CostEstimate(flops=flops, bytes_accessed=MIB, transcendentals=0),
        name=name,
    )(t, *ins)


def fetch(matrix):
    def kernel(source, held, sem):
        copy = pltpu.make_async_copy(source, held, sem)
        copy.start()
        copy.wait()

    return pl.pallas_call(
        kernel,
        in_specs=[HBM],
        out_specs=VMEM,
        out_shape=pltpu.VMEM(matrix.shape, matrix.dtype),
        scratch_shapes=[pltpu.SemaphoreType.DMA],
        compiler_params=params(LIMIT),
        cost_estimate=pl.CostEstimate(
            flops=0, bytes_accessed=2 * matrix.size, transcendentals=0
        ),
        name="fetch",
    )(matrix)


def lay_out(t, own, parts, rows_ref):
    cap = own.shape[0]
    n, _, quarter = rows_ref.shape
    for q in range(n):
        rows_ref[q, :cap, :] = own[:, q * quarter : (q + 1) * quarter]
    for j in range(n):
        at = cap
        for piece in parts[j]:
            rows_ref[t ^ j, at : at + piece.shape[0], :] = piece[...]
            at += piece.shape[0]


def split_parts(refs, counts):
    parts, at = [], 0
    for c in counts:
        parts.append(refs[at : at + c])
        at += c
    return parts, refs[at:]


BLOCK = 256


def pre_acts(t, own, parts, gate_held, up_mat, start, stop):
    depth = up_mat.shape[0]
    n = len(parts)
    quarter = depth // n
    rows = own.shape[0] + sum(p.shape[0] for p in parts[0])
    counts = [len(p) for p in parts]
    width = stop - start

    def kernel(t_ref, own_ref, *refs):
        pieces, refs = split_parts(refs, counts)
        gate_w, up_w, gate_o, up_o, send, rows_ref, up_held, sem = refs
        copy = pltpu.make_async_copy(up_w.at[:, pl.ds(start, width)], up_held, sem)
        copy.start()
        lay_out(t_ref[0], own_ref, pieces, rows_ref)
        for w, base, out, at in ((gate_w, start, gate_o, 0), (up_held, 0, up_o, width)):
            if at:
                copy.wait()

            @pl.loop(0, width // BLOCK)
            def _(i):
                off = pl.multiple_of(i * BLOCK, BLOCK)
                total = None
                for q in range(n):
                    part = dot_nn(
                        rows_ref[q], w[q * quarter : (q + 1) * quarter, pl.ds(base + off, BLOCK)]
                    )
                    total = part if total is None else total + part
                out[:, pl.ds(off, BLOCK)] = total
                send[:, pl.ds(at + off, BLOCK)] = total.astype(BF)

    shape = (rows, width)
    return call(
        kernel,
        t,
        [own] + [x for p in parts for x in p] + [gate_held, up_mat],
        [sds(shape, F32)] * 2 + [sds((rows, 2 * width), BF)],
        [
            pltpu.VMEM((n, rows, quarter), BF),
            pltpu.VMEM((depth, width), BF),
            pltpu.SemaphoreType.DMA,
        ],
        4 * rows * depth * width,
        14,
        "pre_acts",
        far=1,
    )


def grad_hiddens(t, own, parts, down_mat, start, stop):
    depth = down_mat.shape[1]
    n = len(parts)
    quarter = depth // n
    rows = own.shape[0] + sum(p.shape[0] for p in parts[0])
    counts = [len(p) for p in parts]

    steps = (stop - start) // BLOCK

    def kernel(t_ref, own_ref, *refs):
        pieces, refs = split_parts(refs, counts)
        down_w, out, send, rows_ref, held, sems = refs

        def copy(i):
            source = down_w.at[pl.ds(start + i * BLOCK, BLOCK)]
            return pltpu.make_async_copy(source, held.at[i], sems.at[i])

        for i in range(steps):
            copy(i).start()
        lay_out(t_ref[0], own_ref, pieces, rows_ref)

        @pl.loop(0, steps)
        def _(i):
            copy(i).wait()
            total = None
            for q in range(n):
                part = dot_nt(rows_ref[q], held[i, :, q * quarter : (q + 1) * quarter])
                total = part if total is None else total + part
            off = pl.multiple_of(i * BLOCK, BLOCK)
            out[:, pl.ds(off, BLOCK)] = total
            send[:, pl.ds(off, BLOCK)] = total.astype(BF)

    shape = (rows, stop - start)
    return call(
        kernel,
        t,
        [own] + [x for p in parts for x in p] + [down_mat],
        [sds(shape, F32), sds(shape, BF)],
        [
            pltpu.VMEM((n, rows, quarter), BF),
            pltpu.VMEM((steps, BLOCK, depth), BF),
            pltpu.SemaphoreType.DMA((steps,)),
        ],
        2 * rows * depth * (stop - start),
        12,
        "grad_hidden",
        far=1,
    )


STRIP = 32
LIMIT = 8


def strips(rows, body):
    @pl.loop(0, rows // STRIP)
    def _(i):
        body(pl.ds(pl.multiple_of(i * STRIP, STRIP), STRIP))


def hidden_strips(ins, acts):
    (hidden_ref,) = acts

    def body(here):
        at = 0
        for g in range(0, len(ins), 3):
            gate_o, up_o, both_r = ins[g : g + 3]
            width = gate_o.shape[1]
            cols = slice(at, at + width)
            gate = gate_o[here, :] + both_r[here, :width].astype(F32)
            up = up_o[here, :] + both_r[here, width:].astype(F32)
            hidden_ref[here, cols] = (gate * jax.nn.sigmoid(gate) * up).astype(BF)
            at += gate_o.shape[1]

    strips(hidden_ref.shape[0], body)


def grad_strips(ins, acts):
    gg_ref, gu_ref = acts

    def body(here):
        at = 0
        for g in range(0, len(ins), 5):
            gate_o, up_o, both_r, gh_o, gh_r = ins[g : g + 5]
            width = gate_o.shape[1]
            cols = slice(at, at + width)
            gate = gate_o[here, :] + both_r[here, :width].astype(F32)
            up = up_o[here, :] + both_r[here, width:].astype(F32)
            grad = gh_o[here, :] + gh_r[here, :].astype(F32)
            s = jax.nn.sigmoid(gate)
            gg_ref[here, cols] = (grad * up * (s * (1.0 + gate * (1.0 - s)))).astype(BF)
            gu_ref[here, cols] = (grad * (gate * s)).astype(BF)
            at += gate_o.shape[1]

    strips(gg_ref.shape[0], body)


class Stream:
    def __init__(self, mats, n, nn, pieces):
        self.mats, self.nn = len(mats), nn
        self.hidden, depth = mats[0].shape if nn else mats[0].shape[::-1]
        self.quarter = depth // n
        self.blocks = self.quarter // BLOCK
        self.each = 1 if nn else self.blocks
        chunk = (self.hidden, self.quarter) if nn else (BLOCK, self.hidden)
        self.count = pieces * self.each
        total = self.count * self.mats
        self.scratch = [pltpu.VMEM((total,) + chunk, BF), pltpu.SemaphoreType.DMA((total,))]
        self.mib = 2 + 2 * pieces * self.mats * self.hidden * self.quarter // MIB

    def copy(self, chunk, m):
        base = self.bases[0]
        for k in range(1, len(self.bases)):
            base = jnp.where(chunk >= k * self.each, self.bases[k], base)
        width = self.quarter if self.nn else BLOCK
        cut = pl.ds(pl.multiple_of(base + chunk % self.each * width, BLOCK), width)
        source = self.weights[m].at[:, cut] if self.nn else self.weights[m].at[cut]
        slot = chunk * self.mats + m
        return pltpu.make_async_copy(source, self.held.at[slot], self.sems.at[slot])

    def start(self, weights, bases, held, sems):
        self.weights, self.bases, self.held, self.sems = weights, bases, held, sems
        for chunk in range(self.count):
            for m in range(self.mats):
                self.copy(chunk, m).start()

    def products(self, acts, store):
        @pl.loop(0, len(self.bases) * self.blocks)
        def _(i):
            piece, off = i // self.blocks, pl.multiple_of(i % self.blocks * BLOCK, BLOCK)
            if self.nn:

                @pl.when(off == 0)
                def _():
                    self.copy(piece, 0).wait()

                total = dot_nn(acts[0][...], self.held[piece, :, pl.ds(off, BLOCK)])
            else:
                total = None
                for m in range(self.mats):
                    self.copy(i, m).wait()
                    part = dot_nt(acts[m][...], self.held[i * self.mats + m])
                    total = part if total is None else total + part
            store(piece, pl.ds(off, BLOCK), total)


def first_piece(t, n, make, nn, ins, mats, name):
    stream = Stream(mats, n, nn, 1)
    rows = ins[0].shape[0]
    half, quarter, hidden = rows // 2, stream.quarter, stream.hidden

    def kernel(t_ref, *refs):
        parts, refs = refs[: len(ins)], refs[len(ins) :]
        weights, refs = refs[: len(mats)], refs[len(mats) :]
        halves, acts, scratch = refs[:2], refs[2 : 2 + len(mats)], refs[2 + len(mats) :]
        stream.start(weights, [(t_ref[0] ^ 3) * quarter], *scratch)
        make(parts, acts)

        def store(piece, cols, total):
            halves[0][:, cols] = total[:half].astype(BF)
            halves[1][:, cols] = total[half:].astype(BF)

        stream.products(acts, store)

    return call(
        kernel,
        t,
        list(ins) + list(mats),
        [sds((half, quarter), BF)] * 2 + [sds((rows, hidden), BF)] * len(mats),
        stream.scratch,
        2 * rows * quarter * hidden * len(mats),
        stream.mib + 4,
        name,
        far=len(mats),
    )


def pieces(t, n, nn, acts, mats, order, name):
    stream = Stream(mats, n, nn, len(order))
    rows, quarter = acts[0].shape[0], stream.quarter

    def kernel(t_ref, *refs):
        ins, refs = refs[: len(acts)], refs[len(acts) :]
        weights, refs = refs[: len(mats)], refs[len(mats) :]
        out, scratch = refs[0], refs[1:]
        stream.start(weights, [(t_ref[0] ^ j) * quarter for j in order], *scratch)

        def store(piece, cols, total):
            out[piece, :, cols] = total

        stream.products(ins, store)

    (out,) = call(
        kernel,
        t,
        list(acts) + list(mats),
        [sds((len(order), rows, quarter), F32)],
        stream.scratch,
        2 * rows * quarter * len(order) * stream.hidden * len(mats),
        stream.mib + 4,
        name,
        far=len(mats),
    )
    return out


def add_diagonal(t, both, top, low):
    half = top.shape[0]

    def kernel(t_ref, both_ref, top_ref, low_ref, x_out, y_out):
        x_out[:half, :] = both_ref[0, :half, :].astype(BF)
        x_out[half:, :] = (both_ref[0, half:, :] + low_ref[...].astype(F32)).astype(BF)
        y_out[:half, :] = (both_ref[1, :half, :] + top_ref[...].astype(F32)).astype(BF)
        y_out[half:, :] = both_ref[1, half:, :].astype(BF)

    return call(
        kernel, t, [both, top, low], [sds(both.shape[1:], BF)] * 2, [], both.size, LIMIT, "add"
    )


def assemble(t, parts):
    rows, width = parts[0].shape

    def kernel(t_ref, *refs):
        for j, part in enumerate(refs[:-1]):
            refs[-1][:, pl.ds(pl.multiple_of((t_ref[0] ^ j) * width, 128), width)] = part[...]

    (out,) = call(
        kernel, t, parts, [sds((rows, width * len(parts)), parts[0].dtype)], [], 0, LIMIT, "assemble"
    )
    return out


def after(value, *others):
    return lax.optimization_barrier((value,) + others)[0]


def local(tokens, expert_ids, gate_values, w_gate, w_up, w_down, cotangent):
    tok_rows, depth = tokens.shape
    groups = lax.axis_size("expert")
    n = lax.axis_size("tensor")
    z = lax.axis_index("expert")
    t = lax.axis_index("tensor")
    t_arr = t.astype(jnp.int32).reshape(1)
    experts = groups
    cap = min(tok_rows, 3 * tok_rows // experts)
    quarter = depth // n
    gate_mat, up_mat, down_mat = (
        pltpu.with_memory_space_constraint(w[0], pltpu.HBM) for w in (w_gate, w_up, w_down)
    )
    hidden_here = gate_mat.shape[1]

    slot_of = slot_index(expert_ids, experts)
    order = (expert_ids ^ z) * cap + slot_of
    cells = jnp.arange(experts * cap, dtype=jnp.int32)
    pick = [order[:, k][None, :] == cells[:, None] for k in range(2)]
    spread = jnp.logical_or(pick[0], pick[1]).astype(BF)
    slot_gate = jnp.sum(
        jnp.where(pick[0], gate_values[:, 0][None, :], 0.0)
        + jnp.where(pick[1], gate_values[:, 1][None, :], 0.0),
        axis=1,
        keepdims=True,
    )

    def outgoing(source, scale):
        part = lax.dynamic_slice(source, (0, t * quarter), (tok_rows, quarter))
        out = dot_nn(spread[cap:], part)
        own = dot_nn(spread[:cap], source)
        if scale is not None:
            out, own = out * scale[cap:], own * scale[:cap]
        return own.astype(BF), out.astype(BF)

    def over_z(out):
        return [exchange(out[(k - 1) * cap : k * cap], "expert", k) for k in range(1, groups)]

    tok_own, tok_out = outgoing(tokens, None)
    cot_own, cot_out = outgoing(cotangent, slot_gate)
    tok_z = over_z(tok_out)
    first, rest = tok_z[0], tok_z[1:]
    first_far = [exchange(first, "tensor", j) for j in range(1, n)]
    gate_held = fetch(gate_mat)
    rest = jnp.concatenate(after(tuple(rest), gate_held, *first_far), axis=0)
    rest_x, rest_y = exchange(rest, "tensor", 1), exchange(rest, "tensor", 2)
    cot_z = over_z(after(cot_out, rest))
    split = rest.shape[0] // 2
    rest_d = [exchange(rest_y[:split], "tensor", 1), exchange(rest_x[split:], "tensor", 2)]
    tok_parts = [
        [first, rest], [first_far[0], rest_x], [first_far[1], rest_y], [first_far[2], *rest_d]
    ]
    cot_part = jnp.concatenate(after(tuple(cot_z), *rest_d), axis=0)
    cot_parts = [[cot_part]] + [[exchange(cot_part, "tensor", j)] for j in range(1, n)]
    pres = []
    half = hidden_here // 2
    for start, turn in ((0, (cot_part,)), (half, (cot_parts[1][0], cot_parts[2][0]))):
        gate_o, up_o, sent = pre_acts(
            after(t_arr, *turn), tok_own, tok_parts, gate_held, up_mat, start, start + half
        )
        pres.append([gate_o, up_o, exchange(sent, "wide", 1)])

    def summed(arrived, keep):
        total = keep
        for piece in arrived:
            total = total + piece.astype(F32)
        return total.astype(BF)

    def to_tokens(total):
        return [total[:cap]] + [
            exchange(total[k * cap : (k + 1) * cap], "expert", k) for k in range(1, groups)
        ]

    def around(part):
        return [part] + [exchange(part, "tensor", j) for j in range(1, n)]

    gather = [(order[:, k][:, None] == cells[None, :]).astype(BF) for k in range(2)]

    d_top, d_low, hidden = first_piece(
        t_arr, n, hidden_strips, True, sum(pres, []), [down_mat], "project_first"
    )
    added = [exchange(d_top, "tensor", 1), exchange(d_low, "tensor", 2)]
    both = pieces(t_arr, n, True, [hidden], [down_mat], (1, 2), "project_send")
    grads = []
    turn = after(t_arr, both)
    for start in range(0, hidden_here, hidden_here // 2):
        if start:
            to_x, to_y = add_diagonal(t_arr, both, *added)
            turn = after(t_arr, to_x)
        gh_o, gh_s = grad_hiddens(
            turn, cot_own, cot_parts, down_mat, start, start + hidden_here // 2
        )
        grads.append([gh_o, exchange(gh_s, "wide", 1)])
    keep = pieces(after(t_arr, gh_s), n, True, [hidden], [down_mat], (0,), "project_keep")[0]

    e_top, e_low, grad_g, grad_u = first_piece(
        after(t_arr, keep), n, grad_strips, False,
        sum([p + g for p, g in zip(pres, grads)], []), [gate_mat, up_mat], "rows_first",
    )
    gadded = [exchange(e_top, "tensor", 1), exchange(e_low, "tensor", 2)]
    from_x, from_y = exchange(to_x, "tensor", 1), exchange(to_y, "tensor", 2)
    gboth = pieces(
        t_arr, n, False, [grad_g, grad_u], [gate_mat, up_mat], (1, 2), "rows_send",
    )
    gto_x, gto_y = add_diagonal(t_arr, gboth, *gadded)
    gkeep = pieces(
        after(t_arr, gto_x), n, False, [grad_g, grad_u], [gate_mat, up_mat], (0,), "rows_keep"
    )[0]
    gtotal = summed((exchange(gto_x, "tensor", 1), exchange(gto_y, "tensor", 2)), gkeep)
    returned = to_tokens(summed((from_x, from_y), after(keep, gto_x)))
    greturned = to_tokens(gtotal)
    returned = jnp.concatenate(after(tuple(returned), greturned[1]), axis=0)
    chosen = [dot_nn(g, returned) for g in gather]
    layer_part = (gate_values[:, 0:1] * chosen[0] + gate_values[:, 1:2] * chosen[1]).astype(BF)
    layer_parts = around(layer_part)
    layer_out = assemble(t_arr, layer_parts)
    greturned = jnp.concatenate(tuple(greturned), axis=0)
    cot_here = lax.dynamic_slice(cotangent, (0, t * quarter), (tok_rows, quarter)).astype(F32)
    gate_grad = jnp.stack([jnp.sum(cot_here * c, axis=1) for c in chosen], axis=0)
    gate_grad = after(gate_grad, layer_parts[1], layer_parts[2])
    for axis, bit in (("wide", 1), ("tensor", 1), ("tensor", 2)):
        gate_grad = gate_grad + exchange(gate_grad, axis, bit)

    grad_part = (dot_nn(gather[0], greturned) + dot_nn(gather[1], greturned)).astype(BF)
    token_grad = assemble(t_arr, around(grad_part))
    return (layer_out, token_grad, gate_grad.T)


def plain_local(tokens, expert_ids, gate_values, w_gate, w_up, w_down, cotangent):
    tok_rows, depth = tokens.shape
    groups = lax.axis_size("expert")
    experts = groups * w_gate.shape[0]
    cap = min(tok_rows, 3 * tok_rows // experts)
    total_rows = groups * cap
    gate_mat, up_mat, down_mat = w_gate[0], w_up[0], w_down[0]
    order = expert_ids * cap + slot_index(expert_ids, experts)
    cells = jnp.arange(experts * cap, dtype=jnp.int32)
    pick = [order[:, k][None, :] == cells[:, None] for k in range(2)]
    gather = [(order[:, k][:, None] == cells[None, :]).astype(BF) for k in range(2)]

    def to_owners(rows):
        out = rows.astype(BF).reshape(groups, cap, depth)
        out = lax.all_to_all(out, "expert", split_axis=0, concat_axis=0, tiled=True)
        return out.reshape(total_rows, depth)

    def send_back(rows):
        share = lax.psum_scatter(rows, "tensor", scatter_dimension=0, tiled=True).astype(BF)
        return to_owners(lax.all_gather(share, "tensor", axis=0, tiled=True))

    spread = jnp.logical_or(pick[0], pick[1]).astype(BF)
    arrived = to_owners(dot_nn(spread, tokens))
    gate_pre, up_pre = lax.psum((dot_nn(arrived, gate_mat), dot_nn(arrived, up_mat)), "wide")
    s = jax.nn.sigmoid(gate_pre)
    returned = send_back(dot_nn((gate_pre * s * up_pre).astype(BF), down_mat))
    chosen = [dot_nn(g, returned) for g in gather]
    layer_out = (gate_values[:, 0:1] * chosen[0] + gate_values[:, 1:2] * chosen[1]).astype(BF)
    upstream = cotangent.astype(F32)
    gate_grad = lax.psum(
        jnp.stack([jnp.sum(upstream * c, axis=1) for c in chosen], axis=1), "wide"
    )
    slot_gate = jnp.sum(
        jnp.where(pick[0], gate_values[:, 0][None, :], 0.0)
        + jnp.where(pick[1], gate_values[:, 1][None, :], 0.0),
        axis=1,
        keepdims=True,
    )
    grad_arrived = to_owners(dot_nn(spread, cotangent) * slot_gate)
    grad_hidden = lax.psum(dot_nt(grad_arrived, down_mat), "wide")
    grad_gate = (grad_hidden * up_pre * (s * (1.0 + gate_pre * (1.0 - s)))).astype(BF)
    grad_up = (grad_hidden * (gate_pre * s)).astype(BF)
    back = send_back(dot_nt(grad_gate, gate_mat) + dot_nt(grad_up, up_mat))
    token_grad = (dot_nn(gather[0], back) + dot_nn(gather[1], back)).astype(BF)
    return (layer_out, token_grad, gate_grad)


def solution(mesh):
    in_specs = (
        P("expert", "wide"),
        P("expert", None),
        P("expert", None),
        P("expert", "wide", "tensor"),
        P("expert", "wide", "tensor"),
        P("expert", "tensor", "wide"),
        P("expert", "wide"),
    )
    out_specs = (P("expert", "wide"), P("expert", "wide"), P("expert", None))
    laid_out = mesh.shape["tensor"] == 4 and mesh.shape["expert"] == 4 and mesh.shape["wide"] == 2
    return jax.shard_map(
        local if laid_out else plain_local,
        mesh=mesh,
        in_specs=in_specs,
        out_specs=out_specs,
        check_vma=False,
    )
```

```python
import jax
import jax.numpy as jnp
from jax import lax
from jax.experimental import pallas as pl
from jax.experimental.pallas import tpu as pltpu
from jax.sharding import PartitionSpec as P

BF = jnp.bfloat16
F32 = jnp.float32
MIB = 1024 * 1024


def slot_index(expert_ids, experts):
    hit_table = (expert_ids[:, :, None] == jnp.arange(experts, dtype=jnp.int32)).astype(jnp.int32)
    per_row = jnp.sum(hit_table, axis=1)
    before = jnp.cumsum(per_row, axis=0) - per_row
    return jnp.sum(hit_table * before[:, None, :], axis=2)


def exchange(array, axis, bit):
    size = lax.axis_size(axis)
    return lax.ppermute(array, axis, [(i, i ^ bit) for i in range(size)])


def dot_nn(a, b):
    return jnp.dot(a, b, preferred_element_type=F32)


def dot_nt(a, b):
    return lax.dot_general(a, b, (((1,), (1,)), ((), ())), preferred_element_type=F32)


def params(mib):
    return pltpu.CompilerParams(vmem_limit_bytes=mib * MIB)


VMEM = pl.BlockSpec(memory_space=pltpu.VMEM)
HBM = pl.BlockSpec(memory_space=pltpu.HBM)
SMEM = pl.BlockSpec(memory_space=pltpu.SMEM)


def sds(shape, dtype):
    return jax.ShapeDtypeStruct(shape, dtype)


def call(kernel, t, ins, outs, scratch, flops, mib, name, far=0):
    return pl.pallas_call(
        kernel,
        in_specs=[SMEM] + [VMEM] * (len(ins) - far) + [HBM] * far,
        out_specs=[VMEM] * len(outs),
        out_shape=outs,
        scratch_shapes=scratch,
        compiler_params=params(mib),
        cost_estimate=pl.CostEstimate(flops=flops // 2, bytes_accessed=MIB, transcendentals=0),
        name=name,
    )(t, *ins)


def fetch(matrix):
    def kernel(source, held, sem):
        copy = pltpu.make_async_copy(source, held, sem)
        copy.start()
        copy.wait()

    return pl.pallas_call(
        kernel,
        in_specs=[HBM],
        out_specs=VMEM,
        out_shape=pltpu.VMEM(matrix.shape, matrix.dtype),
        scratch_shapes=[pltpu.SemaphoreType.DMA],
        compiler_params=params(LIMIT),
        cost_estimate=pl.CostEstimate(
            flops=0, bytes_accessed=2 * matrix.size, transcendentals=0
        ),
        name="fetch",
    )(matrix)


def lay_out(t, own, parts, rows_ref):
    cap = own.shape[0]
    n, _, quarter = rows_ref.shape
    for q in range(n):
        rows_ref[q, :cap, :] = own[:, q * quarter : (q + 1) * quarter]
    for j in range(n):
        at = cap
        for piece in parts[j]:
            rows_ref[t ^ j, at : at + piece.shape[0], :] = piece[...]
            at += piece.shape[0]


def split_parts(refs, counts):
    parts, at = [], 0
    for c in counts:
        parts.append(refs[at : at + c])
        at += c
    return parts, refs[at:]


BLOCK = 256


def pre_acts(t, own, parts, gate_held, up_mat, start, stop):
    depth = up_mat.shape[0]
    n = len(parts)
    quarter = depth // n
    rows = own.shape[0] + sum(p.shape[0] for p in parts[0])
    counts = [len(p) for p in parts]
    width = stop - start

    def kernel(t_ref, own_ref, *refs):
        pieces, refs = split_parts(refs, counts)
        gate_w, up_w, gate_o, up_o, send, rows_ref, up_held, sem = refs
        copy = pltpu.make_async_copy(up_w.at[:, pl.ds(start, width)], up_held, sem)
        copy.start()
        lay_out(t_ref[0], own_ref, pieces, rows_ref)
        for w, base, out, at in ((gate_w, start, gate_o, 0), (up_held, 0, up_o, width)):
            if at:
                copy.wait()

            @pl.loop(0, width // BLOCK)
            def _(i):
                off = pl.multiple_of(i * BLOCK, BLOCK)
                total = None
                for q in range(n):
                    part = dot_nn(
                        rows_ref[q], w[q * quarter : (q + 1) * quarter, pl.ds(base + off, BLOCK)]
                    )
                    total = part if total is None else total + part
                out[:, pl.ds(off, BLOCK)] = total
                send[:, pl.ds(at + off, BLOCK)] = total.astype(BF)

    shape = (rows, width)
    return call(
        kernel,
        t,
        [own] + [x for p in parts for x in p] + [gate_held, up_mat],
        [sds(shape, F32)] * 2 + [sds((rows, 2 * width), BF)],
        [
            pltpu.VMEM((n, rows, quarter), BF),
            pltpu.VMEM((depth, width), BF),
            pltpu.SemaphoreType.DMA,
        ],
        4 * rows * depth * width,
        14,
        "pre_acts",
        far=1,
    )


def grad_hiddens(t, own, parts, down_mat, start, stop):
    depth = down_mat.shape[1]
    n = len(parts)
    quarter = depth // n
    rows = own.shape[0] + sum(p.shape[0] for p in parts[0])
    counts = [len(p) for p in parts]

    steps = (stop - start) // BLOCK

    def kernel(t_ref, own_ref, *refs):
        pieces, refs = split_parts(refs, counts)
        down_w, out, send, rows_ref, held, sems = refs

        def copy(i):
            source = down_w.at[pl.ds(start + i * BLOCK, BLOCK)]
            return pltpu.make_async_copy(source, held.at[i], sems.at[i])

        for i in range(steps):
            copy(i).start()
        lay_out(t_ref[0], own_ref, pieces, rows_ref)

        @pl.loop(0, steps)
        def _(i):
            copy(i).wait()
            total = None
            for q in range(n):
                part = dot_nt(rows_ref[q], held[i, :, q * quarter : (q + 1) * quarter])
                total = part if total is None else total + part
            off = pl.multiple_of(i * BLOCK, BLOCK)
            out[:, pl.ds(off, BLOCK)] = total
            send[:, pl.ds(off, BLOCK)] = total.astype(BF)

    shape = (rows, stop - start)
    return call(
        kernel,
        t,
        [own] + [x for p in parts for x in p] + [down_mat],
        [sds(shape, F32), sds(shape, BF)],
        [
            pltpu.VMEM((n, rows, quarter), BF),
            pltpu.VMEM((steps, BLOCK, depth), BF),
            pltpu.SemaphoreType.DMA((steps,)),
        ],
        2 * rows * depth * (stop - start),
        12,
        "grad_hidden",
        far=1,
    )


STRIP = 32
LIMIT = 8


def strips(rows, body):
    @pl.loop(0, rows // STRIP)
    def _(i):
        body(pl.ds(pl.multiple_of(i * STRIP, STRIP), STRIP))


def hidden_strips(ins, acts):
    (hidden_ref,) = acts

    def body(here):
        at = 0
        for g in range(0, len(ins), 3):
            gate_o, up_o, both_r = ins[g : g + 3]
            width = gate_o.shape[1]
            cols = slice(at, at + width)
            gate = gate_o[here, :] + both_r[here, :width].astype(F32)
            up = up_o[here, :] + both_r[here, width:].astype(F32)
            hidden_ref[here, cols] = (gate * jax.nn.sigmoid(gate) * up).astype(BF)
            at += gate_o.shape[1]

    strips(hidden_ref.shape[0], body)


def grad_strips(ins, acts):
    gg_ref, gu_ref = acts

    def body(here):
        at = 0
        for g in range(0, len(ins), 5):
            gate_o, up_o, both_r, gh_o, gh_r = ins[g : g + 5]
            width = gate_o.shape[1]
            cols = slice(at, at + width)
            gate = gate_o[here, :] + both_r[here, :width].astype(F32)
            up = up_o[here, :] + both_r[here, width:].astype(F32)
            grad = gh_o[here, :] + gh_r[here, :].astype(F32)
            s = jax.nn.sigmoid(gate)
            gg_ref[here, cols] = (grad * up * (s * (1.0 + gate * (1.0 - s)))).astype(BF)
            gu_ref[here, cols] = (grad * (gate * s)).astype(BF)
            at += gate_o.shape[1]

    strips(gg_ref.shape[0], body)


class Stream:
    def __init__(self, mats, n, nn, pieces):
        self.mats, self.nn = len(mats), nn
        self.hidden, depth = mats[0].shape if nn else mats[0].shape[::-1]
        self.quarter = depth // n
        self.blocks = self.quarter // BLOCK
        self.each = 1 if nn else self.blocks
        chunk = (self.hidden, self.quarter) if nn else (BLOCK, self.hidden)
        self.count = pieces * self.each
        total = self.count * self.mats
        self.scratch = [pltpu.VMEM((total,) + chunk, BF), pltpu.SemaphoreType.DMA((total,))]
        self.mib = 2 + 2 * pieces * self.mats * self.hidden * self.quarter // MIB

    def copy(self, chunk, m):
        base = self.bases[0]
        for k in range(1, len(self.bases)):
            base = jnp.where(chunk >= k * self.each, self.bases[k], base)
        width = self.quarter if self.nn else BLOCK
        cut = pl.ds(pl.multiple_of(base + chunk % self.each * width, BLOCK), width)
        source = self.weights[m].at[:, cut] if self.nn else self.weights[m].at[cut]
        slot = chunk * self.mats + m
        return pltpu.make_async_copy(source, self.held.at[slot], self.sems.at[slot])

    def start(self, weights, bases, held, sems):
        self.weights, self.bases, self.held, self.sems = weights, bases, held, sems
        for chunk in range(self.count):
            for m in range(self.mats):
                self.copy(chunk, m).start()

    def products(self, acts, store):
        @pl.loop(0, len(self.bases) * self.blocks)
        def _(i):
            piece, off = i // self.blocks, pl.multiple_of(i % self.blocks * BLOCK, BLOCK)
            if self.nn:

                @pl.when(off == 0)
                def _():
                    self.copy(piece, 0).wait()

                total = dot_nn(acts[0][...], self.held[piece, :, pl.ds(off, BLOCK)])
            else:
                total = None
                for m in range(self.mats):
                    self.copy(i, m).wait()
                    part = dot_nt(acts[m][...], self.held[i * self.mats + m])
                    total = part if total is None else total + part
            store(piece, pl.ds(off, BLOCK), total)


def first_piece(t, n, make, nn, ins, mats, name):
    stream = Stream(mats, n, nn, 1)
    rows = ins[0].shape[0]
    half, quarter, hidden = rows // 2, stream.quarter, stream.hidden

    def kernel(t_ref, *refs):
        parts, refs = refs[: len(ins)], refs[len(ins) :]
        weights, refs = refs[: len(mats)], refs[len(mats) :]
        halves, acts, scratch = refs[:2], refs[2 : 2 + len(mats)], refs[2 + len(mats) :]
        stream.start(weights, [(t_ref[0] ^ 3) * quarter], *scratch)
        make(parts, acts)

        def store(piece, cols, total):
            halves[0][:, cols] = total[:half].astype(BF)
            halves[1][:, cols] = total[half:].astype(BF)

        stream.products(acts, store)

    return call(
        kernel,
        t,
        list(ins) + list(mats),
        [sds((half, quarter), BF)] * 2 + [sds((rows, hidden), BF)] * len(mats),
        stream.scratch,
        2 * rows * quarter * hidden * len(mats),
        stream.mib + 4,
        name,
        far=len(mats),
    )


def pieces(t, n, nn, acts, mats, order, name):
    stream = Stream(mats, n, nn, len(order))
    rows, quarter = acts[0].shape[0], stream.quarter

    def kernel(t_ref, *refs):
        ins, refs = refs[: len(acts)], refs[len(acts) :]
        weights, refs = refs[: len(mats)], refs[len(mats) :]
        out, scratch = refs[0], refs[1:]
        stream.start(weights, [(t_ref[0] ^ j) * quarter for j in order], *scratch)

        def store(piece, cols, total):
            out[piece, :, cols] = total

        stream.products(ins, store)

    (out,) = call(
        kernel,
        t,
        list(acts) + list(mats),
        [sds((len(order), rows, quarter), F32)],
        stream.scratch,
        2 * rows * quarter * len(order) * stream.hidden * len(mats),
        stream.mib + 4,
        name,
        far=len(mats),
    )
    return out


def add_diagonal(t, both, top, low):
    half = top.shape[0]

    def kernel(t_ref, both_ref, top_ref, low_ref, x_out, y_out):
        x_out[:half, :] = both_ref[0, :half, :].astype(BF)
        x_out[half:, :] = (both_ref[0, half:, :] + low_ref[...].astype(F32)).astype(BF)
        y_out[:half, :] = (both_ref[1, :half, :] + top_ref[...].astype(F32)).astype(BF)
        y_out[half:, :] = both_ref[1, half:, :].astype(BF)

    return call(
        kernel, t, [both, top, low], [sds(both.shape[1:], BF)] * 2, [], both.size, LIMIT, "add"
    )


def assemble(t, parts):
    rows, width = parts[0].shape

    def kernel(t_ref, *refs):
        for j, part in enumerate(refs[:-1]):
            refs[-1][:, pl.ds(pl.multiple_of((t_ref[0] ^ j) * width, 128), width)] = part[...]

    (out,) = call(
        kernel, t, parts, [sds((rows, width * len(parts)), parts[0].dtype)], [], 0, LIMIT, "assemble"
    )
    return out


def after(value, *others):
    return lax.optimization_barrier((value,) + others)[0]


def local(tokens, expert_ids, gate_values, w_gate, w_up, w_down, cotangent):
    tok_rows, depth = tokens.shape
    groups = lax.axis_size("expert")
    n = lax.axis_size("tensor")
    z = lax.axis_index("expert")
    t = lax.axis_index("tensor")
    t_arr = t.astype(jnp.int32).reshape(1)
    experts = groups
    cap = min(tok_rows, 3 * tok_rows // experts)
    quarter = depth // n
    gate_mat, up_mat, down_mat = (
        pltpu.with_memory_space_constraint(w[0], pltpu.HBM) for w in (w_gate, w_up, w_down)
    )
    hidden_here = gate_mat.shape[1]

    slot_of = slot_index(expert_ids, experts)
    order = (expert_ids ^ z) * cap + slot_of
    cells = jnp.arange(experts * cap, dtype=jnp.int32)
    pick = [order[:, k][None, :] == cells[:, None] for k in range(2)]
    spread = jnp.logical_or(pick[0], pick[1]).astype(BF)
    slot_gate = jnp.sum(
        jnp.where(pick[0], gate_values[:, 0][None, :], 0.0)
        + jnp.where(pick[1], gate_values[:, 1][None, :], 0.0),
        axis=1,
        keepdims=True,
    )

    def outgoing(source, scale):
        part = lax.dynamic_slice(source, (0, t * quarter), (tok_rows, quarter))
        out = dot_nn(spread[cap:], part)
        own = dot_nn(spread[:cap], source)
        if scale is not None:
            out, own = out * scale[cap:], own * scale[:cap]
        return own.astype(BF), out.astype(BF)

    def over_z(out):
        return [exchange(out[(k - 1) * cap : k * cap], "expert", k) for k in range(1, groups)]

    tok_own, tok_out = outgoing(tokens, None)
    cot_own, cot_out = outgoing(cotangent, slot_gate)
    tok_z = over_z(tok_out)
    first, rest = tok_z[0], tok_z[1:]
    first_far = [exchange(first, "tensor", j) for j in range(1, n)]
    gate_held = fetch(gate_mat)
    rest = jnp.concatenate(after(tuple(rest), gate_held, *first_far), axis=0)
    rest_x, rest_y = exchange(rest, "tensor", 1), exchange(rest, "tensor", 2)
    cot_z = over_z(after(cot_out, rest))
    split = rest.shape[0] // 2
    rest_d = [exchange(rest_y[:split], "tensor", 1), exchange(rest_x[split:], "tensor", 2)]
    tok_parts = [
        [first, rest], [first_far[0], rest_x], [first_far[1], rest_y], [first_far[2], *rest_d]
    ]
    cot_part = jnp.concatenate(after(tuple(cot_z), *rest_d), axis=0)
    cot_parts = [[cot_part]] + [[exchange(cot_part, "tensor", j)] for j in range(1, n)]
    pres = []
    half = hidden_here // 2
    for start, turn in ((0, (cot_part,)), (half, (cot_parts[1][0], cot_parts[2][0]))):
        gate_o, up_o, sent = pre_acts(
            after(t_arr, *turn), tok_own, tok_parts, gate_held, up_mat, start, start + half
        )
        pres.append([gate_o, up_o, exchange(sent, "wide", 1)])

    def summed(arrived, keep):
        total = keep
        for piece in arrived:
            total = total + piece.astype(F32)
        return total.astype(BF)

    def to_tokens(total):
        return [total[:cap]] + [
            exchange(total[k * cap : (k + 1) * cap], "expert", k) for k in range(1, groups)
        ]

    def around(part):
        return [part] + [exchange(part, "tensor", j) for j in range(1, n)]

    gather = [(order[:, k][:, None] == cells[None, :]).astype(BF) for k in range(2)]

    d_top, d_low, hidden = first_piece(
        t_arr, n, hidden_strips, True, sum(pres, []), [down_mat], "project_first"
    )
    added = [exchange(d_top, "tensor", 1), exchange(d_low, "tensor", 2)]
    both = pieces(t_arr, n, True, [hidden], [down_mat], (1, 2), "project_send")
    grads = []
    turn = after(t_arr, both)
    for start in range(0, hidden_here, hidden_here // 2):
        if start:
            to_x, to_y = add_diagonal(t_arr, both, *added)
            turn = after(t_arr, to_x)
        gh_o, gh_s = grad_hiddens(
            turn, cot_own, cot_parts, down_mat, start, start + hidden_here // 2
        )
        grads.append([gh_o, exchange(gh_s, "wide", 1)])
    keep = pieces(after(t_arr, gh_s), n, True, [hidden], [down_mat], (0,), "project_keep")[0]

    e_top, e_low, grad_g, grad_u = first_piece(
        after(t_arr, keep), n, grad_strips, False,
        sum([p + g for p, g in zip(pres, grads)], []), [gate_mat, up_mat], "rows_first",
    )
    gadded = [exchange(e_top, "tensor", 1), exchange(e_low, "tensor", 2)]
    from_x, from_y = exchange(to_x, "tensor", 1), exchange(to_y, "tensor", 2)
    gboth = pieces(
        t_arr, n, False, [grad_g, grad_u], [gate_mat, up_mat], (1, 2), "rows_send",
    )
    gto_x, gto_y = add_diagonal(t_arr, gboth, *gadded)
    gkeep = pieces(
        after(t_arr, gto_x), n, False, [grad_g, grad_u], [gate_mat, up_mat], (0,), "rows_keep"
    )[0]
    gtotal = summed((exchange(gto_x, "tensor", 1), exchange(gto_y, "tensor", 2)), gkeep)
    returned = to_tokens(summed((from_x, from_y), after(keep, gto_x)))
    greturned = to_tokens(gtotal)
    returned = jnp.concatenate(after(tuple(returned), greturned[1]), axis=0)
    chosen = [dot_nn(g, returned) for g in gather]
    layer_part = (gate_values[:, 0:1] * chosen[0] + gate_values[:, 1:2] * chosen[1]).astype(BF)
    layer_parts = around(layer_part)
    layer_out = assemble(t_arr, layer_parts)
    greturned = jnp.concatenate(tuple(greturned), axis=0)
    cot_here = lax.dynamic_slice(cotangent, (0, t * quarter), (tok_rows, quarter)).astype(F32)
    gate_grad = jnp.stack([jnp.sum(cot_here * c, axis=1) for c in chosen], axis=0)
    gate_grad = after(gate_grad, layer_parts[1], layer_parts[2])
    for axis, bit in (("wide", 1), ("tensor", 1), ("tensor", 2)):
        gate_grad = gate_grad + exchange(gate_grad, axis, bit)

    grad_part = (dot_nn(gather[0], greturned) + dot_nn(gather[1], greturned)).astype(BF)
    token_grad = assemble(t_arr, around(grad_part))
    return (layer_out, token_grad, gate_grad.T)


def plain_local(tokens, expert_ids, gate_values, w_gate, w_up, w_down, cotangent):
    tok_rows, depth = tokens.shape
    groups = lax.axis_size("expert")
    experts = groups * w_gate.shape[0]
    cap = min(tok_rows, 3 * tok_rows // experts)
    total_rows = groups * cap
    gate_mat, up_mat, down_mat = w_gate[0], w_up[0], w_down[0]
    order = expert_ids * cap + slot_index(expert_ids, experts)
    cells = jnp.arange(experts * cap, dtype=jnp.int32)
    pick = [order[:, k][None, :] == cells[:, None] for k in range(2)]
    gather = [(order[:, k][:, None] == cells[None, :]).astype(BF) for k in range(2)]

    def to_owners(rows):
        out = rows.astype(BF).reshape(groups, cap, depth)
        out = lax.all_to_all(out, "expert", split_axis=0, concat_axis=0, tiled=True)
        return out.reshape(total_rows, depth)

    def send_back(rows):
        share = lax.psum_scatter(rows, "tensor", scatter_dimension=0, tiled=True).astype(BF)
        return to_owners(lax.all_gather(share, "tensor", axis=0, tiled=True))

    spread = jnp.logical_or(pick[0], pick[1]).astype(BF)
    arrived = to_owners(dot_nn(spread, tokens))
    gate_pre, up_pre = lax.psum((dot_nn(arrived, gate_mat), dot_nn(arrived, up_mat)), "wide")
    s = jax.nn.sigmoid(gate_pre)
    returned = send_back(dot_nn((gate_pre * s * up_pre).astype(BF), down_mat))
    chosen = [dot_nn(g, returned) for g in gather]
    layer_out = (gate_values[:, 0:1] * chosen[0] + gate_values[:, 1:2] * chosen[1]).astype(BF)
    upstream = cotangent.astype(F32)
    gate_grad = lax.psum(
        jnp.stack([jnp.sum(upstream * c, axis=1) for c in chosen], axis=1), "wide"
    )
    slot_gate = jnp.sum(
        jnp.where(pick[0], gate_values[:, 0][None, :], 0.0)
        + jnp.where(pick[1], gate_values[:, 1][None, :], 0.0),
        axis=1,
        keepdims=True,
    )
    grad_arrived = to_owners(dot_nn(spread, cotangent) * slot_gate)
    grad_hidden = lax.psum(dot_nt(grad_arrived, down_mat), "wide")
    grad_gate = (grad_hidden * up_pre * (s * (1.0 + gate_pre * (1.0 - s)))).astype(BF)
    grad_up = (grad_hidden * (gate_pre * s)).astype(BF)
    back = send_back(dot_nt(grad_gate, gate_mat) + dot_nt(grad_up, up_mat))
    token_grad = (dot_nn(gather[0], back) + dot_nn(gather[1], back)).astype(BF)
    return (layer_out, token_grad, gate_grad)


def solution(mesh):
    in_specs = (
        P("expert", "wide"),
        P("expert", None),
        P("expert", None),
        P("expert", "wide", "tensor"),
        P("expert", "wide", "tensor"),
        P("expert", "tensor", "wide"),
        P("expert", "wide"),
    )
    out_specs = (P("expert", "wide"), P("expert", "wide"), P("expert", None))
    laid_out = mesh.shape["tensor"] == 4 and mesh.shape["expert"] == 4 and mesh.shape["wide"] == 2
    return jax.shard_map(
        local if laid_out else plain_local,
        mesh=mesh,
        in_specs=in_specs,
        out_specs=out_specs,
        check_vma=False,
    )
```

```python
import jax
import jax.numpy as jnp
from jax import lax
from jax.experimental import pallas as pl
from jax.experimental.pallas import tpu as pltpu
from jax.sharding import PartitionSpec as P

BF = jnp.bfloat16
F32 = jnp.float32
MIB = 1024 * 1024


def slot_index(expert_ids, experts):
    hit_table = (expert_ids[:, :, None] == jnp.arange(experts, dtype=jnp.int32)).astype(jnp.int32)
    per_row = jnp.sum(hit_table, axis=1)
    before = jnp.cumsum(per_row, axis=0) - per_row
    return jnp.sum(hit_table * before[:, None, :], axis=2)


def exchange(array, axis, bit):
    size = lax.axis_size(axis)
    return lax.ppermute(array, axis, [(i, i ^ bit) for i in range(size)])


def dot_nn(a, b):
    return jnp.dot(a, b, preferred_element_type=F32)


def dot_nt(a, b):
    return lax.dot_general(a, b, (((1,), (1,)), ((), ())), preferred_element_type=F32)


def params(mib):
    return pltpu.CompilerParams(vmem_limit_bytes=mib * MIB)


VMEM = pl.BlockSpec(memory_space=pltpu.VMEM)
HBM = pl.BlockSpec(memory_space=pltpu.HBM)
SMEM = pl.BlockSpec(memory_space=pltpu.SMEM)


def sds(shape, dtype):
    return jax.ShapeDtypeStruct(shape, dtype)


def call(kernel, t, ins, outs, scratch, flops, mib, name, far=0):
    return pl.pallas_call(
        kernel,
        in_specs=[SMEM] + [VMEM] * (len(ins) - far) + [HBM] * far,
        out_specs=[VMEM] * len(outs),
        out_shape=outs,
        scratch_shapes=scratch,
        compiler_params=params(mib),
        cost_estimate=pl.CostEstimate(flops=flops // 2, bytes_accessed=MIB, transcendentals=0),
        name=name,
    )(t, *ins)


def fetch(matrix):
    def kernel(source, held, sem):
        copy = pltpu.make_async_copy(source, held, sem)
        copy.start()
        copy.wait()

    return pl.pallas_call(
        kernel,
        in_specs=[HBM],
        out_specs=VMEM,
        out_shape=pltpu.VMEM(matrix.shape, matrix.dtype),
        scratch_shapes=[pltpu.SemaphoreType.DMA],
        compiler_params=params(LIMIT),
        cost_estimate=pl.CostEstimate(
            flops=0, bytes_accessed=2 * matrix.size, transcendentals=0
        ),
        name="fetch",
    )(matrix)


def lay_out(t, own, parts, rows_ref):
    cap = own.shape[0]
    n, _, quarter = rows_ref.shape
    for q in range(n):
        rows_ref[q, :cap, :] = own[:, q * quarter : (q + 1) * quarter]
    for j in range(n):
        at = cap
        for piece in parts[j]:
            rows_ref[t ^ j, at : at + piece.shape[0], :] = piece[...]
            at += piece.shape[0]


def split_parts(refs, counts):
    parts, at = [], 0
    for c in counts:
        parts.append(refs[at : at + c])
        at += c
    return parts, refs[at:]


BLOCK = 256


def pre_acts(t, own, parts, gate_held, up_mat, start, stop):
    depth = up_mat.shape[0]
    n = len(parts)
    quarter = depth // n
    rows = own.shape[0] + sum(p.shape[0] for p in parts[0])
    counts = [len(p) for p in parts]
    width = stop - start

    def kernel(t_ref, own_ref, *refs):
        pieces, refs = split_parts(refs, counts)
        gate_w, up_w, gate_o, up_o, send, rows_ref, up_held, sem = refs
        copy = pltpu.make_async_copy(up_w.at[:, pl.ds(start, width)], up_held, sem)
        copy.start()
        lay_out(t_ref[0], own_ref, pieces, rows_ref)
        for w, base, out, at in ((gate_w, start, gate_o, 0), (up_held, 0, up_o, width)):
            if at:
                copy.wait()

            @pl.loop(0, width // BLOCK)
            def _(i):
                off = pl.multiple_of(i * BLOCK, BLOCK)
                total = None
                for q in range(n):
                    part = dot_nn(
                        rows_ref[q], w[q * quarter : (q + 1) * quarter, pl.ds(base + off, BLOCK)]
                    )
                    total = part if total is None else total + part
                out[:, pl.ds(off, BLOCK)] = total
                send[:, pl.ds(at + off, BLOCK)] = total.astype(BF)

    shape = (rows, width)
    return call(
        kernel,
        t,
        [own] + [x for p in parts for x in p] + [gate_held, up_mat],
        [sds(shape, F32)] * 2 + [sds((rows, 2 * width), BF)],
        [
            pltpu.VMEM((n, rows, quarter), BF),
            pltpu.VMEM((depth, width), BF),
            pltpu.SemaphoreType.DMA,
        ],
        4 * rows * depth * width,
        14,
        "pre_acts",
        far=1,
    )


def grad_hiddens(t, own, parts, down_mat, start, stop):
    depth = down_mat.shape[1]
    n = len(parts)
    quarter = depth // n
    rows = own.shape[0] + sum(p.shape[0] for p in parts[0])
    counts = [len(p) for p in parts]

    steps = (stop - start) // BLOCK

    def kernel(t_ref, own_ref, *refs):
        pieces, refs = split_parts(refs, counts)
        down_w, out, send, rows_ref, held, sems = refs

        def copy(i):
            source = down_w.at[pl.ds(start + i * BLOCK, BLOCK)]
            return pltpu.make_async_copy(source, held.at[i], sems.at[i])

        for i in range(steps):
            copy(i).start()
        lay_out(t_ref[0], own_ref, pieces, rows_ref)

        @pl.loop(0, steps)
        def _(i):
            copy(i).wait()
            total = None
            for q in range(n):
                part = dot_nt(rows_ref[q], held[i, :, q * quarter : (q + 1) * quarter])
                total = part if total is None else total + part
            off = pl.multiple_of(i * BLOCK, BLOCK)
            out[:, pl.ds(off, BLOCK)] = total
            send[:, pl.ds(off, BLOCK)] = total.astype(BF)

    shape = (rows, stop - start)
    return call(
        kernel,
        t,
        [own] + [x for p in parts for x in p] + [down_mat],
        [sds(shape, F32), sds(shape, BF)],
        [
            pltpu.VMEM((n, rows, quarter), BF),
            pltpu.VMEM((steps, BLOCK, depth), BF),
            pltpu.SemaphoreType.DMA((steps,)),
        ],
        4 * rows * depth * (stop - start),
        18,
        "grad_hidden",
        far=1,
    )


STRIP = 32
LIMIT = 8


def strips(rows, body):
    @pl.loop(0, rows // STRIP)
    def _(i):
        body(pl.ds(pl.multiple_of(i * STRIP, STRIP), STRIP))


def hidden_strips(ins, acts):
    (hidden_ref,) = acts

    def body(here):
        at = 0
        for g in range(0, len(ins), 3):
            gate_o, up_o, both_r = ins[g : g + 3]
            width = gate_o.shape[1]
            cols = slice(at, at + width)
            gate = gate_o[here, :] + both_r[here, :width].astype(F32)
            up = up_o[here, :] + both_r[here, width:].astype(F32)
            hidden_ref[here, cols] = (gate * jax.nn.sigmoid(gate) * up).astype(BF)
            at += gate_o.shape[1]

    strips(hidden_ref.shape[0], body)


def grad_strips(ins, acts):
    gg_ref, gu_ref = acts
    share = len(ins) // 5
    ins, grads = ins[: 3 * share], ins[3 * share :]

    def body(here):
        at = 0
        for g in range(share):
            gate_o, up_o, both_r = ins[3 * g : 3 * g + 3]
            gh_o, gh_r = grads[2 * g : 2 * g + 2]
            width = gate_o.shape[1]
            cols = slice(at, at + width)
            gate = gate_o[here, :] + both_r[here, :width].astype(F32)
            up = up_o[here, :] + both_r[here, width:].astype(F32)
            grad = gh_o[here, :] + gh_r[here, :].astype(F32)
            s = jax.nn.sigmoid(gate)
            gg_ref[here, cols] = (grad * up * (s * (1.0 + gate * (1.0 - s)))).astype(BF)
            gu_ref[here, cols] = (grad * (gate * s)).astype(BF)
            at += width

    strips(gg_ref.shape[0], body)


class Stream:
    def __init__(self, mats, n, nn, pieces):
        self.mats, self.nn = len(mats), nn
        self.hidden, depth = mats[0].shape if nn else mats[0].shape[::-1]
        self.quarter = depth // n
        self.blocks = self.quarter // BLOCK
        self.each = 1 if nn else self.blocks
        chunk = (self.hidden, self.quarter) if nn else (BLOCK, self.hidden)
        self.count = pieces * self.each
        total = self.count * self.mats
        self.scratch = [pltpu.VMEM((total,) + chunk, BF), pltpu.SemaphoreType.DMA((total,))]
        self.mib = 2 + 2 * pieces * self.mats * self.hidden * self.quarter // MIB

    def copy(self, chunk, m):
        base = self.bases[0]
        for k in range(1, len(self.bases)):
            base = jnp.where(chunk >= k * self.each, self.bases[k], base)
        width = self.quarter if self.nn else BLOCK
        cut = pl.ds(pl.multiple_of(base + chunk % self.each * width, BLOCK), width)
        source = self.weights[m].at[:, cut] if self.nn else self.weights[m].at[cut]
        slot = chunk * self.mats + m
        return pltpu.make_async_copy(source, self.held.at[slot], self.sems.at[slot])

    def start(self, weights, bases, held, sems):
        self.weights, self.bases, self.held, self.sems = weights, bases, held, sems
        for chunk in range(self.count):
            for m in range(self.mats):
                self.copy(chunk, m).start()

    def products(self, acts, store):
        @pl.loop(0, len(self.bases) * self.blocks)
        def _(i):
            piece, off = i // self.blocks, pl.multiple_of(i % self.blocks * BLOCK, BLOCK)
            if self.nn:

                @pl.when(off == 0)
                def _():
                    self.copy(piece, 0).wait()

                total = dot_nn(acts[0][...], self.held[piece, :, pl.ds(off, BLOCK)])
            else:
                total = None
                for m in range(self.mats):
                    self.copy(i, m).wait()
                    part = dot_nt(acts[m][...], self.held[i * self.mats + m])
                    total = part if total is None else total + part
            store(piece, pl.ds(off, BLOCK), total)


def first_piece(t, n, make, nn, ins, mats, others, name):
    stream = Stream(mats, n, nn, 1 + len(others))
    rows = ins[0].shape[0]
    half, quarter, hidden = rows // 2, stream.quarter, stream.hidden

    def kernel(t_ref, *refs):
        parts, refs = refs[: len(ins)], refs[len(ins) :]
        weights, refs = refs[: len(mats)], refs[len(mats) :]
        halves, acts, refs = refs[:2], refs[2 : 2 + len(mats)], refs[2 + len(mats) :]
        stream.start(weights, [(t_ref[0] ^ j) * quarter for j in (3, *others)], *refs[-2:])
        make(parts, acts)

        def store(piece, cols, total):
            @pl.when(piece == 0)
            def _():
                halves[0][:, cols] = total[:half].astype(BF)
                halves[1][:, cols] = total[half:].astype(BF)

            if others:

                @pl.when(piece > 0)
                def _():
                    refs[0][piece - 1, :, cols] = total

        stream.products(acts, store)

    outs = [sds((half, quarter), BF)] * 2 + [sds((rows, hidden), BF)] * len(mats)
    return call(
        kernel,
        t,
        list(ins) + list(mats),
        outs + ([sds((len(others), rows, quarter), F32)] if others else []),
        stream.scratch,
        2 * rows * quarter * (1 + len(others)) * hidden * len(mats),
        stream.mib + 4,
        name,
        far=len(mats),
    )


def pieces(t, n, nn, acts, mats, order, name):
    stream = Stream(mats, n, nn, len(order))
    rows, quarter = acts[0].shape[0], stream.quarter

    def kernel(t_ref, *refs):
        ins, refs = refs[: len(acts)], refs[len(acts) :]
        weights, refs = refs[: len(mats)], refs[len(mats) :]
        out, scratch = refs[0], refs[1:]
        stream.start(weights, [(t_ref[0] ^ j) * quarter for j in order], *scratch)

        def store(piece, cols, total):
            out[piece, :, cols] = total

        stream.products(ins, store)

    (out,) = call(
        kernel,
        t,
        list(acts) + list(mats),
        [sds((len(order), rows, quarter), F32)],
        stream.scratch,
        2 * rows * quarter * len(order) * stream.hidden * len(mats),
        stream.mib + 4,
        name,
        far=len(mats),
    )
    return out


def add_diagonal(t, both, top, low):
    half = top.shape[0]

    def kernel(t_ref, both_ref, top_ref, low_ref, x_out, y_out):
        x_out[:half, :] = both_ref[0, :half, :].astype(BF)
        x_out[half:, :] = (both_ref[0, half:, :] + low_ref[...].astype(F32)).astype(BF)
        y_out[:half, :] = (both_ref[1, :half, :] + top_ref[...].astype(F32)).astype(BF)
        y_out[half:, :] = both_ref[1, half:, :].astype(BF)

    return call(
        kernel, t, [both, top, low], [sds(both.shape[1:], BF)] * 2, [], both.size, LIMIT, "add"
    )


def assemble(t, parts):
    rows, width = parts[0].shape

    def kernel(t_ref, *refs):
        for j, part in enumerate(refs[:-1]):
            refs[-1][:, pl.ds(pl.multiple_of((t_ref[0] ^ j) * width, 128), width)] = part[...]

    (out,) = call(
        kernel, t, parts, [sds((rows, width * len(parts)), parts[0].dtype)], [], 0, LIMIT, "assemble"
    )
    return out


def after(value, *others):
    return lax.optimization_barrier((value,) + others)[0]


def local(tokens, expert_ids, gate_values, w_gate, w_up, w_down, cotangent):
    tok_rows, depth = tokens.shape
    groups = lax.axis_size("expert")
    n = lax.axis_size("tensor")
    z = lax.axis_index("expert")
    t = lax.axis_index("tensor")
    t_arr = t.astype(jnp.int32).reshape(1)
    experts = groups
    cap = min(tok_rows, 3 * tok_rows // experts)
    quarter = depth // n
    gate_mat, up_mat, down_mat = (
        pltpu.with_memory_space_constraint(w[0], pltpu.HBM) for w in (w_gate, w_up, w_down)
    )
    hidden_here = gate_mat.shape[1]

    slot_of = slot_index(expert_ids, experts)
    order = (expert_ids ^ z) * cap + slot_of
    cells = jnp.arange(experts * cap, dtype=jnp.int32)
    pick = [order[:, k][None, :] == cells[:, None] for k in range(2)]
    spread = jnp.logical_or(pick[0], pick[1]).astype(BF)
    slot_gate = jnp.sum(
        jnp.where(pick[0], gate_values[:, 0][None, :], 0.0)
        + jnp.where(pick[1], gate_values[:, 1][None, :], 0.0),
        axis=1,
        keepdims=True,
    )

    def outgoing(source, scale):
        part = lax.dynamic_slice(source, (0, t * quarter), (tok_rows, quarter))
        out = dot_nn(spread[cap:], part)
        own = dot_nn(spread[:cap], source)
        if scale is not None:
            out, own = out * scale[cap:], own * scale[:cap]
        return own.astype(BF), out.astype(BF)

    def over_z(out):
        return [exchange(out[(k - 1) * cap : k * cap], "expert", k) for k in range(1, groups)]

    tok_own, tok_out = outgoing(tokens, None)
    cot_own, cot_out = outgoing(cotangent, slot_gate)
    tok_z = over_z(tok_out)
    first, rest = tok_z[0], tok_z[1:]
    first_far = [exchange(first, "tensor", j) for j in range(1, n)]
    gate_held = fetch(gate_mat)
    rest = jnp.concatenate(after(tuple(rest), gate_held, *first_far), axis=0)
    rest_x, rest_y = exchange(rest, "tensor", 1), exchange(rest, "tensor", 2)
    cot_z = over_z(after(cot_out, rest))
    split = rest.shape[0] // 2
    rest_d = [exchange(rest_y[:split], "tensor", 1), exchange(rest_x[split:], "tensor", 2)]
    tok_parts = [
        [first, rest], [first_far[0], rest_x], [first_far[1], rest_y], [first_far[2], *rest_d]
    ]
    cot_part = jnp.concatenate(after(tuple(cot_z), *rest_d), axis=0)
    cot_parts = [[cot_part]] + [[exchange(cot_part, "tensor", j)] for j in range(1, n)]
    pres = []
    cut = hidden_here * 5 // 8 // BLOCK * BLOCK
    for start, stop, turn in (
        (0, cut, (cot_part,)),
        (cut, hidden_here, (cot_parts[1][0], cot_parts[2][0])),
    ):
        gate_o, up_o, sent = pre_acts(
            after(t_arr, *turn), tok_own, tok_parts, gate_held, up_mat, start, stop
        )
        pres += [gate_o, up_o, exchange(sent, "wide", 1)]

    def summed(arrived, keep):
        total = keep
        for piece in arrived:
            total = total + piece.astype(F32)
        return total.astype(BF)

    def to_tokens(total):
        return [total[:cap]] + [
            exchange(total[k * cap : (k + 1) * cap], "expert", k) for k in range(1, groups)
        ]

    def around(part):
        return [part] + [exchange(part, "tensor", j) for j in range(1, n)]

    gather = [(order[:, k][:, None] == cells[None, :]).astype(BF) for k in range(2)]

    d_top, d_low, hidden, both = first_piece(
        t_arr, n, hidden_strips, True, pres, [down_mat], (1, 2), "project_send"
    )
    added = [exchange(d_top, "tensor", 1), exchange(d_low, "tensor", 2)]
    grads = []
    turn = after(t_arr, both)
    for start, stop in ((0, cut), (cut, hidden_here)):
        if start:
            to_x, to_y = add_diagonal(t_arr, both, *added)
            turn = after(t_arr, to_x)
        gh_o, gh_s = grad_hiddens(turn, cot_own, cot_parts, down_mat, start, stop)
        grads += [gh_o, exchange(gh_s, "wide", 1)]
    keep = pieces(after(t_arr, gh_s), n, True, [hidden], [down_mat], (0,), "project_keep")[0]

    e_top, e_low, grad_g, grad_u = first_piece(
        after(t_arr, keep), n, grad_strips, False,
        pres + grads, [gate_mat, up_mat], (), "rows_first",
    )
    gadded = [exchange(e_top, "tensor", 1), exchange(e_low, "tensor", 2)]
    from_x, from_y = exchange(to_x, "tensor", 1), exchange(to_y, "tensor", 2)
    gboth = pieces(
        t_arr, n, False, [grad_g, grad_u], [gate_mat, up_mat], (1, 2), "rows_send",
    )
    gto_x, gto_y = add_diagonal(t_arr, gboth, *gadded)
    gkeep = pieces(
        after(t_arr, gto_x), n, False, [grad_g, grad_u], [gate_mat, up_mat], (0,), "rows_keep"
    )[0]
    gtotal = summed((exchange(gto_x, "tensor", 1), exchange(gto_y, "tensor", 2)), gkeep)
    returned = to_tokens(summed((from_x, from_y), after(keep, gto_x)))
    greturned = to_tokens(gtotal)
    returned = jnp.concatenate(after(tuple(returned), greturned[1]), axis=0)
    chosen = [dot_nn(g, returned) for g in gather]
    layer_part = (gate_values[:, 0:1] * chosen[0] + gate_values[:, 1:2] * chosen[1]).astype(BF)
    layer_parts = around(layer_part)
    layer_out = assemble(t_arr, layer_parts)
    greturned = jnp.concatenate(tuple(greturned), axis=0)
    cot_here = lax.dynamic_slice(cotangent, (0, t * quarter), (tok_rows, quarter)).astype(F32)
    gate_grad = jnp.stack([jnp.sum(cot_here * c, axis=1) for c in chosen], axis=0)
    gate_grad = after(gate_grad, layer_parts[1], layer_parts[2])
    for axis, bit in (("wide", 1), ("tensor", 1), ("tensor", 2)):
        gate_grad = gate_grad + exchange(gate_grad, axis, bit)

    grad_part = (dot_nn(gather[0], greturned) + dot_nn(gather[1], greturned)).astype(BF)
    token_grad = assemble(t_arr, around(grad_part))
    return (layer_out, token_grad, gate_grad.T)


def plain_local(tokens, expert_ids, gate_values, w_gate, w_up, w_down, cotangent):
    tok_rows, depth = tokens.shape
    groups = lax.axis_size("expert")
    experts = groups * w_gate.shape[0]
    cap = min(tok_rows, 3 * tok_rows // experts)
    total_rows = groups * cap
    gate_mat, up_mat, down_mat = w_gate[0], w_up[0], w_down[0]
    order = expert_ids * cap + slot_index(expert_ids, experts)
    cells = jnp.arange(experts * cap, dtype=jnp.int32)
    pick = [order[:, k][None, :] == cells[:, None] for k in range(2)]
    gather = [(order[:, k][:, None] == cells[None, :]).astype(BF) for k in range(2)]

    def to_owners(rows):
        out = rows.astype(BF).reshape(groups, cap, depth)
        out = lax.all_to_all(out, "expert", split_axis=0, concat_axis=0, tiled=True)
        return out.reshape(total_rows, depth)

    def send_back(rows):
        share = lax.psum_scatter(rows, "tensor", scatter_dimension=0, tiled=True).astype(BF)
        return to_owners(lax.all_gather(share, "tensor", axis=0, tiled=True))

    spread = jnp.logical_or(pick[0], pick[1]).astype(BF)
    arrived = to_owners(dot_nn(spread, tokens))
    gate_pre, up_pre = lax.psum((dot_nn(arrived, gate_mat), dot_nn(arrived, up_mat)), "wide")
    s = jax.nn.sigmoid(gate_pre)
    returned = send_back(dot_nn((gate_pre * s * up_pre).astype(BF), down_mat))
    chosen = [dot_nn(g, returned) for g in gather]
    layer_out = (gate_values[:, 0:1] * chosen[0] + gate_values[:, 1:2] * chosen[1]).astype(BF)
    upstream = cotangent.astype(F32)
    gate_grad = lax.psum(
        jnp.stack([jnp.sum(upstream * c, axis=1) for c in chosen], axis=1), "wide"
    )
    slot_gate = jnp.sum(
        jnp.where(pick[0], gate_values[:, 0][None, :], 0.0)
        + jnp.where(pick[1], gate_values[:, 1][None, :], 0.0),
        axis=1,
        keepdims=True,
    )
    grad_arrived = to_owners(dot_nn(spread, cotangent) * slot_gate)
    grad_hidden = lax.psum(dot_nt(grad_arrived, down_mat), "wide")
    grad_gate = (grad_hidden * up_pre * (s * (1.0 + gate_pre * (1.0 - s)))).astype(BF)
    grad_up = (grad_hidden * (gate_pre * s)).astype(BF)
    back = send_back(dot_nt(grad_gate, gate_mat) + dot_nt(grad_up, up_mat))
    token_grad = (dot_nn(gather[0], back) + dot_nn(gather[1], back)).astype(BF)
    return (layer_out, token_grad, gate_grad)


def solution(mesh):
    in_specs = (
        P("expert", "wide"),
        P("expert", None),
        P("expert", None),
        P("expert", "wide", "tensor"),
        P("expert", "wide", "tensor"),
        P("expert", "tensor", "wide"),
        P("expert", "wide"),
    )
    out_specs = (P("expert", "wide"), P("expert", "wide"), P("expert", None))
    laid_out = mesh.shape["tensor"] == 4 and mesh.shape["expert"] == 4 and mesh.shape["wide"] == 2
    return jax.shard_map(
        local if laid_out else plain_local,
        mesh=mesh,
        in_specs=in_specs,
        out_specs=out_specs,
        check_vma=False,
    )
```

```python
import jax
import jax.numpy as jnp
from jax import lax
from jax.experimental import pallas as pl
from jax.experimental.pallas import tpu as pltpu
from jax.sharding import PartitionSpec as P

BF = jnp.bfloat16
F32 = jnp.float32
MIB = 1024 * 1024


def slot_index(expert_ids, experts):
    hit_table = (expert_ids[:, :, None] == jnp.arange(experts, dtype=jnp.int32)).astype(jnp.int32)
    per_row = jnp.sum(hit_table, axis=1)
    before = jnp.cumsum(per_row, axis=0) - per_row
    return jnp.sum(hit_table * before[:, None, :], axis=2)


def exchange(array, axis, bit):
    size = lax.axis_size(axis)
    return lax.ppermute(array, axis, [(i, i ^ bit) for i in range(size)])


def dot_nn(a, b):
    return jnp.dot(a, b, preferred_element_type=F32)


def dot_nt(a, b):
    return lax.dot_general(a, b, (((1,), (1,)), ((), ())), preferred_element_type=F32)


def params(mib):
    return pltpu.CompilerParams(vmem_limit_bytes=mib * MIB)


VMEM = pl.BlockSpec(memory_space=pltpu.VMEM)
HBM = pl.BlockSpec(memory_space=pltpu.HBM)
SMEM = pl.BlockSpec(memory_space=pltpu.SMEM)


def sds(shape, dtype):
    return jax.ShapeDtypeStruct(shape, dtype)


def call(kernel, t, ins, outs, scratch, flops, mib, name, far=0):
    return pl.pallas_call(
        kernel,
        in_specs=[SMEM] + [VMEM] * (len(ins) - far) + [HBM] * far,
        out_specs=[VMEM] * len(outs),
        out_shape=outs,
        scratch_shapes=scratch,
        compiler_params=params(mib),
        cost_estimate=pl.CostEstimate(flops=flops // 2, bytes_accessed=MIB, transcendentals=0),
        name=name,
    )(t, *ins)


def fetch(matrix):
    def kernel(source, held, sem):
        copy = pltpu.make_async_copy(source, held, sem)
        copy.start()
        copy.wait()

    return pl.pallas_call(
        kernel,
        in_specs=[HBM],
        out_specs=VMEM,
        out_shape=pltpu.VMEM(matrix.shape, matrix.dtype),
        scratch_shapes=[pltpu.SemaphoreType.DMA],
        compiler_params=params(LIMIT),
        cost_estimate=pl.CostEstimate(
            flops=0, bytes_accessed=2 * matrix.size, transcendentals=0
        ),
        name="fetch",
    )(matrix)


def lay_out(t, own, parts, rows_ref):
    cap = own.shape[0]
    n, _, quarter = rows_ref.shape
    for q in range(n):
        rows_ref[q, :cap, :] = own[:, q * quarter : (q + 1) * quarter]
    for j in range(n):
        at = cap
        for piece in parts[j]:
            rows_ref[t ^ j, at : at + piece.shape[0], :] = piece[...]
            at += piece.shape[0]


def split_parts(refs, counts):
    parts, at = [], 0
    for c in counts:
        parts.append(refs[at : at + c])
        at += c
    return parts, refs[at:]


BLOCK = 256


def pre_acts(t, own, parts, gate_held, up_mat, start, stop):
    depth = up_mat.shape[0]
    n = len(parts)
    quarter = depth // n
    rows = own.shape[0] + sum(p.shape[0] for p in parts[0])
    counts = [len(p) for p in parts]
    width = stop - start

    def kernel(t_ref, own_ref, *refs):
        pieces, refs = split_parts(refs, counts)
        gate_w, up_w, gate_o, up_o, send, rows_ref, up_held, sem = refs
        copy = pltpu.make_async_copy(up_w.at[:, pl.ds(start, width)], up_held, sem)
        copy.start()
        lay_out(t_ref[0], own_ref, pieces, rows_ref)
        for w, base, out, at in ((gate_w, start, gate_o, 0), (up_held, 0, up_o, width)):
            if at:
                copy.wait()

            @pl.loop(0, width // BLOCK)
            def _(i):
                off = pl.multiple_of(i * BLOCK, BLOCK)
                total = None
                for q in range(n):
                    part = dot_nn(
                        rows_ref[q], w[q * quarter : (q + 1) * quarter, pl.ds(base + off, BLOCK)]
                    )
                    total = part if total is None else total + part
                out[:, pl.ds(off, BLOCK)] = total
                send[:, pl.ds(at + off, BLOCK)] = total.astype(BF)

    shape = (rows, width)
    return call(
        kernel,
        t,
        [own] + [x for p in parts for x in p] + [gate_held, up_mat],
        [sds(shape, F32)] * 2 + [sds((rows, 2 * width), BF)],
        [
            pltpu.VMEM((n, rows, quarter), BF),
            pltpu.VMEM((depth, width), BF),
            pltpu.SemaphoreType.DMA,
        ],
        4 * rows * depth * width,
        14,
        "pre_acts",
        far=1,
    )


def grad_hiddens(t, own, parts, down_mat, start, stop):
    depth = down_mat.shape[1]
    n = len(parts)
    quarter = depth // n
    rows = own.shape[0] + sum(p.shape[0] for p in parts[0])
    counts = [len(p) for p in parts]

    steps = (stop - start) // BLOCK

    def kernel(t_ref, own_ref, *refs):
        pieces, refs = split_parts(refs, counts)
        down_w, out, send, rows_ref, held, sems = refs

        def copy(i):
            source = down_w.at[pl.ds(start + i * BLOCK, BLOCK)]
            return pltpu.make_async_copy(source, held.at[i], sems.at[i])

        for i in range(steps):
            copy(i).start()
        lay_out(t_ref[0], own_ref, pieces, rows_ref)

        @pl.loop(0, steps)
        def _(i):
            copy(i).wait()
            total = None
            for q in range(n):
                part = dot_nt(rows_ref[q], held[i, :, q * quarter : (q + 1) * quarter])
                total = part if total is None else total + part
            off = pl.multiple_of(i * BLOCK, BLOCK)
            out[:, pl.ds(off, BLOCK)] = total
            send[:, pl.ds(off, BLOCK)] = total.astype(BF)

    shape = (rows, stop - start)
    return call(
        kernel,
        t,
        [own] + [x for p in parts for x in p] + [down_mat],
        [sds(shape, F32), sds(shape, BF)],
        [
            pltpu.VMEM((n, rows, quarter), BF),
            pltpu.VMEM((steps, BLOCK, depth), BF),
            pltpu.SemaphoreType.DMA((steps,)),
        ],
        4 * rows * depth * (stop - start),
        18,
        "grad_hidden",
        far=1,
    )


STRIP = 32
LIMIT = 8


def strips(rows, body):
    @pl.loop(0, rows // STRIP)
    def _(i):
        body(pl.ds(pl.multiple_of(i * STRIP, STRIP), STRIP))


def hidden_strips(ins, acts):
    (hidden_ref,) = acts

    def body(here):
        at = 0
        for g in range(0, len(ins), 3):
            gate_o, up_o, both_r = ins[g : g + 3]
            width = gate_o.shape[1]
            cols = slice(at, at + width)
            gate = gate_o[here, :] + both_r[here, :width].astype(F32)
            up = up_o[here, :] + both_r[here, width:].astype(F32)
            hidden_ref[here, cols] = (gate * jax.nn.sigmoid(gate) * up).astype(BF)
            at += gate_o.shape[1]

    strips(hidden_ref.shape[0], body)


def grad_strips(ins, acts):
    gg_ref, gu_ref = acts
    share = len(ins) // 5
    ins, grads = ins[: 3 * share], ins[3 * share :]

    def body(here):
        at = 0
        for g in range(share):
            gate_o, up_o, both_r = ins[3 * g : 3 * g + 3]
            gh_o, gh_r = grads[2 * g : 2 * g + 2]
            width = gate_o.shape[1]
            cols = slice(at, at + width)
            gate = gate_o[here, :] + both_r[here, :width].astype(F32)
            up = up_o[here, :] + both_r[here, width:].astype(F32)
            grad = gh_o[here, :] + gh_r[here, :].astype(F32)
            s = jax.nn.sigmoid(gate)
            gg_ref[here, cols] = (grad * up * (s * (1.0 + gate * (1.0 - s)))).astype(BF)
            gu_ref[here, cols] = (grad * (gate * s)).astype(BF)
            at += width

    strips(gg_ref.shape[0], body)


class Stream:
    def __init__(self, mats, n, nn, pieces):
        self.mats, self.nn = len(mats), nn
        self.hidden, depth = mats[0].shape if nn else mats[0].shape[::-1]
        self.quarter = depth // n
        self.blocks = self.quarter // BLOCK
        self.each = 1 if nn else self.blocks
        chunk = (self.hidden, self.quarter) if nn else (BLOCK, self.hidden)
        self.count = pieces * self.each
        total = self.count * self.mats
        self.scratch = [pltpu.VMEM((total,) + chunk, BF), pltpu.SemaphoreType.DMA((total,))]
        self.mib = 2 + 2 * pieces * self.mats * self.hidden * self.quarter // MIB

    def copy(self, chunk, m):
        base = self.bases[0]
        for k in range(1, len(self.bases)):
            base = jnp.where(chunk >= k * self.each, self.bases[k], base)
        width = self.quarter if self.nn else BLOCK
        cut = pl.ds(pl.multiple_of(base + chunk % self.each * width, BLOCK), width)
        source = self.weights[m].at[:, cut] if self.nn else self.weights[m].at[cut]
        slot = chunk * self.mats + m
        return pltpu.make_async_copy(source, self.held.at[slot], self.sems.at[slot])

    def start(self, weights, bases, held, sems):
        self.weights, self.bases, self.held, self.sems = weights, bases, held, sems
        for chunk in range(self.count):
            for m in range(self.mats):
                self.copy(chunk, m).start()

    def products(self, acts, store):
        @pl.loop(0, len(self.bases) * self.blocks)
        def _(i):
            piece, off = i // self.blocks, pl.multiple_of(i % self.blocks * BLOCK, BLOCK)
            if self.nn:

                @pl.when(off == 0)
                def _():
                    self.copy(piece, 0).wait()

                total = dot_nn(acts[0][...], self.held[piece, :, pl.ds(off, BLOCK)])
            else:
                total = None
                for m in range(self.mats):
                    self.copy(i, m).wait()
                    part = dot_nt(acts[m][...], self.held[i * self.mats + m])
                    total = part if total is None else total + part
            store(piece, pl.ds(off, BLOCK), total)


def first_piece(t, n, make, nn, ins, mats, others, name):
    stream = Stream(mats, n, nn, 1 + len(others))
    rows = ins[0].shape[0]
    half, quarter, hidden = rows // 2, stream.quarter, stream.hidden

    def kernel(t_ref, *refs):
        parts, refs = refs[: len(ins)], refs[len(ins) :]
        weights, refs = refs[: len(mats)], refs[len(mats) :]
        halves, acts, refs = refs[:2], refs[2 : 2 + len(mats)], refs[2 + len(mats) :]
        stream.start(weights, [(t_ref[0] ^ j) * quarter for j in (3, *others)], *refs[-2:])
        make(parts, acts)

        def store(piece, cols, total):
            @pl.when(piece == 0)
            def _():
                halves[0][:, cols] = total[:half].astype(BF)
                halves[1][:, cols] = total[half:].astype(BF)

            if others:

                @pl.when(piece > 0)
                def _():
                    refs[0][piece - 1, :, cols] = total

        stream.products(acts, store)

    outs = [sds((half, quarter), BF)] * 2 + [sds((rows, hidden), BF)] * len(mats)
    return call(
        kernel,
        t,
        list(ins) + list(mats),
        outs + ([sds((len(others), rows, quarter), F32)] if others else []),
        stream.scratch,
        2 * rows * quarter * (1 + len(others)) * hidden * len(mats),
        stream.mib + 4,
        name,
        far=len(mats),
    )


def pieces(t, n, nn, acts, mats, order, name):
    stream = Stream(mats, n, nn, len(order))
    rows, quarter = acts[0].shape[0], stream.quarter

    def kernel(t_ref, *refs):
        ins, refs = refs[: len(acts)], refs[len(acts) :]
        weights, refs = refs[: len(mats)], refs[len(mats) :]
        out, scratch = refs[0], refs[1:]
        stream.start(weights, [(t_ref[0] ^ j) * quarter for j in order], *scratch)

        def store(piece, cols, total):
            out[piece, :, cols] = total

        stream.products(ins, store)

    (out,) = call(
        kernel,
        t,
        list(acts) + list(mats),
        [sds((len(order), rows, quarter), F32)],
        stream.scratch,
        2 * rows * quarter * len(order) * stream.hidden * len(mats),
        stream.mib + 4,
        name,
        far=len(mats),
    )
    return out


def add_diagonal(t, both, top, low):
    half = top.shape[0]

    def kernel(t_ref, both_ref, top_ref, low_ref, x_out, y_out):
        x_out[:half, :] = both_ref[0, :half, :].astype(BF)
        x_out[half:, :] = (both_ref[0, half:, :] + low_ref[...].astype(F32)).astype(BF)
        y_out[:half, :] = (both_ref[1, :half, :] + top_ref[...].astype(F32)).astype(BF)
        y_out[half:, :] = both_ref[1, half:, :].astype(BF)

    return call(
        kernel, t, [both, top, low], [sds(both.shape[1:], BF)] * 2, [], both.size, LIMIT, "add"
    )


def assemble(t, parts):
    rows, width = parts[0].shape

    def kernel(t_ref, *refs):
        for j, part in enumerate(refs[:-1]):
            refs[-1][:, pl.ds(pl.multiple_of((t_ref[0] ^ j) * width, 128), width)] = part[...]

    (out,) = call(
        kernel, t, parts, [sds((rows, width * len(parts)), parts[0].dtype)], [], 0, LIMIT, "assemble"
    )
    return out


def after(value, *others):
    return lax.optimization_barrier((value,) + others)[0]


def local(tokens, expert_ids, gate_values, w_gate, w_up, w_down, cotangent):
    tok_rows, depth = tokens.shape
    groups = lax.axis_size("expert")
    n = lax.axis_size("tensor")
    z = lax.axis_index("expert")
    t = lax.axis_index("tensor")
    t_arr = t.astype(jnp.int32).reshape(1)
    experts = groups
    cap = min(tok_rows, 3 * tok_rows // experts)
    quarter = depth // n
    gate_mat, up_mat, down_mat = (
        pltpu.with_memory_space_constraint(w[0], pltpu.HBM) for w in (w_gate, w_up, w_down)
    )
    hidden_here = gate_mat.shape[1]

    slot_of = slot_index(expert_ids, experts)
    order = (expert_ids ^ z) * cap + slot_of
    cells = jnp.arange(experts * cap, dtype=jnp.int32)
    pick = [order[:, k][None, :] == cells[:, None] for k in range(2)]
    spread = jnp.logical_or(pick[0], pick[1]).astype(BF)
    slot_gate = jnp.sum(
        jnp.where(pick[0], gate_values[:, 0][None, :], 0.0)
        + jnp.where(pick[1], gate_values[:, 1][None, :], 0.0),
        axis=1,
        keepdims=True,
    )

    def outgoing(source, scale):
        part = lax.dynamic_slice(source, (0, t * quarter), (tok_rows, quarter))
        out = dot_nn(spread[cap:], part)
        own = dot_nn(spread[:cap], source)
        if scale is not None:
            out, own = out * scale[cap:], own * scale[:cap]
        return own.astype(BF), out.astype(BF)

    def over_z(out):
        return [exchange(out[(k - 1) * cap : k * cap], "expert", k) for k in range(1, groups)]

    tok_own, tok_out = outgoing(tokens, None)
    cot_own, cot_out = outgoing(cotangent, slot_gate)
    tok_z = over_z(tok_out)
    first, rest = tok_z[0], tok_z[1:]
    first_far = [exchange(first, "tensor", j) for j in range(1, n)]
    gate_held = fetch(gate_mat)
    rest = jnp.concatenate(after(tuple(rest), gate_held, *first_far), axis=0)
    rest_x, rest_y = exchange(rest, "tensor", 1), exchange(rest, "tensor", 2)
    cot_z = over_z(after(cot_out, rest))
    split = rest.shape[0] // 2
    rest_d = [exchange(rest_y[:split], "tensor", 1), exchange(rest_x[split:], "tensor", 2)]
    tok_parts = [
        [first, rest], [first_far[0], rest_x], [first_far[1], rest_y], [first_far[2], *rest_d]
    ]
    cot_part = jnp.concatenate(after(tuple(cot_z), *rest_d), axis=0)
    cot_parts = [[cot_part]] + [[exchange(cot_part, "tensor", j)] for j in range(1, n)]
    pres = []
    cut = hidden_here // 2
    for start, stop, turn in (
        (0, cut, (cot_part,)),
        (cut, hidden_here, (cot_parts[1][0], cot_parts[2][0])),
    ):
        gate_o, up_o, sent = pre_acts(
            after(t_arr, *turn), tok_own, tok_parts, gate_held, up_mat, start, stop
        )
        pres += [gate_o, up_o, exchange(sent, "wide", 1)]

    def summed(arrived, keep):
        total = keep
        for piece in arrived:
            total = total + piece.astype(F32)
        return total.astype(BF)

    def to_tokens(total):
        return [total[:cap]] + [
            exchange(total[k * cap : (k + 1) * cap], "expert", k) for k in range(1, groups)
        ]

    def around(part):
        return [part] + [exchange(part, "tensor", j) for j in range(1, n)]

    gather = [(order[:, k][:, None] == cells[None, :]).astype(BF) for k in range(2)]

    d_top, d_low, hidden, both = first_piece(
        t_arr, n, hidden_strips, True, pres, [down_mat], (1, 2), "project_send"
    )
    added = [exchange(d_top, "tensor", 1), exchange(d_low, "tensor", 2)]
    grads = []
    turn = after(t_arr, both)
    for start, stop in ((0, cut), (cut, hidden_here)):
        if start:
            to_x, to_y = add_diagonal(t_arr, both, *added)
            turn = after(t_arr, to_x)
        gh_o, gh_s = grad_hiddens(turn, cot_own, cot_parts, down_mat, start, stop)
        grads += [gh_o, exchange(gh_s, "wide", 1)]
    keep = pieces(after(t_arr, gh_s), n, True, [hidden], [down_mat], (0,), "project_keep")[0]

    e_top, e_low, grad_g, grad_u = first_piece(
        after(t_arr, keep), n, grad_strips, False,
        pres + grads, [gate_mat, up_mat], (), "rows_first",
    )
    gadded = [exchange(e_top, "tensor", 1), exchange(e_low, "tensor", 2)]
    from_x, from_y = exchange(to_x, "tensor", 1), exchange(to_y, "tensor", 2)
    gboth = pieces(
        t_arr, n, False, [grad_g, grad_u], [gate_mat, up_mat], (1, 2), "rows_send",
    )
    gto_x, gto_y = add_diagonal(t_arr, gboth, *gadded)
    gkeep = pieces(
        after(t_arr, gto_x), n, False, [grad_g, grad_u], [gate_mat, up_mat], (0,), "rows_keep"
    )[0]
    gtotal = summed((exchange(gto_x, "tensor", 1), exchange(gto_y, "tensor", 2)), gkeep)
    returned = to_tokens(summed((from_x, from_y), after(keep, gto_x)))
    greturned = to_tokens(gtotal)
    returned = jnp.concatenate(after(tuple(returned), greturned[1]), axis=0)
    chosen = [dot_nn(g, returned) for g in gather]
    layer_part = (gate_values[:, 0:1] * chosen[0] + gate_values[:, 1:2] * chosen[1]).astype(BF)
    layer_parts = around(layer_part)
    layer_out = assemble(t_arr, layer_parts)
    greturned = jnp.concatenate(tuple(greturned), axis=0)
    cot_here = lax.dynamic_slice(cotangent, (0, t * quarter), (tok_rows, quarter)).astype(F32)
    gate_grad = jnp.stack([jnp.sum(cot_here * c, axis=1) for c in chosen], axis=0)
    gate_grad = after(gate_grad, layer_parts[1], layer_parts[2])
    for axis, bit in (("wide", 1), ("tensor", 1), ("tensor", 2)):
        gate_grad = gate_grad + exchange(gate_grad, axis, bit)

    grad_part = (dot_nn(gather[0], greturned) + dot_nn(gather[1], greturned)).astype(BF)
    token_grad = assemble(t_arr, around(grad_part))
    return (layer_out, token_grad, gate_grad.T)


def plain_local(tokens, expert_ids, gate_values, w_gate, w_up, w_down, cotangent):
    tok_rows, depth = tokens.shape
    groups = lax.axis_size("expert")
    experts = groups * w_gate.shape[0]
    cap = min(tok_rows, 3 * tok_rows // experts)
    total_rows = groups * cap
    gate_mat, up_mat, down_mat = w_gate[0], w_up[0], w_down[0]
    order = expert_ids * cap + slot_index(expert_ids, experts)
    cells = jnp.arange(experts * cap, dtype=jnp.int32)
    pick = [order[:, k][None, :] == cells[:, None] for k in range(2)]
    gather = [(order[:, k][:, None] == cells[None, :]).astype(BF) for k in range(2)]

    def to_owners(rows):
        out = rows.astype(BF).reshape(groups, cap, depth)
        out = lax.all_to_all(out, "expert", split_axis=0, concat_axis=0, tiled=True)
        return out.reshape(total_rows, depth)

    def send_back(rows):
        share = lax.psum_scatter(rows, "tensor", scatter_dimension=0, tiled=True).astype(BF)
        return to_owners(lax.all_gather(share, "tensor", axis=0, tiled=True))

    spread = jnp.logical_or(pick[0], pick[1]).astype(BF)
    arrived = to_owners(dot_nn(spread, tokens))
    gate_pre, up_pre = lax.psum((dot_nn(arrived, gate_mat), dot_nn(arrived, up_mat)), "wide")
    s = jax.nn.sigmoid(gate_pre)
    returned = send_back(dot_nn((gate_pre * s * up_pre).astype(BF), down_mat))
    chosen = [dot_nn(g, returned) for g in gather]
    layer_out = (gate_values[:, 0:1] * chosen[0] + gate_values[:, 1:2] * chosen[1]).astype(BF)
    upstream = cotangent.astype(F32)
    gate_grad = lax.psum(
        jnp.stack([jnp.sum(upstream * c, axis=1) for c in chosen], axis=1), "wide"
    )
    slot_gate = jnp.sum(
        jnp.where(pick[0], gate_values[:, 0][None, :], 0.0)
        + jnp.where(pick[1], gate_values[:, 1][None, :], 0.0),
        axis=1,
        keepdims=True,
    )
    grad_arrived = to_owners(dot_nn(spread, cotangent) * slot_gate)
    grad_hidden = lax.psum(dot_nt(grad_arrived, down_mat), "wide")
    grad_gate = (grad_hidden * up_pre * (s * (1.0 + gate_pre * (1.0 - s)))).astype(BF)
    grad_up = (grad_hidden * (gate_pre * s)).astype(BF)
    back = send_back(dot_nt(grad_gate, gate_mat) + dot_nt(grad_up, up_mat))
    token_grad = (dot_nn(gather[0], back) + dot_nn(gather[1], back)).astype(BF)
    return (layer_out, token_grad, gate_grad)


def solution(mesh):
    in_specs = (
        P("expert", "wide"),
        P("expert", None),
        P("expert", None),
        P("expert", "wide", "tensor"),
        P("expert", "wide", "tensor"),
        P("expert", "tensor", "wide"),
        P("expert", "wide"),
    )
    out_specs = (P("expert", "wide"), P("expert", "wide"), P("expert", None))
    laid_out = mesh.shape["tensor"] == 4 and mesh.shape["expert"] == 4 and mesh.shape["wide"] == 2
    return jax.shard_map(
        local if laid_out else plain_local,
        mesh=mesh,
        in_specs=in_specs,
        out_specs=out_specs,
        check_vma=False,
    )
```

```python
import jax
import jax.numpy as jnp
from jax import lax
from jax.experimental import pallas as pl
from jax.experimental.pallas import tpu as pltpu
from jax.sharding import PartitionSpec as P

BF = jnp.bfloat16
F32 = jnp.float32
MIB = 1024 * 1024


def slot_index(expert_ids, experts):
    hit_table = (expert_ids[:, :, None] == jnp.arange(experts, dtype=jnp.int32)).astype(jnp.int32)
    per_row = jnp.sum(hit_table, axis=1)
    before = jnp.cumsum(per_row, axis=0) - per_row
    return jnp.sum(hit_table * before[:, None, :], axis=2)


def exchange(array, axis, bit):
    size = lax.axis_size(axis)
    return lax.ppermute(array, axis, [(i, i ^ bit) for i in range(size)])


def dot_nn(a, b):
    return jnp.dot(a, b, preferred_element_type=F32)


def dot_nt(a, b):
    return lax.dot_general(a, b, (((1,), (1,)), ((), ())), preferred_element_type=F32)


def params(mib):
    return pltpu.CompilerParams(vmem_limit_bytes=mib * MIB)


VMEM = pl.BlockSpec(memory_space=pltpu.VMEM)
HBM = pl.BlockSpec(memory_space=pltpu.HBM)
SMEM = pl.BlockSpec(memory_space=pltpu.SMEM)


def sds(shape, dtype):
    return jax.ShapeDtypeStruct(shape, dtype)


def call(kernel, t, ins, outs, scratch, flops, mib, name, far=0):
    return pl.pallas_call(
        kernel,
        in_specs=[SMEM] + [VMEM] * (len(ins) - far) + [HBM] * far,
        out_specs=[VMEM] * len(outs),
        out_shape=outs,
        scratch_shapes=scratch,
        compiler_params=params(mib),
        cost_estimate=pl.CostEstimate(flops=flops // 2, bytes_accessed=MIB, transcendentals=0),
        name=name,
    )(t, *ins)


def fetch(matrix):
    def kernel(source, held, sem):
        copy = pltpu.make_async_copy(source, held, sem)
        copy.start()
        copy.wait()

    return pl.pallas_call(
        kernel,
        in_specs=[HBM],
        out_specs=VMEM,
        out_shape=pltpu.VMEM(matrix.shape, matrix.dtype),
        scratch_shapes=[pltpu.SemaphoreType.DMA],
        compiler_params=params(LIMIT),
        cost_estimate=pl.CostEstimate(
            flops=0, bytes_accessed=2 * matrix.size, transcendentals=0
        ),
        name="fetch",
    )(matrix)


def lay_out(t, own, parts, rows_ref):
    cap = own.shape[0]
    n, _, quarter = rows_ref.shape
    for q in range(n):
        rows_ref[q, :cap, :] = own[:, q * quarter : (q + 1) * quarter]
    for j in range(n):
        at = cap
        for piece in parts[j]:
            rows_ref[t ^ j, at : at + piece.shape[0], :] = piece[...]
            at += piece.shape[0]


def split_parts(refs, counts):
    parts, at = [], 0
    for c in counts:
        parts.append(refs[at : at + c])
        at += c
    return parts, refs[at:]


BLOCK = 256


def pre_acts(t, own, parts, gate_held, up_mat, start, stop):
    depth = up_mat.shape[0]
    n = len(parts)
    quarter = depth // n
    rows = own.shape[0] + sum(p.shape[0] for p in parts[0])
    counts = [len(p) for p in parts]
    width = stop - start

    def kernel(t_ref, own_ref, *refs):
        pieces, refs = split_parts(refs, counts)
        gate_w, up_w, gate_o, up_o, send, rows_ref, up_held, sem = refs
        copy = pltpu.make_async_copy(up_w.at[:, pl.ds(start, width)], up_held, sem)
        copy.start()
        lay_out(t_ref[0], own_ref, pieces, rows_ref)
        for w, base, out, at in ((gate_w, start, gate_o, 0), (up_held, 0, up_o, width)):
            if at:
                copy.wait()

            @pl.loop(0, width // BLOCK)
            def _(i):
                off = pl.multiple_of(i * BLOCK, BLOCK)
                total = None
                for q in range(n):
                    part = dot_nn(
                        rows_ref[q], w[q * quarter : (q + 1) * quarter, pl.ds(base + off, BLOCK)]
                    )
                    total = part if total is None else total + part
                out[:, pl.ds(off, BLOCK)] = total
                send[:, pl.ds(at + off, BLOCK)] = total.astype(BF)

    shape = (rows, width)
    return call(
        kernel,
        t,
        [own] + [x for p in parts for x in p] + [gate_held, up_mat],
        [sds(shape, F32)] * 2 + [sds((rows, 2 * width), BF)],
        [
            pltpu.VMEM((n, rows, quarter), BF),
            pltpu.VMEM((depth, width), BF),
            pltpu.SemaphoreType.DMA,
        ],
        4 * rows * depth * width,
        14,
        "pre_acts",
        far=1,
    )


def grad_hiddens(t, own, parts, down_mat, start, stop):
    depth = down_mat.shape[1]
    n = len(parts)
    quarter = depth // n
    rows = own.shape[0] + sum(p.shape[0] for p in parts[0])
    counts = [len(p) for p in parts]

    steps = (stop - start) // BLOCK

    def kernel(t_ref, own_ref, *refs):
        pieces, refs = split_parts(refs, counts)
        down_w, out, send, rows_ref, held, sems = refs

        def copy(i):
            source = down_w.at[pl.ds(start + i * BLOCK, BLOCK)]
            return pltpu.make_async_copy(source, held.at[i], sems.at[i])

        for i in range(steps):
            copy(i).start()
        lay_out(t_ref[0], own_ref, pieces, rows_ref)

        @pl.loop(0, steps)
        def _(i):
            copy(i).wait()
            total = None
            for q in range(n):
                part = dot_nt(rows_ref[q], held[i, :, q * quarter : (q + 1) * quarter])
                total = part if total is None else total + part
            off = pl.multiple_of(i * BLOCK, BLOCK)
            out[:, pl.ds(off, BLOCK)] = total
            send[:, pl.ds(off, BLOCK)] = total.astype(BF)

    shape = (rows, stop - start)
    return call(
        kernel,
        t,
        [own] + [x for p in parts for x in p] + [down_mat],
        [sds(shape, F32), sds(shape, BF)],
        [
            pltpu.VMEM((n, rows, quarter), BF),
            pltpu.VMEM((steps, BLOCK, depth), BF),
            pltpu.SemaphoreType.DMA((steps,)),
        ],
        2 * rows * depth * (stop - start),
        12,
        "grad_hidden",
        far=1,
    )


STRIP = 16
LIMIT = 8


def strips(rows, body):
    @pl.loop(0, rows // STRIP)
    def _(i):
        body(pl.ds(pl.multiple_of(i * STRIP, STRIP), STRIP))


def hidden_strips(ins, acts):
    (hidden_ref,) = acts

    def body(here):
        at = 0
        for g in range(0, len(ins), 3):
            gate_o, up_o, both_r = ins[g : g + 3]
            width = gate_o.shape[1]
            cols = slice(at, at + width)
            gate = gate_o[here, :] + both_r[here, :width].astype(F32)
            up = up_o[here, :] + both_r[here, width:].astype(F32)
            hidden_ref[here, cols] = (gate * jax.nn.sigmoid(gate) * up).astype(BF)
            at += gate_o.shape[1]

    strips(hidden_ref.shape[0], body)


def grad_strips(ins, acts):
    gg_ref, gu_ref = acts

    def body(here):
        at = 0
        for g in range(0, len(ins), 5):
            gate_o, up_o, both_r, gh_o, gh_r = ins[g : g + 5]
            width = gate_o.shape[1]
            cols = slice(at, at + width)
            gate = gate_o[here, :] + both_r[here, :width].astype(F32)
            up = up_o[here, :] + both_r[here, width:].astype(F32)
            grad = gh_o[here, :] + gh_r[here, :].astype(F32)
            s = jax.nn.sigmoid(gate)
            gg_ref[here, cols] = (grad * up * (s * (1.0 + gate * (1.0 - s)))).astype(BF)
            gu_ref[here, cols] = (grad * (gate * s)).astype(BF)
            at += gate_o.shape[1]

    strips(gg_ref.shape[0], body)


class Stream:
    def __init__(self, mats, n, nn, pieces):
        self.mats, self.nn = len(mats), nn
        self.hidden, depth = mats[0].shape if nn else mats[0].shape[::-1]
        self.quarter = depth // n
        self.blocks = self.quarter // BLOCK
        self.each = 1 if nn else self.blocks
        chunk = (self.hidden, self.quarter) if nn else (BLOCK, self.hidden)
        self.count = pieces * self.each
        total = self.count * self.mats
        self.scratch = [pltpu.VMEM((total,) + chunk, BF), pltpu.SemaphoreType.DMA((total,))]
        self.mib = 2 + 2 * pieces * self.mats * self.hidden * self.quarter // MIB

    def copy(self, chunk, m):
        base = self.bases[0]
        for k in range(1, len(self.bases)):
            base = jnp.where(chunk >= k * self.each, self.bases[k], base)
        width = self.quarter if self.nn else BLOCK
        cut = pl.ds(pl.multiple_of(base + chunk % self.each * width, BLOCK), width)
        source = self.weights[m].at[:, cut] if self.nn else self.weights[m].at[cut]
        slot = chunk * self.mats + m
        return pltpu.make_async_copy(source, self.held.at[slot], self.sems.at[slot])

    def start(self, weights, bases, held, sems):
        self.weights, self.bases, self.held, self.sems = weights, bases, held, sems
        for chunk in range(self.count):
            for m in range(self.mats):
                self.copy(chunk, m).start()

    def products(self, acts, store):
        @pl.loop(0, len(self.bases) * self.blocks)
        def _(i):
            piece, off = i // self.blocks, pl.multiple_of(i % self.blocks * BLOCK, BLOCK)
            if self.nn:

                @pl.when(off == 0)
                def _():
                    self.copy(piece, 0).wait()

                total = dot_nn(acts[0][...], self.held[piece, :, pl.ds(off, BLOCK)])
            else:
                total = None
                for m in range(self.mats):
                    self.copy(i, m).wait()
                    part = dot_nt(acts[m][...], self.held[i * self.mats + m])
                    total = part if total is None else total + part
            store(piece, pl.ds(off, BLOCK), total)


def first_piece(t, n, make, nn, ins, mats, name):
    stream = Stream(mats, n, nn, 1)
    rows = ins[0].shape[0]
    half, quarter, hidden = rows // 2, stream.quarter, stream.hidden

    def kernel(t_ref, *refs):
        parts, refs = refs[: len(ins)], refs[len(ins) :]
        weights, refs = refs[: len(mats)], refs[len(mats) :]
        halves, acts, scratch = refs[:2], refs[2 : 2 + len(mats)], refs[2 + len(mats) :]
        stream.start(weights, [(t_ref[0] ^ 3) * quarter], *scratch)
        make(parts, acts)

        def store(piece, cols, total):
            halves[0][:, cols] = total[:half].astype(BF)
            halves[1][:, cols] = total[half:].astype(BF)

        stream.products(acts, store)

    return call(
        kernel,
        t,
        list(ins) + list(mats),
        [sds((half, quarter), BF)] * 2 + [sds((rows, hidden), BF)] * len(mats),
        stream.scratch,
        2 * rows * quarter * hidden * len(mats),
        stream.mib + 4,
        name,
        far=len(mats),
    )


def pieces(t, n, nn, acts, mats, order, name):
    stream = Stream(mats, n, nn, len(order))
    rows, quarter = acts[0].shape[0], stream.quarter

    def kernel(t_ref, *refs):
        ins, refs = refs[: len(acts)], refs[len(acts) :]
        weights, refs = refs[: len(mats)], refs[len(mats) :]
        out, scratch = refs[0], refs[1:]
        stream.start(weights, [(t_ref[0] ^ j) * quarter for j in order], *scratch)

        def store(piece, cols, total):
            out[piece, :, cols] = total

        stream.products(ins, store)

    (out,) = call(
        kernel,
        t,
        list(acts) + list(mats),
        [sds((len(order), rows, quarter), F32)],
        stream.scratch,
        2 * rows * quarter * len(order) * stream.hidden * len(mats),
        stream.mib + 4,
        name,
        far=len(mats),
    )
    return out


def add_diagonal(t, both, top, low):
    half = top.shape[0]

    def kernel(t_ref, both_ref, top_ref, low_ref, x_out, y_out):
        x_out[:half, :] = both_ref[0, :half, :].astype(BF)
        x_out[half:, :] = (both_ref[0, half:, :] + low_ref[...].astype(F32)).astype(BF)
        y_out[:half, :] = (both_ref[1, :half, :] + top_ref[...].astype(F32)).astype(BF)
        y_out[half:, :] = both_ref[1, half:, :].astype(BF)

    return call(
        kernel, t, [both, top, low], [sds(both.shape[1:], BF)] * 2, [], both.size, LIMIT, "add"
    )


def assemble(t, parts):
    rows, width = parts[0].shape

    def kernel(t_ref, *refs):
        for j, part in enumerate(refs[:-1]):
            refs[-1][:, pl.ds(pl.multiple_of((t_ref[0] ^ j) * width, 128), width)] = part[...]

    (out,) = call(
        kernel, t, parts, [sds((rows, width * len(parts)), parts[0].dtype)], [], 0, LIMIT, "assemble"
    )
    return out


def after(value, *others):
    return lax.optimization_barrier((value,) + others)[0]


def local(tokens, expert_ids, gate_values, w_gate, w_up, w_down, cotangent):
    tok_rows, depth = tokens.shape
    groups = lax.axis_size("expert")
    n = lax.axis_size("tensor")
    z = lax.axis_index("expert")
    t = lax.axis_index("tensor")
    t_arr = t.astype(jnp.int32).reshape(1)
    experts = groups
    cap = min(tok_rows, 3 * tok_rows // experts)
    quarter = depth // n
    gate_mat, up_mat, down_mat = (
        pltpu.with_memory_space_constraint(w[0], pltpu.HBM) for w in (w_gate, w_up, w_down)
    )
    hidden_here = gate_mat.shape[1]

    slot_of = slot_index(expert_ids, experts)
    order = (expert_ids ^ z) * cap + slot_of
    cells = jnp.arange(experts * cap, dtype=jnp.int32)
    pick = [order[:, k][None, :] == cells[:, None] for k in range(2)]
    spread = jnp.logical_or(pick[0], pick[1]).astype(BF)
    slot_gate = jnp.sum(
        jnp.where(pick[0], gate_values[:, 0][None, :], 0.0)
        + jnp.where(pick[1], gate_values[:, 1][None, :], 0.0),
        axis=1,
        keepdims=True,
    )

    def outgoing(source, scale):
        part = lax.dynamic_slice(source, (0, t * quarter), (tok_rows, quarter))
        out = dot_nn(spread[cap:], part)
        own = dot_nn(spread[:cap], source)
        if scale is not None:
            out, own = out * scale[cap:], own * scale[:cap]
        return own.astype(BF), out.astype(BF)

    def over_z(out):
        return [exchange(out[(k - 1) * cap : k * cap], "expert", k) for k in range(1, groups)]

    tok_own, tok_out = outgoing(tokens, None)
    cot_own, cot_out = outgoing(cotangent, slot_gate)
    tok_z = over_z(tok_out)
    first, rest = tok_z[0], tok_z[1:]
    first_far = [exchange(first, "tensor", j) for j in range(1, n)]
    gate_held = fetch(gate_mat)
    rest = jnp.concatenate(after(tuple(rest), gate_held, *first_far), axis=0)
    rest_x, rest_y = exchange(rest, "tensor", 1), exchange(rest, "tensor", 2)
    cot_z = over_z(after(cot_out, rest))
    split = rest.shape[0] // 2
    rest_d = [exchange(rest_y[:split], "tensor", 1), exchange(rest_x[split:], "tensor", 2)]
    tok_parts = [
        [first, rest], [first_far[0], rest_x], [first_far[1], rest_y], [first_far[2], *rest_d]
    ]
    cot_part = jnp.concatenate(after(tuple(cot_z), *rest_d), axis=0)
    cot_parts = [[cot_part]] + [[exchange(cot_part, "tensor", j)] for j in range(1, n)]
    pres = []
    half = hidden_here // 2
    for start, turn in ((0, (cot_part,)), (half, (cot_parts[1][0], cot_parts[2][0]))):
        gate_o, up_o, sent = pre_acts(
            after(t_arr, *turn), tok_own, tok_parts, gate_held, up_mat, start, start + half
        )
        pres.append([gate_o, up_o, exchange(sent, "wide", 1)])

    def summed(arrived, keep):
        total = keep
        for piece in arrived:
            total = total + piece.astype(F32)
        return total.astype(BF)

    def to_tokens(total):
        return [total[:cap]] + [
            exchange(total[k * cap : (k + 1) * cap], "expert", k) for k in range(1, groups)
        ]

    def around(part):
        return [part] + [exchange(part, "tensor", j) for j in range(1, n)]

    gather = [(order[:, k][:, None] == cells[None, :]).astype(BF) for k in range(2)]

    d_top, d_low, hidden = first_piece(
        t_arr, n, hidden_strips, True, sum(pres, []), [down_mat], "project_first"
    )
    added = [exchange(d_top, "tensor", 1), exchange(d_low, "tensor", 2)]
    both = pieces(t_arr, n, True, [hidden], [down_mat], (1, 2), "project_send")
    grads = []
    turn = after(t_arr, both)
    for start in range(0, hidden_here, hidden_here // 2):
        if start:
            to_x, to_y = add_diagonal(t_arr, both, *added)
            turn = after(t_arr, to_x)
        gh_o, gh_s = grad_hiddens(
            turn, cot_own, cot_parts, down_mat, start, start + hidden_here // 2
        )
        grads.append([gh_o, exchange(gh_s, "wide", 1)])
    keep = pieces(after(t_arr, gh_s), n, True, [hidden], [down_mat], (0,), "project_keep")[0]

    e_top, e_low, grad_g, grad_u = first_piece(
        after(t_arr, keep), n, grad_strips, False,
        sum([p + g for p, g in zip(pres, grads)], []), [gate_mat, up_mat], "rows_first",
    )
    gadded = [exchange(e_top, "tensor", 1), exchange(e_low, "tensor", 2)]
    from_x, from_y = exchange(to_x, "tensor", 1), exchange(to_y, "tensor", 2)
    gboth = pieces(
        t_arr, n, False, [grad_g, grad_u], [gate_mat, up_mat], (1, 2), "rows_send",
    )
    gto_x, gto_y = add_diagonal(t_arr, gboth, *gadded)
    gkeep = pieces(
        after(t_arr, gto_x), n, False, [grad_g, grad_u], [gate_mat, up_mat], (0,), "rows_keep"
    )[0]
    gtotal = summed((exchange(gto_x, "tensor", 1), exchange(gto_y, "tensor", 2)), gkeep)
    returned = to_tokens(summed((from_x, from_y), after(keep, gto_x)))
    greturned = to_tokens(gtotal)
    returned = jnp.concatenate(after(tuple(returned), greturned[1]), axis=0)
    chosen = [dot_nn(g, returned) for g in gather]
    layer_part = (gate_values[:, 0:1] * chosen[0] + gate_values[:, 1:2] * chosen[1]).astype(BF)
    layer_parts = around(layer_part)
    layer_out = assemble(t_arr, layer_parts)
    greturned = jnp.concatenate(tuple(greturned), axis=0)
    cot_here = lax.dynamic_slice(cotangent, (0, t * quarter), (tok_rows, quarter)).astype(F32)
    gate_grad = jnp.stack([jnp.sum(cot_here * c, axis=1) for c in chosen], axis=0)
    gate_grad = after(gate_grad, layer_parts[1], layer_parts[2])
    for axis, bit in (("wide", 1), ("tensor", 1), ("tensor", 2)):
        gate_grad = gate_grad + exchange(gate_grad, axis, bit)

    grad_part = (dot_nn(gather[0], greturned) + dot_nn(gather[1], greturned)).astype(BF)
    token_grad = assemble(t_arr, around(grad_part))
    return (layer_out, token_grad, gate_grad.T)


def plain_local(tokens, expert_ids, gate_values, w_gate, w_up, w_down, cotangent):
    tok_rows, depth = tokens.shape
    groups = lax.axis_size("expert")
    experts = groups * w_gate.shape[0]
    cap = min(tok_rows, 3 * tok_rows // experts)
    total_rows = groups * cap
    gate_mat, up_mat, down_mat = w_gate[0], w_up[0], w_down[0]
    order = expert_ids * cap + slot_index(expert_ids, experts)
    cells = jnp.arange(experts * cap, dtype=jnp.int32)
    pick = [order[:, k][None, :] == cells[:, None] for k in range(2)]
    gather = [(order[:, k][:, None] == cells[None, :]).astype(BF) for k in range(2)]

    def to_owners(rows):
        out = rows.astype(BF).reshape(groups, cap, depth)
        out = lax.all_to_all(out, "expert", split_axis=0, concat_axis=0, tiled=True)
        return out.reshape(total_rows, depth)

    def send_back(rows):
        share = lax.psum_scatter(rows, "tensor", scatter_dimension=0, tiled=True).astype(BF)
        return to_owners(lax.all_gather(share, "tensor", axis=0, tiled=True))

    spread = jnp.logical_or(pick[0], pick[1]).astype(BF)
    arrived = to_owners(dot_nn(spread, tokens))
    gate_pre, up_pre = lax.psum((dot_nn(arrived, gate_mat), dot_nn(arrived, up_mat)), "wide")
    s = jax.nn.sigmoid(gate_pre)
    returned = send_back(dot_nn((gate_pre * s * up_pre).astype(BF), down_mat))
    chosen = [dot_nn(g, returned) for g in gather]
    layer_out = (gate_values[:, 0:1] * chosen[0] + gate_values[:, 1:2] * chosen[1]).astype(BF)
    upstream = cotangent.astype(F32)
    gate_grad = lax.psum(
        jnp.stack([jnp.sum(upstream * c, axis=1) for c in chosen], axis=1), "wide"
    )
    slot_gate = jnp.sum(
        jnp.where(pick[0], gate_values[:, 0][None, :], 0.0)
        + jnp.where(pick[1], gate_values[:, 1][None, :], 0.0),
        axis=1,
        keepdims=True,
    )
    grad_arrived = to_owners(dot_nn(spread, cotangent) * slot_gate)
    grad_hidden = lax.psum(dot_nt(grad_arrived, down_mat), "wide")
    grad_gate = (grad_hidden * up_pre * (s * (1.0 + gate_pre * (1.0 - s)))).astype(BF)
    grad_up = (grad_hidden * (gate_pre * s)).astype(BF)
    back = send_back(dot_nt(grad_gate, gate_mat) + dot_nt(grad_up, up_mat))
    token_grad = (dot_nn(gather[0], back) + dot_nn(gather[1], back)).astype(BF)
    return (layer_out, token_grad, gate_grad)


def solution(mesh):
    in_specs = (
        P("expert", "wide"),
        P("expert", None),
        P("expert", None),
        P("expert", "wide", "tensor"),
        P("expert", "wide", "tensor"),
        P("expert", "tensor", "wide"),
        P("expert", "wide"),
    )
    out_specs = (P("expert", "wide"), P("expert", "wide"), P("expert", None))
    laid_out = mesh.shape["tensor"] == 4 and mesh.shape["expert"] == 4 and mesh.shape["wide"] == 2
    return jax.shard_map(
        local if laid_out else plain_local,
        mesh=mesh,
        in_specs=in_specs,
        out_specs=out_specs,
        check_vma=False,
    )
```

```python
import jax
import jax.numpy as jnp
from jax import lax
from jax.experimental import pallas as pl
from jax.experimental.pallas import tpu as pltpu
from jax.sharding import PartitionSpec as P

BF = jnp.bfloat16
F32 = jnp.float32
MIB = 1024 * 1024


def slot_index(expert_ids, experts):
    hit_table = (expert_ids[:, :, None] == jnp.arange(experts, dtype=jnp.int32)).astype(jnp.int32)
    per_row = jnp.sum(hit_table, axis=1)
    before = jnp.cumsum(per_row, axis=0) - per_row
    return jnp.sum(hit_table * before[:, None, :], axis=2)


def exchange(array, axis, bit):
    size = lax.axis_size(axis)
    return lax.ppermute(array, axis, [(i, i ^ bit) for i in range(size)])


def dot_nn(a, b):
    return jnp.dot(a, b, preferred_element_type=F32)


def dot_nt(a, b):
    return lax.dot_general(a, b, (((1,), (1,)), ((), ())), preferred_element_type=F32)


def params(mib):
    return pltpu.CompilerParams(vmem_limit_bytes=mib * MIB)


VMEM = pl.BlockSpec(memory_space=pltpu.VMEM)
HBM = pl.BlockSpec(memory_space=pltpu.HBM)
SMEM = pl.BlockSpec(memory_space=pltpu.SMEM)


def sds(shape, dtype):
    return jax.ShapeDtypeStruct(shape, dtype)


def call(kernel, t, ins, outs, scratch, flops, mib, name, far=0):
    return pl.pallas_call(
        kernel,
        in_specs=[SMEM] + [VMEM] * (len(ins) - far) + [HBM] * far,
        out_specs=[VMEM] * len(outs),
        out_shape=outs,
        scratch_shapes=scratch,
        compiler_params=params(mib),
        cost_estimate=pl.CostEstimate(flops=flops // 2, bytes_accessed=MIB, transcendentals=0),
        name=name,
    )(t, *ins)


def fetch(matrix):
    def kernel(source, held, sem):
        copy = pltpu.make_async_copy(source, held, sem)
        copy.start()
        copy.wait()

    return pl.pallas_call(
        kernel,
        in_specs=[HBM],
        out_specs=VMEM,
        out_shape=pltpu.VMEM(matrix.shape, matrix.dtype),
        scratch_shapes=[pltpu.SemaphoreType.DMA],
        compiler_params=params(LIMIT),
        cost_estimate=pl.CostEstimate(
            flops=0, bytes_accessed=2 * matrix.size, transcendentals=0
        ),
        name="fetch",
    )(matrix)


def lay_out(t, own, parts, rows_ref):
    cap = own.shape[0]
    n, _, quarter = rows_ref.shape
    for q in range(n):
        rows_ref[q, :cap, :] = own[:, q * quarter : (q + 1) * quarter]
    for j in range(n):
        at = cap
        for piece in parts[j]:
            rows_ref[t ^ j, at : at + piece.shape[0], :] = piece[...]
            at += piece.shape[0]


def split_parts(refs, counts):
    parts, at = [], 0
    for c in counts:
        parts.append(refs[at : at + c])
        at += c
    return parts, refs[at:]


BLOCK = 256


def pre_acts(t, own, parts, gate_held, up_mat, start, stop):
    depth = up_mat.shape[0]
    n = len(parts)
    quarter = depth // n
    rows = own.shape[0] + sum(p.shape[0] for p in parts[0])
    counts = [len(p) for p in parts]
    width = stop - start

    def kernel(t_ref, own_ref, *refs):
        pieces, refs = split_parts(refs, counts)
        gate_w, up_w, gate_o, up_o, send, rows_ref, up_held, sem = refs
        copy = pltpu.make_async_copy(up_w.at[:, pl.ds(start, width)], up_held, sem)
        copy.start()
        lay_out(t_ref[0], own_ref, pieces, rows_ref)
        for w, base, out, at in ((gate_w, start, gate_o, 0), (up_held, 0, up_o, width)):
            if at:
                copy.wait()

            @pl.loop(0, width // BLOCK)
            def _(i):
                off = pl.multiple_of(i * BLOCK, BLOCK)
                total = None
                for q in range(n):
                    part = dot_nn(
                        rows_ref[q], w[q * quarter : (q + 1) * quarter, pl.ds(base + off, BLOCK)]
                    )
                    total = part if total is None else total + part
                out[:, pl.ds(off, BLOCK)] = total
                send[:, pl.ds(at + off, BLOCK)] = total.astype(BF)

    shape = (rows, width)
    return call(
        kernel,
        t,
        [own] + [x for p in parts for x in p] + [gate_held, up_mat],
        [sds(shape, F32)] * 2 + [sds((rows, 2 * width), BF)],
        [
            pltpu.VMEM((n, rows, quarter), BF),
            pltpu.VMEM((depth, width), BF),
            pltpu.SemaphoreType.DMA,
        ],
        4 * rows * depth * width,
        14,
        "pre_acts",
        far=1,
    )


def grad_hiddens(t, own, parts, down_mat, start, stop):
    depth = down_mat.shape[1]
    n = len(parts)
    quarter = depth // n
    rows = own.shape[0] + sum(p.shape[0] for p in parts[0])
    counts = [len(p) for p in parts]

    steps = (stop - start) // BLOCK

    def kernel(t_ref, own_ref, *refs):
        pieces, refs = split_parts(refs, counts)
        down_w, out, send, rows_ref, held, sems = refs

        def copy(i):
            source = down_w.at[pl.ds(start + i * BLOCK, BLOCK)]
            return pltpu.make_async_copy(source, held.at[i], sems.at[i])

        for i in range(steps):
            copy(i).start()
        lay_out(t_ref[0], own_ref, pieces, rows_ref)

        @pl.loop(0, steps)
        def _(i):
            copy(i).wait()
            total = None
            for q in range(n):
                part = dot_nt(rows_ref[q], held[i, :, q * quarter : (q + 1) * quarter])
                total = part if total is None else total + part
            off = pl.multiple_of(i * BLOCK, BLOCK)
            out[:, pl.ds(off, BLOCK)] = total
            send[:, pl.ds(off, BLOCK)] = total.astype(BF)

    shape = (rows, stop - start)
    return call(
        kernel,
        t,
        [own] + [x for p in parts for x in p] + [down_mat],
        [sds(shape, F32), sds(shape, BF)],
        [
            pltpu.VMEM((n, rows, quarter), BF),
            pltpu.VMEM((steps, BLOCK, depth), BF),
            pltpu.SemaphoreType.DMA((steps,)),
        ],
        4 * rows * depth * (stop - start),
        18,
        "grad_hidden",
        far=1,
    )


STRIP = 16
LIMIT = 8


def strips(rows, body):
    @pl.loop(0, rows // STRIP)
    def _(i):
        body(pl.ds(pl.multiple_of(i * STRIP, STRIP), STRIP))


def hidden_strips(ins, acts):
    (hidden_ref,) = acts

    def body(here):
        at = 0
        for g in range(0, len(ins), 3):
            gate_o, up_o, both_r = ins[g : g + 3]
            width = gate_o.shape[1]
            cols = slice(at, at + width)
            gate = gate_o[here, :] + both_r[here, :width].astype(F32)
            up = up_o[here, :] + both_r[here, width:].astype(F32)
            hidden_ref[here, cols] = (gate * jax.nn.sigmoid(gate) * up).astype(BF)
            at += gate_o.shape[1]

    strips(hidden_ref.shape[0], body)


def grad_strips(ins, acts):
    gg_ref, gu_ref = acts
    share = len(ins) // 5
    ins, grads = ins[: 3 * share], ins[3 * share :]

    def body(here):
        at = 0
        for g in range(share):
            gate_o, up_o, both_r = ins[3 * g : 3 * g + 3]
            gh_o, gh_r = grads[2 * g : 2 * g + 2]
            width = gate_o.shape[1]
            cols = slice(at, at + width)
            gate = gate_o[here, :] + both_r[here, :width].astype(F32)
            up = up_o[here, :] + both_r[here, width:].astype(F32)
            grad = gh_o[here, :] + gh_r[here, :].astype(F32)
            s = jax.nn.sigmoid(gate)
            gg_ref[here, cols] = (grad * up * (s * (1.0 + gate * (1.0 - s)))).astype(BF)
            gu_ref[here, cols] = (grad * (gate * s)).astype(BF)
            at += width

    strips(gg_ref.shape[0], body)


class Stream:
    def __init__(self, mats, n, nn, pieces):
        self.mats, self.nn = len(mats), nn
        self.hidden, depth = mats[0].shape if nn else mats[0].shape[::-1]
        self.quarter = depth // n
        self.blocks = self.quarter // BLOCK
        self.each = 1 if nn else self.blocks
        chunk = (self.hidden, self.quarter) if nn else (BLOCK, self.hidden)
        self.count = pieces * self.each
        total = self.count * self.mats
        self.scratch = [pltpu.VMEM((total,) + chunk, BF), pltpu.SemaphoreType.DMA((total,))]
        self.mib = 2 + 2 * pieces * self.mats * self.hidden * self.quarter // MIB

    def copy(self, chunk, m):
        base = self.bases[0]
        for k in range(1, len(self.bases)):
            base = jnp.where(chunk >= k * self.each, self.bases[k], base)
        width = self.quarter if self.nn else BLOCK
        cut = pl.ds(pl.multiple_of(base + chunk % self.each * width, BLOCK), width)
        source = self.weights[m].at[:, cut] if self.nn else self.weights[m].at[cut]
        slot = chunk * self.mats + m
        return pltpu.make_async_copy(source, self.held.at[slot], self.sems.at[slot])

    def start(self, weights, bases, held, sems):
        self.weights, self.bases, self.held, self.sems = weights, bases, held, sems
        for chunk in range(self.count):
            for m in range(self.mats):
                self.copy(chunk, m).start()

    def products(self, acts, store):
        @pl.loop(0, len(self.bases) * self.blocks)
        def _(i):
            piece, off = i // self.blocks, pl.multiple_of(i % self.blocks * BLOCK, BLOCK)
            if self.nn:

                @pl.when(off == 0)
                def _():
                    self.copy(piece, 0).wait()

                total = dot_nn(acts[0][...], self.held[piece, :, pl.ds(off, BLOCK)])
            else:
                total = None
                for m in range(self.mats):
                    self.copy(i, m).wait()
                    part = dot_nt(acts[m][...], self.held[i * self.mats + m])
                    total = part if total is None else total + part
            store(piece, pl.ds(off, BLOCK), total)


def first_piece(t, n, make, nn, ins, mats, others, name):
    stream = Stream(mats, n, nn, 1 + len(others))
    rows = ins[0].shape[0]
    half, quarter, hidden = rows // 2, stream.quarter, stream.hidden

    def kernel(t_ref, *refs):
        parts, refs = refs[: len(ins)], refs[len(ins) :]
        weights, refs = refs[: len(mats)], refs[len(mats) :]
        halves, acts, refs = refs[:2], refs[2 : 2 + len(mats)], refs[2 + len(mats) :]
        stream.start(weights, [(t_ref[0] ^ j) * quarter for j in (3, *others)], *refs[-2:])
        make(parts, acts)

        def store(piece, cols, total):
            @pl.when(piece == 0)
            def _():
                halves[0][:, cols] = total[:half].astype(BF)
                halves[1][:, cols] = total[half:].astype(BF)

            if others:

                @pl.when(piece > 0)
                def _():
                    refs[0][piece - 1, :, cols] = total

        stream.products(acts, store)

    outs = [sds((half, quarter), BF)] * 2 + [sds((rows, hidden), BF)] * len(mats)
    return call(
        kernel,
        t,
        list(ins) + list(mats),
        outs + ([sds((len(others), rows, quarter), F32)] if others else []),
        stream.scratch,
        2 * rows * quarter * (1 + len(others)) * hidden * len(mats),
        stream.mib + 4,
        name,
        far=len(mats),
    )


def pieces(t, n, nn, acts, mats, order, name):
    stream = Stream(mats, n, nn, len(order))
    rows, quarter = acts[0].shape[0], stream.quarter

    def kernel(t_ref, *refs):
        ins, refs = refs[: len(acts)], refs[len(acts) :]
        weights, refs = refs[: len(mats)], refs[len(mats) :]
        out, scratch = refs[0], refs[1:]
        stream.start(weights, [(t_ref[0] ^ j) * quarter for j in order], *scratch)

        def store(piece, cols, total):
            out[piece, :, cols] = total

        stream.products(ins, store)

    (out,) = call(
        kernel,
        t,
        list(acts) + list(mats),
        [sds((len(order), rows, quarter), F32)],
        stream.scratch,
        2 * rows * quarter * len(order) * stream.hidden * len(mats),
        stream.mib + 4,
        name,
        far=len(mats),
    )
    return out


def add_diagonal(t, both, top, low):
    half = top.shape[0]

    def kernel(t_ref, both_ref, top_ref, low_ref, x_out, y_out):
        x_out[:half, :] = both_ref[0, :half, :].astype(BF)
        x_out[half:, :] = (both_ref[0, half:, :] + low_ref[...].astype(F32)).astype(BF)
        y_out[:half, :] = (both_ref[1, :half, :] + top_ref[...].astype(F32)).astype(BF)
        y_out[half:, :] = both_ref[1, half:, :].astype(BF)

    return call(
        kernel, t, [both, top, low], [sds(both.shape[1:], BF)] * 2, [], both.size, LIMIT, "add"
    )


def assemble(t, parts):
    rows, width = parts[0].shape

    def kernel(t_ref, *refs):
        for j, part in enumerate(refs[:-1]):
            refs[-1][:, pl.ds(pl.multiple_of((t_ref[0] ^ j) * width, 128), width)] = part[...]

    (out,) = call(
        kernel, t, parts, [sds((rows, width * len(parts)), parts[0].dtype)], [], 0, LIMIT, "assemble"
    )
    return out


def after(value, *others):
    return lax.optimization_barrier((value,) + others)[0]


def local(tokens, expert_ids, gate_values, w_gate, w_up, w_down, cotangent):
    tok_rows, depth = tokens.shape
    groups = lax.axis_size("expert")
    n = lax.axis_size("tensor")
    z = lax.axis_index("expert")
    t = lax.axis_index("tensor")
    t_arr = t.astype(jnp.int32).reshape(1)
    experts = groups
    cap = min(tok_rows, 3 * tok_rows // experts)
    quarter = depth // n
    gate_mat, up_mat, down_mat = (
        pltpu.with_memory_space_constraint(w[0], pltpu.HBM) for w in (w_gate, w_up, w_down)
    )
    hidden_here = gate_mat.shape[1]

    slot_of = slot_index(expert_ids, experts)
    order = (expert_ids ^ z) * cap + slot_of
    cells = jnp.arange(experts * cap, dtype=jnp.int32)
    pick = [order[:, k][None, :] == cells[:, None] for k in range(2)]
    spread = jnp.logical_or(pick[0], pick[1]).astype(BF)
    slot_gate = jnp.sum(
        jnp.where(pick[0], gate_values[:, 0][None, :], 0.0)
        + jnp.where(pick[1], gate_values[:, 1][None, :], 0.0),
        axis=1,
        keepdims=True,
    )

    def outgoing(source, scale):
        part = lax.dynamic_slice(source, (0, t * quarter), (tok_rows, quarter))
        out = dot_nn(spread[cap:], part)
        own = dot_nn(spread[:cap], source)
        if scale is not None:
            out, own = out * scale[cap:], own * scale[:cap]
        return own.astype(BF), out.astype(BF)

    def over_z(out):
        return [exchange(out[(k - 1) * cap : k * cap], "expert", k) for k in range(1, groups)]

    tok_own, tok_out = outgoing(tokens, None)
    cot_own, cot_out = outgoing(cotangent, slot_gate)
    tok_z = over_z(tok_out)
    first, rest = tok_z[0], tok_z[1:]
    first_far = [exchange(first, "tensor", j) for j in range(1, n)]
    gate_held = fetch(gate_mat)
    rest = jnp.concatenate(after(tuple(rest), gate_held, *first_far), axis=0)
    rest_x, rest_y = exchange(rest, "tensor", 1), exchange(rest, "tensor", 2)
    cot_z = over_z(after(cot_out, rest))
    split = rest.shape[0] // 2
    rest_d = [exchange(rest_y[:split], "tensor", 1), exchange(rest_x[split:], "tensor", 2)]
    tok_parts = [
        [first, rest], [first_far[0], rest_x], [first_far[1], rest_y], [first_far[2], *rest_d]
    ]
    cot_part = jnp.concatenate(after(tuple(cot_z), *rest_d), axis=0)
    cot_parts = [[cot_part]] + [[exchange(cot_part, "tensor", j)] for j in range(1, n)]
    pres = []
    cut = hidden_here // 2
    for start, stop, turn in (
        (0, cut, (cot_part,)),
        (cut, hidden_here, (cot_parts[1][0], cot_parts[2][0])),
    ):
        gate_o, up_o, sent = pre_acts(
            after(t_arr, *turn), tok_own, tok_parts, gate_held, up_mat, start, stop
        )
        pres += [gate_o, up_o, exchange(sent, "wide", 1)]

    def summed(arrived, keep):
        total = keep
        for piece in arrived:
            total = total + piece.astype(F32)
        return total.astype(BF)

    def to_tokens(total):
        return [total[:cap]] + [
            exchange(total[k * cap : (k + 1) * cap], "expert", k) for k in range(1, groups)
        ]

    def around(part):
        return [part] + [exchange(part, "tensor", j) for j in range(1, n)]

    gather = [(order[:, k][:, None] == cells[None, :]).astype(BF) for k in range(2)]

    d_top, d_low, hidden, both = first_piece(
        t_arr, n, hidden_strips, True, pres, [down_mat], (1, 2), "project_send"
    )
    added = [exchange(d_top, "tensor", 1), exchange(d_low, "tensor", 2)]
    grads = []
    turn = after(t_arr, both)
    for start, stop in ((0, cut), (cut, hidden_here)):
        if start:
            to_x, to_y = add_diagonal(t_arr, both, *added)
            turn = after(t_arr, to_x)
        gh_o, gh_s = grad_hiddens(turn, cot_own, cot_parts, down_mat, start, stop)
        grads += [gh_o, exchange(gh_s, "wide", 1)]
    keep = pieces(after(t_arr, gh_s), n, True, [hidden], [down_mat], (0,), "project_keep")[0]

    e_top, e_low, grad_g, grad_u = first_piece(
        after(t_arr, keep), n, grad_strips, False,
        pres + grads, [gate_mat, up_mat], (), "rows_first",
    )
    gadded = [exchange(e_top, "tensor", 1), exchange(e_low, "tensor", 2)]
    from_x, from_y = exchange(to_x, "tensor", 1), exchange(to_y, "tensor", 2)
    gboth = pieces(
        t_arr, n, False, [grad_g, grad_u], [gate_mat, up_mat], (1, 2), "rows_send",
    )
    gto_x, gto_y = add_diagonal(t_arr, gboth, *gadded)
    gkeep = pieces(
        after(t_arr, gto_x), n, False, [grad_g, grad_u], [gate_mat, up_mat], (0,), "rows_keep"
    )[0]
    gtotal = summed((exchange(gto_x, "tensor", 1), exchange(gto_y, "tensor", 2)), gkeep)
    returned = to_tokens(summed((from_x, from_y), after(keep, gto_x)))
    greturned = to_tokens(gtotal)
    returned = jnp.concatenate(after(tuple(returned), greturned[1]), axis=0)
    chosen = [dot_nn(g, returned) for g in gather]
    layer_part = (gate_values[:, 0:1] * chosen[0] + gate_values[:, 1:2] * chosen[1]).astype(BF)
    layer_parts = around(layer_part)
    layer_out = assemble(t_arr, layer_parts)
    greturned = jnp.concatenate(tuple(greturned), axis=0)
    cot_here = lax.dynamic_slice(cotangent, (0, t * quarter), (tok_rows, quarter)).astype(F32)
    gate_grad = jnp.stack([jnp.sum(cot_here * c, axis=1) for c in chosen], axis=0)
    gate_grad = after(gate_grad, layer_parts[1], layer_parts[2])
    for axis, bit in (("wide", 1), ("tensor", 1), ("tensor", 2)):
        gate_grad = gate_grad + exchange(gate_grad, axis, bit)

    grad_part = (dot_nn(gather[0], greturned) + dot_nn(gather[1], greturned)).astype(BF)
    token_grad = assemble(t_arr, around(grad_part))
    return (layer_out, token_grad, gate_grad.T)


def plain_local(tokens, expert_ids, gate_values, w_gate, w_up, w_down, cotangent):
    tok_rows, depth = tokens.shape
    groups = lax.axis_size("expert")
    experts = groups * w_gate.shape[0]
    cap = min(tok_rows, 3 * tok_rows // experts)
    total_rows = groups * cap
    gate_mat, up_mat, down_mat = w_gate[0], w_up[0], w_down[0]
    order = expert_ids * cap + slot_index(expert_ids, experts)
    cells = jnp.arange(experts * cap, dtype=jnp.int32)
    pick = [order[:, k][None, :] == cells[:, None] for k in range(2)]
    gather = [(order[:, k][:, None] == cells[None, :]).astype(BF) for k in range(2)]

    def to_owners(rows):
        out = rows.astype(BF).reshape(groups, cap, depth)
        out = lax.all_to_all(out, "expert", split_axis=0, concat_axis=0, tiled=True)
        return out.reshape(total_rows, depth)

    def send_back(rows):
        share = lax.psum_scatter(rows, "tensor", scatter_dimension=0, tiled=True).astype(BF)
        return to_owners(lax.all_gather(share, "tensor", axis=0, tiled=True))

    spread = jnp.logical_or(pick[0], pick[1]).astype(BF)
    arrived = to_owners(dot_nn(spread, tokens))
    gate_pre, up_pre = lax.psum((dot_nn(arrived, gate_mat), dot_nn(arrived, up_mat)), "wide")
    s = jax.nn.sigmoid(gate_pre)
    returned = send_back(dot_nn((gate_pre * s * up_pre).astype(BF), down_mat))
    chosen = [dot_nn(g, returned) for g in gather]
    layer_out = (gate_values[:, 0:1] * chosen[0] + gate_values[:, 1:2] * chosen[1]).astype(BF)
    upstream = cotangent.astype(F32)
    gate_grad = lax.psum(
        jnp.stack([jnp.sum(upstream * c, axis=1) for c in chosen], axis=1), "wide"
    )
    slot_gate = jnp.sum(
        jnp.where(pick[0], gate_values[:, 0][None, :], 0.0)
        + jnp.where(pick[1], gate_values[:, 1][None, :], 0.0),
        axis=1,
        keepdims=True,
    )
    grad_arrived = to_owners(dot_nn(spread, cotangent) * slot_gate)
    grad_hidden = lax.psum(dot_nt(grad_arrived, down_mat), "wide")
    grad_gate = (grad_hidden * up_pre * (s * (1.0 + gate_pre * (1.0 - s)))).astype(BF)
    grad_up = (grad_hidden * (gate_pre * s)).astype(BF)
    back = send_back(dot_nt(grad_gate, gate_mat) + dot_nt(grad_up, up_mat))
    token_grad = (dot_nn(gather[0], back) + dot_nn(gather[1], back)).astype(BF)
    return (layer_out, token_grad, gate_grad)


def solution(mesh):
    in_specs = (
        P("expert", "wide"),
        P("expert", None),
        P("expert", None),
        P("expert", "wide", "tensor"),
        P("expert", "wide", "tensor"),
        P("expert", "tensor", "wide"),
        P("expert", "wide"),
    )
    out_specs = (P("expert", "wide"), P("expert", "wide"), P("expert", None))
    laid_out = mesh.shape["tensor"] == 4 and mesh.shape["expert"] == 4 and mesh.shape["wide"] == 2
    return jax.shard_map(
        local if laid_out else plain_local,
        mesh=mesh,
        in_specs=in_specs,
        out_specs=out_specs,
        check_vma=False,
    )
```
